128 devices in a mesh: dp: 16 (over x, z_hi, core), tensor: 8 (over z_lo, y).
Axes of the slice: x: 4, y: 4, z: 4 (z_hi: 2, z_lo: 2; z = z_hi * 2 + z_lo), core: 2. Of those that a mesh axis runs over, the one named last changes fastest.
Arguments:
- tokens: bfloat16 [16, 1024, 2048], P('dp', 'tensor'), may hold values from -6 to 6
- query_weight: bfloat16 [2048, 2048], P(None, 'tensor'), may hold values from -0.125 to 0.125
- key_weight: bfloat16 [2048, 2048], P(None, 'tensor'), may hold values from -0.125 to 0.125
- value_weight: bfloat16 [2048, 2048], P(None, 'tensor'), may hold values from -0.125 to 0.125
- output_weight: bfloat16 [2048, 2048], P('tensor'), may hold values from -2 to 2
- gate_weight: bfloat16 [2048, 5504], P(None, 'tensor'), may hold values from -0.125 to 0.125
- up_weight: bfloat16 [2048, 5504], P(None, 'tensor'), may hold values from -0.125 to 0.125
- down_weight: bfloat16 [5504, 2048], P('tensor'), may hold values from -0.109375 to 0.109375
- attn_gain: float32 [2048], replicated, may hold values from 0.1 to 1.9
- mlp_gain: float32 [2048], replicated, may hold values from 0.1 to 1.9
- cotangent: bfloat16 [16, 1024, 2048], P('dp', 'tensor'), may hold values from -6 to 6
Outputs:
- activations: bfloat16 [16, 1024, 2048], P('dp', 'tensor')
- input_grad: float32 [16, 1024, 2048], P('dp', 'tensor')
- query_weight_gradient: float32 [2048, 2048], P(None, 'tensor')
- key_weight_gradient: float32 [2048, 2048], P(None, 'tensor')
- value_weight_gradient: float32 [2048, 2048], P(None, 'tensor')
- output_weight_gradient: float32 [2048, 2048], P('tensor')
- gate_weight_gradient: float32 [2048, 5504], P(None, 'tensor')
- up_weight_gradient: float32 [2048, 5504], P(None, 'tensor')
- down_weight_gradient: float32 [5504, 2048], P('tensor')
- attn_gain_grad: float32 [2048], P('tensor')
- mlp_gain_grad: float32 [2048], P('tensor')
The draws below stay inside these ranges and needn't reach their ends.
All inputs are finite; a program needn't handle non-finite values.
Results may differ from the reference program's by a relative error of at most 0.03.
Values may be sent and summed in bfloat16 or wider, within the bound.
A program may use at most 192 MiB of HBM per device.

```python
import jax
import jax.numpy as jnp
from jax import lax

D = 2048
HEADS = 16
HEAD_DIM = 128
FF = 5504
LEN = 1024
SEQS = 16


def block_scale(rng, extent, shards, smallest, largest):
    factor_of = 1.0
    for dim, parts in shards:
        heights = jax.random.uniform(jax.random.fold_in(jax.random.fold_in(rng, 6), dim), (parts,), jnp.float32, smallest / len(shards), largest / len(shards))
        factor_of = factor_of * jnp.repeat(jnp.exp(heights), extent[dim] // parts).reshape((-1,) + (1,) * (len(extent) - 1 - dim))
    return factor_of


def scatter_about(stream_key, shape, scale, reach, split=(), kind=jnp.bfloat16):
    factor_of = block_scale(stream_key, shape, split, -0.22, 0.18) if split else 1.0
    array = jax.random.normal(stream_key, shape, jnp.float32) * scale * factor_of
    return jnp.minimum(jnp.maximum(array, -reach), reach).astype(kind)


def setup_inputs(seed: int = 0) -> dict:
    arg_keys = jax.random.split(jax.random.key(seed), 12)
    tokens = scatter_about(arg_keys[0], (SEQS, LEN, D), 1.0, 6.0, ((0, 16), (1, 8)))
    query_weight = scatter_about(arg_keys[1], (D, D), D ** -0.5, 0.125, ((1, 8),))
    key_weight = scatter_about(arg_keys[2], (D, D), D ** -0.5, 0.125, ((1, 8),))
    value_weight = scatter_about(arg_keys[3], (D, D), D ** -0.5, 0.125, ((1, 8),))
    output_weight = scatter_about(arg_keys[4], (D, D), (max(1, 4 * D // LEN)) ** -0.5, 2.0, ((0, 8),))
    gate_weight = scatter_about(arg_keys[5], (D, FF), D ** -0.5, 0.125, ((1, 8),))
    up_weight = scatter_about(arg_keys[6], (D, FF), D ** -0.5, 0.125, ((1, 8),))
    down_weight = scatter_about(arg_keys[7], (FF, D), (FF // 2) ** -0.5, 0.109375, ((0, 8),))
    attn_gain = jnp.clip(1.0 + 0.18 * jax.random.normal(arg_keys[8], (D,), jnp.float32), 0.1, 1.9)
    mlp_gain = jnp.clip(1.0 + 0.18 * jax.random.normal(arg_keys[9], (D,), jnp.float32), 0.1, 1.9)
    cotangent = scatter_about(arg_keys[10], (SEQS, LEN, D), 1.0, 6.0, ((0, 16), (1, 8)))
    return {"tokens": tokens, "query_weight": query_weight, "key_weight": key_weight, "value_weight": value_weight, "output_weight": output_weight, "gate_weight": gate_weight, "up_weight": up_weight, "down_weight": down_weight, "attn_gain": attn_gain, "mlp_gain": mlp_gain, "cotangent": cotangent}


@jax.custom_vjp
def reduced_precision(v):
    return lax.optimization_barrier(v.astype(jnp.bfloat16)).astype(jnp.float32)

@jax.custom_vjp
def reduced_precision_backward(v):
    return v

def low_keep(v):
    return (reduced_precision(v), None)

def low_pass(kept, grad):
    return (grad,)

def back_keep(v):
    return (v, None)

def back_low(kept, grad):
    return (reduced_precision(grad),)
reduced_precision.defvjp(low_keep, low_pass)
reduced_precision_backward.defvjp(back_keep, back_low)
norm_eps = 1e-05
rope_base = 10000.0
block_limit = 512
highest = lax.Precision.HIGHEST

def tables(length, head_dim):
    half = head_dim // 2
    freqs = rope_base ** (-(2.0 * jnp.arange(half, dtype=jnp.float32)) / head_dim)
    angles = jnp.arange(length, dtype=jnp.float32)[:, None] * freqs[None, :]
    cosine_table = jnp.cos(angles)
    sine_table = jnp.sin(angles)
    return (jnp.concatenate([cosine_table, cosine_table], 1), jnp.concatenate([sine_table, sine_table], 1))

def apply_rotation(values, cosine_table, sine_table):
    half = values.shape[-1] // 2
    turned = jnp.concatenate([-values[..., half:], values[..., :half]], -1)
    return values * cosine_table[:, None, :] + turned * sine_table[:, None, :]

def normalize(values, gain):
    factor = lax.rsqrt(lax.optimization_barrier(jnp.mean(values * values, axis=-1, keepdims=True)) + norm_eps)
    return values * factor * gain

def matrix_product(form, left, right):
    return jnp.einsum(form, left, right, precision=highest)

def one_block(start, seq_query, seq_key, seq_value):
    rows = min(block_limit, LEN)
    scale = HEAD_DIM ** (-0.5)
    q_block = lax.dynamic_slice_in_dim(seq_query, start, rows, 0)
    scores = reduced_precision_backward(matrix_product('qhd,khd->hqk', q_block, seq_key)) * scale
    places = start + jnp.arange(rows, dtype=jnp.int32)[:, None]
    seen = jnp.arange(LEN, dtype=jnp.int32)[None, :] <= places
    scores = jnp.where(seen[None, :, :], scores, -1e+30)
    highest_score = lax.optimization_barrier(jnp.max(scores, -1, keepdims=True))
    raised = jnp.exp(scores - highest_score)
    probs = reduced_precision(raised / lax.optimization_barrier(jnp.sum(raised, -1, keepdims=True)))
    return matrix_product('hqk,khd->qhd', probs, seq_value)

def attention(query_rows, key, value_rows):
    rows = min(block_limit, LEN)
    blocks = LEN // rows
    starts = jnp.arange(blocks, dtype=jnp.int32) * rows
    block_fn = jax.checkpoint(one_block)

    def one_sequence(item):
        seq_query, seq_key, seq_value = item
        result = lax.map(lambda start: block_fn(start, seq_query, seq_key, seq_value), starts)
        return result.reshape(LEN, HEADS, HEAD_DIM)
    return lax.map(jax.checkpoint(one_sequence), (query_rows, key, value_rows))

def forward(token_group_rows, weights):
    query_weight, key_weight, value_weight, output_weight, gate_weight, up_weight, down_weight, attn_gain, mlp_gain = weights
    count = token_group_rows.shape[0]
    cosine_table, sine_table = tables(LEN, HEAD_DIM)
    array_dimensions = (count, LEN, HEADS, HEAD_DIM)
    normalized_first = reduced_precision(normalize(token_group_rows, attn_gain))
    query_rows = reduced_precision(apply_rotation(reduced_precision_backward(matrix_product('ozb,bv->ozv', normalized_first, query_weight)).reshape(array_dimensions), cosine_table, sine_table))
    key = reduced_precision(apply_rotation(reduced_precision_backward(matrix_product('ozb,bv->ozv', normalized_first, key_weight)).reshape(array_dimensions), cosine_table, sine_table))
    value_rows = reduced_precision(reduced_precision_backward(matrix_product('ozb,bv->ozv', normalized_first, value_weight))).reshape(array_dimensions)
    head_outputs = reduced_precision(reduced_precision_backward(attention(query_rows, key, value_rows).reshape(count, LEN, D)))
    residual_stream = token_group_rows + reduced_precision_backward(matrix_product('ahw,wz->ahz', head_outputs, output_weight))
    normalized_second = reduced_precision(normalize(residual_stream, mlp_gain))
    gate_activation = reduced_precision_backward(matrix_product('jpq,qa->jpa', normalized_second, gate_weight))
    up_activation = reduced_precision_backward(matrix_product('jpq,qa->jpa', normalized_second, up_weight))
    hidden_activation = reduced_precision(jax.nn.silu(gate_activation) * up_activation)
    return residual_stream + reduced_precision_backward(matrix_product('rum,mj->ruj', hidden_activation, down_weight))

def reference(tokens, query_weight, key_weight, value_weight, output_weight, gate_weight, up_weight, down_weight, attn_gain, mlp_gain, cotangent):
    group = 1
    for candidate in range(1, SEQS + 1):
        if SEQS % candidate == 0 and candidate * LEN <= max(4096, LEN):
            group = candidate
    weights = tuple((w.astype(jnp.float32) for w in (query_weight, key_weight, value_weight, output_weight, gate_weight, up_weight, down_weight, attn_gain, mlp_gain)))
    inputs = tokens.astype(jnp.float32).reshape(SEQS // group, group, LEN, D)
    arriving = cotangent.astype(jnp.float32).reshape(SEQS // group, group, LEN, D)

    def step(carry, item):
        token_group_rows, group_grads = item
        outputs, pull = jax.vjp(forward, token_group_rows, weights)
        token_grads, weight_grads = pull(group_grads)
        return (tuple((c + g for c, g in zip(carry, weight_grads))), (outputs, token_grads))
    start_sums = tuple((jnp.zeros_like(w) for w in weights))
    totals, (outputs, token_grads) = lax.scan(step, start_sums, (inputs, arriving))
    activations = outputs.reshape(SEQS, LEN, D).astype(jnp.bfloat16)
    input_grad = token_grads.reshape(SEQS, LEN, D)
    return (activations, input_grad, totals[0], totals[1], totals[2], totals[3], totals[4], totals[5], totals[6], totals[7], totals[8])
```

```python
import functools

import jax
import jax.numpy as jnp
import numpy as np
from jax import lax
from jax.experimental import pallas as pl
from jax.experimental.pallas import tpu as pltpu
from jax.sharding import Mesh, PartitionSpec as P

HEAD_DIM = 128
NORM_EPS = 1e-05
ROPE_BASE = 10000.0
F32, BF16 = jnp.float32, jnp.bfloat16
MESH = pl.DeviceIdType.MESH
ANY = pl.BlockSpec(memory_space=pl.ANY)
VM = pl.BlockSpec(memory_space=pltpu.VMEM)
MIB = 2**20


def tables(length, head_dim):
    half = head_dim // 2
    freqs = np.float32(ROPE_BASE) ** (-(np.float32(2.0) * np.arange(half, dtype=np.float32)) / np.float32(head_dim))
    angles = np.arange(length, dtype=np.float32)[:, None] * freqs[None, :]
    cosine, sine = np.cos(angles), np.sin(angles)
    return np.concatenate([cosine, cosine], 1), np.concatenate([-sine, sine], 1)


class Place:
    def __init__(self):
        self.x = lax.axis_index("x")
        self.zh = lax.axis_index("zh")
        self.zl = lax.axis_index("zl")
        self.c = lax.axis_index("core")
        self.y = lax.axis_index("y")
        self.z = self.zh * 2 + self.zl

    def at(self, dx=0, dy=0, dz=0, core=None):
        out = {}
        if dx:
            out["x"] = lax.rem(self.x + dx + 4, 4)
        if dy:
            out["y"] = lax.rem(self.y + dy + 4, 4)
        if dz:
            z = lax.rem(self.z + dz + 4, 4)
            out["zh"], out["zl"] = z // 2, lax.rem(z, 2)
        if core is not None:
            out["core"] = core
        return out

    def sibling(self):
        return {"core": 1 - self.c}

    def yy(self, d):
        return lax.rem(self.y + d + 4, 4)


def meet(devices):
    barrier = pltpu.get_barrier_semaphore()
    for d in devices:
        pl.semaphore_signal(barrier, inc=1, device_id=d, device_id_type=MESH)
    pl.semaphore_wait(barrier, len(devices))


def remote(src, dst, ss, rs, device):
    return pltpu.make_async_remote_copy(
        src_ref=src, dst_ref=dst, send_sem=ss, recv_sem=rs, device_id=device, device_id_type=MESH
    )


def dot(a, b):
    return jnp.dot(a, b, preferred_element_type=F32)


def dot_nt(a, b):
    return lax.dot_general(a, b, (((1,), (1,)), ((), ())), preferred_element_type=F32)


def dot_tn(a, b):
    return lax.dot_general(a, b, (((0,), (0,)), ((), ())), preferred_element_type=F32)


def normed(values):
    factor = lax.rsqrt(jnp.mean(values * values, axis=-1, keepdims=True) + NORM_EPS)
    return values * factor, factor


class Gather:
    N = 10

    def __init__(self, me, buf, ss, rs, rows):
        h = rows // 2
        c, y = me.c, me.y

        def part(d, lo, n):
            return buf.at[me.yy(d), pl.ds(c * rows + lo, n)]

        up, down, sib = me.at(dy=1), me.at(dy=-1), me.sibling()
        spec = [
            (0, 0, h, up), (0, h, h, up), (0, h, h, down), (0, 0, h, down), (0, 0, rows, sib),
            (-1, 0, h, up), (1, h, h, down), (-1, 0, rows, sib), (1, 0, rows, sib), (2, 0, rows, sib),
        ]
        self.copies = [remote(part(d, lo, n), part(d, lo, n), ss.at[i], rs.at[i], to) for i, (d, lo, n, to) in enumerate(spec)]

    def start(self):
        for i in (0, 2, 1, 3, 4):
            self.copies[i].start()

    def got(self, i):
        self.copies[i].wait_recv()

    def forward_one(self):
        self.got(0)
        self.copies[5].start()
        self.got(2)
        self.copies[6].start()

    def near(self):
        self.got(1)
        self.copies[7].start()
        self.got(3)
        self.copies[8].start()

    def far(self):
        self.got(5)
        self.got(6)
        self.copies[9].start()

    def finish(self):
        for cp in self.copies:
            cp.wait_send()


class Scatter:
    N = 10

    def __init__(self, me, part, own, ra, rb, f1, f2, ss, rs, rows):
        self.me, self.part, self.own, self.rows = me, part, own, rows
        self.ra, self.rb, self.f1, self.f2 = ra, rb, f1, f2
        self.h = rows // 2
        c = me.c
        up, down, sib = me.at(dy=1), me.at(dy=-1), me.sibling()
        h = self.h
        self.order = (2, 1, -1, 0)
        self.sib = {}
        for i, d in enumerate(self.order):
            self.sib[d] = remote(
                part.at[me.yy(d), pl.ds((1 - c) * rows, rows)], own.at[me.yy(d)], ss.at[i], rs.at[i], sib
            )

        def mine(d, lo):
            return part.at[me.yy(d), pl.ds(c * rows + lo, h)]

        self.a2 = remote(mine(2, 0), ra, ss.at[4], rs.at[4], up)
        self.b2 = remote(mine(2, h), rb, ss.at[5], rs.at[5], down)
        self.b1 = remote(mine(1, h), f1.at[pl.ds(h, h)], ss.at[6], rs.at[6], up)
        self.a1 = remote(mine(1, 0), f1.at[pl.ds(0, h)], ss.at[7], rs.at[7], up)
        self.am = remote(mine(-1, 0), f2.at[pl.ds(0, h)], ss.at[8], rs.at[8], down)
        self.bm = remote(mine(-1, h), f2.at[pl.ds(h, h)], ss.at[9], rs.at[9], down)

    def add(self, d, lo, n, other):
        rows = pl.ds(self.me.c * self.rows + lo, n)
        at = self.me.yy(d)
        self.part[at, rows] = (self.part[at, rows].astype(F32) + other.astype(F32)).astype(BF16)

    def ready(self, d):
        self.sib[d].start()

    def stage_two(self):
        self.sib[2].wait_recv()
        self.add(2, 0, self.rows, self.own[self.me.yy(2)])
        self.a2.start()
        self.b2.start()

    def stage_one(self):
        self.sib[1].wait_recv()
        self.add(1, 0, self.rows, self.own[self.me.yy(1)])
        self.b1.start()
        self.sib[-1].wait_recv()
        self.add(-1, 0, self.rows, self.own[self.me.yy(-1)])
        self.am.start()

    def stage_last(self):
        self.a2.wait_recv()
        self.add(1, 0, self.h, self.ra[...])
        self.a1.start()
        self.b2.wait_recv()
        self.add(-1, self.h, self.h, self.rb[...])
        self.bm.start()

    def result(self):
        self.sib[0].wait_recv()
        for cp in (self.b1, self.am, self.a1, self.bm):
            cp.wait_recv()

    def total(self, lo, n):
        me = self.me
        mine = self.part[me.y, pl.ds(me.c * self.rows + lo, n)].astype(F32)
        near = self.f1[pl.ds(lo, n)].astype(F32) + self.f2[pl.ds(lo, n)].astype(F32)
        return mine + self.own[me.y, pl.ds(lo, n)].astype(F32) + near

    def finish(self):
        for cp in (*self.sib.values(), self.a2, self.b2, self.b1, self.a1, self.am, self.bm):
            cp.wait_send()


def scatter_scratch(rows, width):
    return [
        pltpu.VMEM((4, 2 * rows, width), BF16),
        pltpu.VMEM((4, rows, width), BF16),
        pltpu.VMEM((rows // 2, width), BF16),
        pltpu.VMEM((rows // 2, width), BF16),
        pltpu.VMEM((rows, width), BF16),
        pltpu.VMEM((rows, width), BF16),
    ]


def dma(n):
    return pltpu.SemaphoreType.DMA((n,))


def perm(block):
    return (block % 4) * 2 + block // 4


def forward_attention_kernel(
    tok, cot, wq, wk, wv, wo, wg, wu, wd, g1, g2, cosine, sine,
    resid_o, n2_o, tok_o, cot_o, g_o, q_o, k_o, v_o, ho_o, w3_o, wo_o, wg_o, wu_o, wd_o,
    tok_s, g_s, w3_s, wo_s, q_s, k_s, v_s, ho_s, resid_s, n2_s,
    part, own, ra, rb, f1, f2,
    ag_ss, ag_rs, rs_ss, rs_rs, w_ss, w_rs, loc, out_sem,
):
    me = Place()
    c, zl = me.c, me.zl
    rows = tok.shape[0]
    stays = c == zl
    swap = {"zl": 1 - zl, "core": 1 - c}
    others = [me.at(dy=1), me.at(dy=-1), me.sibling()]
    others += [me.at(dz=s, core=k) for s in (1, -1) for k in (0, 1)]
    meet(others)

    z_other = lax.rem(me.z + jnp.where(zl == 0, 3, 1), 4)
    far_z = {"zh": z_other // 2, "zl": lax.rem(z_other, 2), "core": c}

    heads = (wq, wk, wv)

    def halves(i, src, dst_all, axis_rows):
        h = axis_rows // 2
        a = remote(src.at[pl.ds(0, h)], dst_all.at[pl.ds(0, h)], w_ss.at[i], w_rs.at[2 * i], swap)
        b = remote(src.at[pl.ds(h, h)], dst_all.at[pl.ds(h, h)], w_ss.at[i], w_rs.at[2 * i + 1], far_z)
        return a, b

    def w3_part(i):
        return w3_s.at[:, pl.ds(256 * i, 256)]

    moved = [halves(i, w, w3_part(i), w.shape[0]) for i, w in enumerate(heads)]
    moved.append(halves(3, wo, wo_s, wo.shape[0]))
    later = [halves(4, wg, wg_o, wg.shape[0]), halves(5, wu, wu_o, wu.shape[0])]
    ffd = wd.shape[0]
    hd = (ffd // 2) // 16 * 16
    later.append((
        remote(wd.at[pl.ds(0, hd)], wd_o.at[pl.ds(0, hd)], w_ss.at[6], w_rs.at[12], swap),
        remote(wd.at[pl.ds(hd, ffd - hd)], wd_o.at[pl.ds(hd, ffd - hd)], w_ss.at[6], w_rs.at[13], far_z),
    ))
    tok_move = remote(tok, tok_s, w_ss.at[7], w_rs.at[14], swap)
    cot_move = remote(cot, cot_o, w_ss.at[8], w_rs.at[15], swap)
    local = [pltpu.make_async_copy(w, w3_part(i), loc.at[i]) for i, w in enumerate(heads)]
    local.append(pltpu.make_async_copy(wo, wo_s, loc.at[3]))
    local_later = [
        pltpu.make_async_copy(a, b, loc.at[4 + i]) for i, (a, b) in enumerate(((wg, wg_o), (wu, wu_o), (wd, wd_o), (cot, cot_o)))
    ]
    tok_local = pltpu.make_async_copy(tok, tok_s, loc.at[8])

    @pl.when(stays)
    def _():
        tok_local.start()
        for cp in local:
            cp.start()
        for _, b in moved:
            b.start()
        tok_local.wait()

    @pl.when(jnp.logical_not(stays))
    def _():
        tok_move.start()
        tok_move.wait_send()
        for a, _ in moved:
            a.start()
        tok_move.wait_recv()

    out_tok = pltpu.make_async_copy(tok_s, tok_o, out_sem.at[0])
    out_tok.start()
    unit, _ = normed(tok_s[...].astype(F32))
    g_s[me.y, pl.ds(c * rows, rows)] = (unit * g1[...]).astype(BF16)

    gather = Gather(me, g_s, ag_ss, ag_rs, rows)
    gather.start()

    @pl.when(stays)
    def _():
        for cp in local:
            cp.wait()

    @pl.when(jnp.logical_not(stays))
    def _():
        for i in range(8):
            (moved[i // 2][i % 2]).wait_recv()

    def project(d):
        at = me.yy(d)
        out = dot(g_s[at], w3_s[...])
        for half in (0, 1):
            place = pl.ds(pl.multiple_of((at + 4 * half) * rows, rows), rows)
            cs, sn = cosine[place], sine[place]
            for i, ref in enumerate((q_s, k_s, v_s)):
                for head in (0, 1):
                    v = out[half * rows:(half + 1) * rows, i * 256 + head * 128:i * 256 + head * 128 + 128]
                    if i < 2:
                        v = v * cs + pltpu.roll(v, 64, axis=1) * sn
                    ref[head, place] = v.astype(BF16)

    gather.got(4)
    project(0)
    gather.forward_one()
    gather.near()

    @pl.when(stays)
    def _():
        for cp in local_later:
            cp.start()
        for _, b in later:
            b.start()

    @pl.when(jnp.logical_not(stays))
    def _():
        cot_move.start()
        for a, _ in later:
            a.start()

    gather.got(7)
    project(-1)
    gather.got(8)
    project(1)
    gather.far()
    gather.got(9)
    project(2)
    out_g = pltpu.make_async_copy(g_s, g_o, out_sem.at[1])
    out_g.start()
    outs = [out_tok, out_g]
    for i, (a, b) in enumerate(((q_s, q_o), (k_s, k_o), (v_s, v_o), (w3_s, w3_o))):
        cp = pltpu.make_async_copy(a, b, out_sem.at[2 + i])
        cp.start()
        outs.append(cp)

    scale = HEAD_DIM ** (-0.5)
    step = 2 * rows
    for block in range(4):
        stop = (block + 1) * step
        for head in (0, 1):
            s = dot_nt(q_s[head, pl.ds(block * step, step)], k_s[head, pl.ds(0, stop)]) * scale
            places = block * step + lax.broadcasted_iota(jnp.int32, (step, stop), 0)
            s = jnp.where(lax.broadcasted_iota(jnp.int32, (step, stop), 1) <= places, s, -1e30)
            e = jnp.exp(s - jnp.max(s, -1, keepdims=True))
            p = (e / jnp.sum(e, -1, keepdims=True)).astype(BF16)
            o = dot(p, v_s[head, pl.ds(0, stop)]).astype(BF16)
            for half in (0, 1):
                ho_s[pl.ds(perm(2 * block + half) * rows, rows), pl.ds(head * 128, 128)] = o[half * rows:(half + 1) * rows]
    for i, (a, b) in enumerate(((ho_s, ho_o), (wo_s, wo_o))):
        cp = pltpu.make_async_copy(a, b, out_sem.at[6 + i])
        cp.start()
        outs.append(cp)

    scatter = Scatter(me, part, own, ra, rb, f1, f2, rs_ss, rs_rs, rows)

    def out_project(d):
        at = me.yy(d)
        part[at] = dot(ho_s[pl.ds(pl.multiple_of(at * 2 * rows, 2 * rows), 2 * rows)], wo_s[...]).astype(BF16)
        scatter.ready(d)

    out_project(2)
    out_project(1)
    out_project(-1)
    scatter.stage_two()
    out_project(0)
    scatter.stage_one()
    scatter.stage_last()
    scatter.result()
    resid = tok_s[...].astype(F32) + scatter.total(0, rows)
    resid_s[...] = resid
    unit, _ = normed(resid)
    n2_s[...] = (unit * g2[...]).astype(BF16)
    for i, (a, b) in enumerate(((resid_s, resid_o), (n2_s, n2_o))):
        cp = pltpu.make_async_copy(a, b, out_sem.at[8 + i])
        cp.start()
        outs.append(cp)

    gather.finish()
    scatter.finish()
    for cp in outs:
        cp.wait()

    @pl.when(stays)
    def _():
        for cp in local_later:
            cp.wait()
        for _, b in moved + later:
            b.wait_send()

    @pl.when(jnp.logical_not(stays))
    def _():
        cot_move.wait()
        for a, b in later:
            a.wait()
            b.wait_recv()
        for a, _ in moved:
            a.wait_send()


def forward_attention(args):
    tok, cot, wq, wk, wv, wo, wg, wu, wd, g1, g2, cosine, sine = args
    rows, width = tok.shape
    ff = wg.shape[1]
    length = 8 * rows
    sds = jax.ShapeDtypeStruct
    outs = [
        sds((rows, width), F32), sds((rows, width), BF16), sds((rows, width), BF16), sds((rows, width), BF16),
        sds((4, 2 * rows, width), BF16),
        sds((2, length, 128), BF16), sds((2, length, 128), BF16), sds((2, length, 128), BF16),
        sds((length, 256), BF16), sds((width, 768), BF16), sds((256, width), BF16),
        sds((width, ff), BF16), sds((width, ff), BF16), sds((ff, width), BF16),
    ]
    scratch = [
        pltpu.VMEM((rows, width), BF16), pltpu.VMEM((4, 2 * rows, width), BF16),
        pltpu.VMEM((width, 768), BF16), pltpu.VMEM((256, width), BF16),
        *[pltpu.VMEM((2, length, 128), BF16)] * 3, pltpu.VMEM((length, 256), BF16),
        pltpu.VMEM((rows, width), F32), pltpu.VMEM((rows, width), BF16),
        *scatter_scratch(rows, width),
        dma(10), dma(10), dma(10), dma(10), dma(9), dma(16), dma(9), dma(10),
    ]
    return pl.pallas_call(
        forward_attention_kernel,
        name="forward_attention",
        out_shape=outs,
        in_specs=[ANY] * 9 + [VM] * 4,
        out_specs=[ANY] * len(outs),
        scratch_shapes=scratch,
        compiler_params=pltpu.CompilerParams(collective_id=0, has_side_effects=True, vmem_limit_bytes=60 * MIB),
    )(*args)


def norm_back(grads, unit, factor):
    return factor * (grads - unit * jnp.mean(grads * unit, axis=-1, keepdims=True))


TP = ("core", "y")
DP = ("x", "zh", "zl")
SWAP = [(0, 0), (1, 2), (2, 1), (3, 3)]


def natural(g):
    rows = g.shape[1] // 2
    return g.reshape(4, 2, rows, -1).transpose(1, 0, 2, 3).reshape(8 * rows, -1)


def per_device(tokens, wq, wk, wv, wo, wg, wu, wd, attn_gain, mlp_gain, cotangent):
    tokens, cotangent = tokens[0], cotangent[0]
    rows = tokens.shape[0]
    length = 8 * rows
    cosine, sine = (jnp.asarray(t) for t in tables(length, HEAD_DIM))
    (resid, n2, tok, cot, g1, q, k, v, ho, w3, wo, wg, wu, wd) = forward_attention(
        (tokens, cotangent, wq, wk, wv, wo, wg, wu, wd, attn_gain[None], mlp_gain[None], cosine, sine)
    )
    inputs = tok.astype(F32)
    grad_out = cot.astype(F32)
    one = natural(g1)
    ho = natural(ho.reshape(4, 2 * rows, 256))
    unit_one, factor_one = normed(inputs)
    unit_two, factor_two = normed(resid)

    def gathered(x):
        return lax.all_gather(x, TP, axis=0, tiled=True)

    def scattered(x):
        return lax.psum_scatter(x.astype(BF16), TP, scatter_dimension=0, tiled=True).astype(F32)

    two = gathered(n2)
    gate, up = dot(two, wg), dot(two, wu)
    sigma = jax.nn.sigmoid(gate)
    swish = gate * sigma
    hidden = (swish * up).astype(BF16)
    activations = (resid + scattered(dot(hidden, wd))).astype(BF16)
    gm = gathered(cot)
    d_wd = dot_tn(hidden, gm)
    gh = dot_nt(gm, wd)
    d_gate = (gh * up * sigma * (1.0 + gate * (1.0 - sigma))).astype(BF16)
    d_up = (gh * swish).astype(BF16)
    d_wg, d_wu = dot_tn(two, d_gate), dot_tn(two, d_up)
    gn2 = scattered(dot_nt(d_gate, wg) + dot_nt(d_up, wu))
    gain_two = jnp.sum(gn2 * unit_two, axis=0)
    grad_resid = grad_out + norm_back(gn2 * mlp_gain, unit_two, factor_two)
    ga = gathered(grad_resid.astype(BF16))
    d_wo = dot_tn(ho, ga)
    gheads = dot_nt(ga, wo).astype(BF16).reshape(length, 2, 128).transpose(1, 0, 2)
    scale = HEAD_DIM ** (-0.5)
    seen = jnp.tril(jnp.ones((length, length), bool))
    s = jnp.where(seen, jnp.einsum("hqd,hkd->hqk", q, k, preferred_element_type=F32) * scale, -1e30)
    p = jax.nn.softmax(s, -1)
    gv = jnp.einsum("hqk,hqd->hkd", p.astype(BF16), gheads, preferred_element_type=F32).astype(BF16)
    gp = jnp.einsum("hqd,hkd->hqk", gheads, v, preferred_element_type=F32)
    gs = (p * (gp - jnp.sum(p * gp, -1, keepdims=True)) * scale).astype(BF16)
    gq = jnp.einsum("hqk,hkd->hqd", gs, k, preferred_element_type=F32)
    gk = jnp.einsum("hqk,hqd->hkd", gs, q, preferred_element_type=F32)

    def unrotate(g):
        return (g * cosine - jnp.roll(g, 64, -1) * sine).astype(BF16)

    def flat(g):
        return g.transpose(1, 0, 2).reshape(length, 256)

    g3 = jnp.concatenate([flat(unrotate(gq)), flat(unrotate(gk)), flat(gv)], 1)
    d_w3 = dot_tn(one, g3)
    gn1 = scattered(dot_nt(g3, w3))
    gain_one = jnp.sum(gn1 * unit_one, axis=0)
    input_grad = grad_resid + norm_back(gn1 * attn_gain, unit_one, factor_one)
    gains = lax.psum(jnp.stack([gain_one, gain_two]), ("x", "zh", "zl", "core", "y"))
    place = lax.axis_index("zl") * 4 + lax.axis_index("y")
    gains = lax.dynamic_slice_in_dim(gains, place * 256, 256, 1)
    zl = lax.axis_index("zl")

    def total(x):
        x = lax.psum(x.astype(BF16), DP)
        both = lax.all_gather(x, "core", axis=0)
        return lax.dynamic_index_in_dim(both, zl, 0, keepdims=False).astype(F32)

    d_w3 = total(d_w3)

    def back(x):
        return lax.ppermute(x, ("core", "zl"), SWAP)[None]

    return (
        back(activations), back(input_grad), d_w3[:, :256], d_w3[:, 256:512], d_w3[:, 512:], total(d_wo),
        total(d_wg), total(d_wu), total(d_wd), gains[0], gains[1],
    )


def solution(mesh):
    split = Mesh(mesh.devices.reshape(4, 2, 2, 2, 4), ("x", "zh", "core", "zl", "y"))
    dp, tensor = ("x", "zh", "core"), ("zl", "y")
    cols, rows, seqs = P(None, tensor), P(tensor, None), P(dp, tensor, None)
    return jax.shard_map(
        per_device,
        mesh=split,
        in_specs=(seqs, cols, cols, cols, rows, cols, cols, rows, P(), P(), seqs),
        out_specs=(seqs, seqs, cols, cols, cols, rows, cols, cols, rows, P(tensor), P(tensor)),
        check_vma=False,
    )
```

```python
import functools

import jax
import jax.numpy as jnp
import numpy as np
from jax import lax
from jax.experimental import pallas as pl
from jax.experimental.pallas import tpu as pltpu
from jax.sharding import Mesh, PartitionSpec as P

HEAD_DIM = 128
NORM_EPS = 1e-05
ROPE_BASE = 10000.0
F32, BF16 = jnp.float32, jnp.bfloat16
MESH = pl.DeviceIdType.MESH
ANY = pl.BlockSpec(memory_space=pl.ANY)
VM = pl.BlockSpec(memory_space=pltpu.VMEM)
MIB = 2**20


def tables(length, head_dim):
    half = head_dim // 2
    freqs = np.float32(ROPE_BASE) ** (-(np.float32(2.0) * np.arange(half, dtype=np.float32)) / np.float32(head_dim))
    angles = np.arange(length, dtype=np.float32)[:, None] * freqs[None, :]
    cosine, sine = np.cos(angles), np.sin(angles)
    return np.concatenate([cosine, cosine], 1), np.concatenate([-sine, sine], 1)


class Place:
    def __init__(self):
        self.x = lax.axis_index("x")
        self.zh = lax.axis_index("zh")
        self.zl = lax.axis_index("zl")
        self.c = lax.axis_index("core")
        self.y = lax.axis_index("y")
        self.z = self.zh * 2 + self.zl

    def at(self, dx=0, dy=0, dz=0, core=None):
        out = {}
        if dx:
            out["x"] = lax.rem(self.x + dx + 4, 4)
        if dy:
            out["y"] = lax.rem(self.y + dy + 4, 4)
        if dz:
            z = lax.rem(self.z + dz + 4, 4)
            out["zh"], out["zl"] = z // 2, lax.rem(z, 2)
        if core is not None:
            out["core"] = core
        return out

    def sibling(self):
        return {"core": 1 - self.c}

    def yy(self, d):
        return lax.rem(self.y + d + 4, 4)


def meet(devices):
    barrier = pltpu.get_barrier_semaphore()
    for d in devices:
        pl.semaphore_signal(barrier, inc=1, device_id=d, device_id_type=MESH)
    pl.semaphore_wait(barrier, len(devices))


def remote(src, dst, ss, rs, device):
    return pltpu.make_async_remote_copy(
        src_ref=src, dst_ref=dst, send_sem=ss, recv_sem=rs, device_id=device, device_id_type=MESH
    )


def dot(a, b):
    return jnp.dot(a, b, preferred_element_type=F32)


def dot_nt(a, b):
    return lax.dot_general(a, b, (((1,), (1,)), ((), ())), preferred_element_type=F32)


def dot_tn(a, b):
    return lax.dot_general(a, b, (((0,), (0,)), ((), ())), preferred_element_type=F32)


def normed(values):
    factor = lax.rsqrt(jnp.mean(values * values, axis=-1, keepdims=True) + NORM_EPS)
    return values * factor, factor


class Gather:
    N = 10

    def __init__(self, me, buf, ss, rs, rows):
        h = rows // 2
        c, y = me.c, me.y

        def part(d, lo, n):
            return buf.at[me.yy(d), pl.ds(c * rows + lo, n)]

        up, down, sib = me.at(dy=1), me.at(dy=-1), me.sibling()
        spec = [
            (0, 0, h, up), (0, h, h, up), (0, h, h, down), (0, 0, h, down), (0, 0, rows, sib),
            (-1, 0, h, up), (1, h, h, down), (-1, 0, rows, sib), (1, 0, rows, sib), (2, 0, rows, sib),
        ]
        self.copies = [remote(part(d, lo, n), part(d, lo, n), ss.at[i], rs.at[i], to) for i, (d, lo, n, to) in enumerate(spec)]

    def start(self):
        for i in (0, 2, 1, 3, 4):
            self.copies[i].start()

    def got(self, i):
        self.copies[i].wait_recv()

    def forward_one(self):
        self.got(0)
        self.copies[5].start()
        self.got(2)
        self.copies[6].start()

    def near(self):
        self.got(1)
        self.copies[7].start()
        self.got(3)
        self.copies[8].start()

    def far(self):
        self.got(5)
        self.got(6)
        self.copies[9].start()

    def finish(self):
        for cp in self.copies:
            cp.wait_send()


class Scatter:
    N = 10

    def __init__(self, me, part, own, ra, rb, f1, f2, ss, rs, rows):
        self.me, self.part, self.own, self.rows = me, part, own, rows
        self.ra, self.rb, self.f1, self.f2 = ra, rb, f1, f2
        self.h = rows // 2
        c = me.c
        up, down, sib = me.at(dy=1), me.at(dy=-1), me.sibling()
        h = self.h
        self.order = (2, 1, -1, 0)
        self.sib = {}
        for i, d in enumerate(self.order):
            self.sib[d] = remote(
                part.at[me.yy(d), pl.ds((1 - c) * rows, rows)], own.at[me.yy(d)], ss.at[i], rs.at[i], sib
            )

        def mine(d, lo):
            return part.at[me.yy(d), pl.ds(c * rows + lo, h)]

        self.a2 = remote(mine(2, 0), ra, ss.at[4], rs.at[4], up)
        self.b2 = remote(mine(2, h), rb, ss.at[5], rs.at[5], down)
        self.b1 = remote(mine(1, h), f1.at[pl.ds(h, h)], ss.at[6], rs.at[6], up)
        self.a1 = remote(mine(1, 0), f1.at[pl.ds(0, h)], ss.at[7], rs.at[7], up)
        self.am = remote(mine(-1, 0), f2.at[pl.ds(0, h)], ss.at[8], rs.at[8], down)
        self.bm = remote(mine(-1, h), f2.at[pl.ds(h, h)], ss.at[9], rs.at[9], down)

    def add(self, d, lo, n, other):
        rows = pl.ds(self.me.c * self.rows + lo, n)
        at = self.me.yy(d)
        self.part[at, rows] = (self.part[at, rows].astype(F32) + other.astype(F32)).astype(BF16)

    def ready(self, d):
        self.sib[d].start()

    def stage_two(self):
        self.sib[2].wait_recv()
        self.add(2, 0, self.rows, self.own[self.me.yy(2)])
        self.a2.start()
        self.b2.start()

    def stage_one(self):
        self.sib[1].wait_recv()
        self.add(1, 0, self.rows, self.own[self.me.yy(1)])
        self.b1.start()
        self.sib[-1].wait_recv()
        self.add(-1, 0, self.rows, self.own[self.me.yy(-1)])
        self.am.start()

    def stage_last(self):
        self.a2.wait_recv()
        self.add(1, 0, self.h, self.ra[...])
        self.a1.start()
        self.b2.wait_recv()
        self.add(-1, self.h, self.h, self.rb[...])
        self.bm.start()

    def result(self):
        self.sib[0].wait_recv()
        for cp in (self.b1, self.am, self.a1, self.bm):
            cp.wait_recv()

    def total(self, lo, n):
        me = self.me
        mine = self.part[me.y, pl.ds(me.c * self.rows + lo, n)].astype(F32)
        near = self.f1[pl.ds(lo, n)].astype(F32) + self.f2[pl.ds(lo, n)].astype(F32)
        return mine + self.own[me.y, pl.ds(lo, n)].astype(F32) + near

    def finish(self):
        for cp in (*self.sib.values(), self.a2, self.b2, self.b1, self.a1, self.am, self.bm):
            cp.wait_send()


def scatter_scratch(rows, width):
    return [
        pltpu.VMEM((4, 2 * rows, width), BF16),
        pltpu.VMEM((4, rows, width), BF16),
        pltpu.VMEM((rows // 2, width), BF16),
        pltpu.VMEM((rows // 2, width), BF16),
        pltpu.VMEM((rows, width), BF16),
        pltpu.VMEM((rows, width), BF16),
    ]


def dma(n):
    return pltpu.SemaphoreType.DMA((n,))


def perm(block):
    return (block % 4) * 2 + block // 4


def forward_attention_kernel(
    tok, cot, wq, wk, wv, wo, wg, wu, g1, g2, cosine, sine,
    resid_o, n2_o, tok_o, gm_o, g_o, q_o, k_o, v_o, ho_o, w3_o, wo_o, wg_o, wu_o,
    tok_s, g_s, gm_s, w3_s, wo_s, q_s, k_s, v_s, ho_s, resid_s, n2_s,
    part, own, ra, rb, f1, f2,
    ag_ss, ag_rs, ag3_ss, ag3_rs, rs_ss, rs_rs, w_ss, w_rs, loc, out_sem,
):
    me = Place()
    c, zl = me.c, me.zl
    rows = tok.shape[0]
    stays = c == zl
    swap = {"zl": 1 - zl, "core": 1 - c}
    others = [me.at(dy=1), me.at(dy=-1), me.sibling()]
    others += [me.at(dz=s, core=k) for s in (1, -1) for k in (0, 1)]
    meet(others)

    z_other = lax.rem(me.z + jnp.where(zl == 0, 3, 1), 4)
    far_z = {"zh": z_other // 2, "zl": lax.rem(z_other, 2), "core": c}

    heads = (wq, wk, wv)

    def halves(i, src, dst_all, axis_rows):
        h = axis_rows // 32 * 16
        r = axis_rows - h
        a = remote(src.at[pl.ds(0, h)], dst_all.at[pl.ds(0, h)], w_ss.at[i], w_rs.at[2 * i], swap)
        b = remote(src.at[pl.ds(h, r)], dst_all.at[pl.ds(h, r)], w_ss.at[i], w_rs.at[2 * i + 1], far_z)
        return a, b

    def w3_part(i):
        return w3_s.at[:, pl.ds(256 * i, 256)]

    moved = [halves(i, w, w3_part(i), w.shape[0]) for i, w in enumerate(heads)]
    moved.append(halves(3, wo, wo_s, wo.shape[0]))
    later = [halves(4, wg, wg_o, wg.shape[0]), halves(5, wu, wu_o, wu.shape[0])]
    tok_move = remote(tok, tok_s, w_ss.at[7], w_rs.at[14], swap)
    mine = gm_s.at[me.y, pl.ds(c * rows, rows)]
    cot_move = remote(cot, gm_s.at[me.y, pl.ds((1 - c) * rows, rows)], w_ss.at[8], w_rs.at[15], swap)
    local = [pltpu.make_async_copy(w, w3_part(i), loc.at[i]) for i, w in enumerate(heads)]
    local.append(pltpu.make_async_copy(wo, wo_s, loc.at[3]))
    cot_local = pltpu.make_async_copy(cot, mine, loc.at[4])
    tok_local = pltpu.make_async_copy(tok, tok_s, loc.at[8])

    @pl.when(stays)
    def _():
        tok_local.start()
        for cp in local:
            cp.start()
        cot_local.start()
        for _, b in moved:
            b.start()
        tok_local.wait()

    @pl.when(jnp.logical_not(stays))
    def _():
        tok_move.start()
        tok_move.wait_send()
        for a, _ in moved:
            a.start()
        cot_move.start()
        tok_move.wait_recv()

    out_tok = pltpu.make_async_copy(tok_s, tok_o, out_sem.at[0])
    out_tok.start()
    unit, _ = normed(tok_s[...].astype(F32))
    g_s[me.y, pl.ds(c * rows, rows)] = (unit * g1[...]).astype(BF16)

    gather = Gather(me, g_s, ag_ss, ag_rs, rows)
    gather.start()

    @pl.when(stays)
    def _():
        for cp in local:
            cp.wait()

    @pl.when(jnp.logical_not(stays))
    def _():
        for i in range(8):
            (moved[i // 2][i % 2]).wait_recv()

    def project(d):
        at = me.yy(d)
        out = dot(g_s[at], w3_s[...])
        for half in (0, 1):
            place = pl.ds(pl.multiple_of((at + 4 * half) * rows, rows), rows)
            cs, sn = cosine[place], sine[place]
            for i, ref in enumerate((q_s, k_s, v_s)):
                for head in (0, 1):
                    v = out[half * rows:(half + 1) * rows, i * 256 + head * 128:i * 256 + head * 128 + 128]
                    if i < 2:
                        v = v * cs + pltpu.roll(v, 64, axis=1) * sn
                    ref[head, place] = v.astype(BF16)

    gather.got(4)
    project(0)
    gather.forward_one()
    gather.near()

    @pl.when(stays)
    def _():
        for _, b in later:
            b.start()
        cot_local.wait()

    @pl.when(jnp.logical_not(stays))
    def _():
        for a, _ in later:
            a.start()
        cot_move.wait_recv()

    third = Gather(me, gm_s, ag3_ss, ag3_rs, rows)
    third.start()

    gather.got(7)
    project(-1)
    gather.got(8)
    project(1)
    gather.far()
    gather.got(9)
    project(2)
    out_g = pltpu.make_async_copy(g_s, g_o, out_sem.at[1])
    out_g.start()
    outs = [out_tok, out_g]
    for i, (a, b) in enumerate(((q_s, q_o), (k_s, k_o), (v_s, v_o), (w3_s, w3_o))):
        cp = pltpu.make_async_copy(a, b, out_sem.at[2 + i])
        cp.start()
        outs.append(cp)

    third.got(4)
    third.forward_one()
    scale = HEAD_DIM ** (-0.5)
    step = 2 * rows
    for block in range(4):
        stop = (block + 1) * step
        for head in (0, 1):
            s = dot_nt(q_s[head, pl.ds(block * step, step)], k_s[head, pl.ds(0, stop)]) * scale
            places = block * step + lax.broadcasted_iota(jnp.int32, (step, stop), 0)
            s = jnp.where(lax.broadcasted_iota(jnp.int32, (step, stop), 1) <= places, s, -1e30)
            e = jnp.exp(s - jnp.max(s, -1, keepdims=True))
            p = (e / jnp.sum(e, -1, keepdims=True)).astype(BF16)
            o = dot(p, v_s[head, pl.ds(0, stop)]).astype(BF16)
            for half in (0, 1):
                ho_s[pl.ds(perm(2 * block + half) * rows, rows), pl.ds(head * 128, 128)] = o[half * rows:(half + 1) * rows]
    third.near()
    for i, (a, b) in enumerate(((ho_s, ho_o), (wo_s, wo_o))):
        cp = pltpu.make_async_copy(a, b, out_sem.at[6 + i])
        cp.start()
        outs.append(cp)

    scatter = Scatter(me, part, own, ra, rb, f1, f2, rs_ss, rs_rs, rows)

    def out_project(d):
        at = me.yy(d)
        part[at] = dot(ho_s[pl.ds(pl.multiple_of(at * 2 * rows, 2 * rows), 2 * rows)], wo_s[...]).astype(BF16)
        scatter.ready(d)

    out_project(2)
    out_project(1)
    out_project(-1)
    scatter.stage_two()
    out_project(0)
    scatter.stage_one()
    scatter.stage_last()
    third.got(7)
    third.got(8)
    third.far()
    third.got(9)
    cp = pltpu.make_async_copy(gm_s, gm_o, out_sem.at[10])
    cp.start()
    outs.append(cp)
    scatter.result()
    resid = tok_s[...].astype(F32) + scatter.total(0, rows)
    resid_s[...] = resid
    unit, _ = normed(resid)
    n2_s[...] = (unit * g2[...]).astype(BF16)
    for i, (a, b) in enumerate(((resid_s, resid_o), (n2_s, n2_o))):
        cp = pltpu.make_async_copy(a, b, out_sem.at[8 + i])
        cp.start()
        outs.append(cp)

    gather.finish()
    third.finish()
    scatter.finish()
    for cp in outs:
        cp.wait()

    @pl.when(stays)
    def _():
        for _, b in moved + later:
            b.wait_send()

    @pl.when(jnp.logical_not(stays))
    def _():
        cot_move.wait_send()
        for a, b in later:
            a.wait()
            b.wait_recv()
        for a, _ in moved:
            a.wait_send()


def forward_attention(args):
    tok, cot, wq, wk, wv, wo, wg, wu, g1, g2, cosine, sine = args
    rows, width = tok.shape
    ff = wg.shape[0]
    length = 8 * rows
    sds = jax.ShapeDtypeStruct
    outs = [
        sds((rows, width), F32), sds((rows, width), BF16), sds((rows, width), BF16), sds((4, 2 * rows, width), BF16),
        sds((4, 2 * rows, width), BF16),
        sds((2, length, 128), BF16), sds((2, length, 128), BF16), sds((2, length, 128), BF16),
        sds((length, 256), BF16), sds((width, 768), BF16), sds((256, width), BF16),
        sds((ff, width), BF16), sds((ff, width), BF16),
    ]
    scratch = [
        pltpu.VMEM((rows, width), BF16), pltpu.VMEM((4, 2 * rows, width), BF16), pltpu.VMEM((4, 2 * rows, width), BF16),
        pltpu.VMEM((width, 768), BF16), pltpu.VMEM((256, width), BF16),
        *[pltpu.VMEM((2, length, 128), BF16)] * 3, pltpu.VMEM((length, 256), BF16),
        pltpu.VMEM((rows, width), F32), pltpu.VMEM((rows, width), BF16),
        *scatter_scratch(rows, width),
        dma(10), dma(10), dma(10), dma(10), dma(10), dma(10), dma(9), dma(16), dma(9), dma(11),
    ]
    return pl.pallas_call(
        forward_attention_kernel,
        name="forward_attention",
        out_shape=outs,
        in_specs=[ANY] * 8 + [VM] * 4,
        out_specs=[ANY] * len(outs),
        scratch_shapes=scratch,
        compiler_params=pltpu.CompilerParams(collective_id=0, has_side_effects=True, vmem_limit_bytes=60 * MIB),
    )(*args)


def feed_forward_kernel(
    n2, resid, gm, wg, wg_r, wu, wu_r, wd, g2,
    gr_o, ga_o, gain_o, p2_o, dw_o,
    g_s, gm_s, wg_s, wu_s, wd_s, a_s, b_s, hid_s, dg_s, du_s, hid_t, dg_t, du_t, dw_s, p2_s, resid_s, gr_s, ga_s, gain_s,
    part, own, ra, rb, f1, f2,
    ag_ss, ag_rs, rs_ss, rs_rs, w_ss, w_rs, loc, out_sem,
):
    me = Place()
    c, zl = me.c, me.zl
    rows = n2.shape[0]
    step = 2 * rows
    ff = wd.shape[0]
    stays = c == zl
    swap = {"zl": 1 - zl, "core": 1 - c}
    others = [me.at(dy=1), me.at(dy=-1), me.sibling()]
    others += [me.at(dz=s, core=k) for s in (1, -1) for k in (0, 1)]
    loads = [
        pltpu.make_async_copy(n2, g_s.at[me.y, pl.ds(c * rows, rows)], loc.at[0]),
        pltpu.make_async_copy(gm, gm_s, loc.at[1]),
        pltpu.make_async_copy(resid, resid_s, loc.at[2]),
    ]
    for cp in loads:
        cp.start()
    kept = [pltpu.make_async_copy(a, b, loc.at[4 + i]) for i, (a, b) in enumerate(((wg, wg_s), (wu, wu_s), (wd, wd_s)))]
    fetched = [pltpu.make_async_copy(a, b, loc.at[4 + i]) for i, (a, b) in enumerate(((wg_r, wg_s), (wu_r, wu_s)))]
    meet(others)
    z_other = lax.rem(me.z + jnp.where(zl == 0, 3, 1), 4)
    far_z = {"zh": z_other // 2, "zl": lax.rem(z_other, 2), "core": c}
    hd = ff // 32 * 16
    wd_a = remote(wd.at[pl.ds(0, hd)], wd_s.at[pl.ds(0, hd)], w_ss.at[0], w_rs.at[0], swap)
    wd_b = remote(wd.at[pl.ds(hd, ff - hd)], wd_s.at[pl.ds(hd, ff - hd)], w_ss.at[0], w_rs.at[1], far_z)
    loads[0].wait()
    gather = Gather(me, g_s, ag_ss, ag_rs, rows)
    gather.start()

    @pl.when(stays)
    def _():
        for cp in kept:
            cp.start()
        wd_b.start()
        kept[0].wait()
        kept[1].wait()

    @pl.when(jnp.logical_not(stays))
    def _():
        for cp in fetched:
            cp.start()
        wd_a.start()
        for cp in fetched:
            cp.wait()

    def block(d):
        return me.yy(d)

    def forward(d):
        at = block(d)
        x = g_s[at]
        gate = dot_nt(x, wg_s[...])
        up = dot_nt(x, wu_s[...])
        sigma = jax.nn.sigmoid(gate)
        swish = gate * sigma
        b_s[at] = swish
        a_s[at] = up * sigma * (1.0 + gate * (1.0 - sigma))
        hid_s[at] = (swish * up).astype(BF16)

    gather.got(4)
    forward(0)
    gather.forward_one()
    gather.near()
    gather.got(7)
    forward(-1)
    gather.got(8)
    forward(1)
    gather.far()

    @pl.when(stays)
    def _():
        kept[2].wait()

    @pl.when(jnp.logical_not(stays))
    def _():
        wd_a.wait_recv()
        wd_b.wait_recv()

    for cp in loads[1:]:
        cp.wait()
    gather.got(9)
    forward(2)
    scatter = Scatter(me, part, own, ra, rb, f1, f2, rs_ss, rs_rs, rows)

    def backward(d):
        at = block(d)
        gh = dot_nt(gm_s[at], wd_s[...])
        dg = (gh * a_s[at]).astype(BF16)
        du = (gh * b_s[at]).astype(BF16)
        dg_s[at] = dg
        du_s[at] = du
        part[at] = (dot(dg, wg_s[...]) + dot(du, wu_s[...])).astype(BF16)
        scatter.ready(d)

    backward(2)
    backward(1)
    backward(-1)
    scatter.stage_two()
    backward(0)
    scatter.stage_one()

    def turn(src, dst):
        for i in range(4):
            dst[:, i * step:(i + 1) * step] = src[i].T

    def weight(k, turned, y):
        wide = 512
        for j in range(y.shape[2] // wide):
            cols = slice(j * wide, (j + 1) * wide)
            acc = dot(turned[:, 0:step], y[0, :, cols])
            for i in range(1, 4):
                acc += dot(turned[:, i * step:(i + 1) * step], y[i, :, cols])
            dw_s[k, :, cols] = acc.astype(BF16)

    outs = []

    def out(src, dst):
        cp = pltpu.make_async_copy(src, dst, out_sem.at[len(outs)])
        cp.start()
        outs.append(cp)

    turn(hid_s, hid_t)
    weight(0, hid_t, gm_s)
    out(dw_s.at[0], dw_o.at[0])
    scatter.stage_last()
    turn(dg_s, dg_t)
    weight(1, dg_t, g_s)
    out(dw_s.at[1], dw_o.at[1])
    turn(du_s, du_t)
    weight(2, du_t, g_s)
    out(dw_s.at[2], dw_o.at[2])
    for i in range(4):
        p2_s[i] = dot(hid_s[i], wd_s[...]).astype(BF16)
    out(p2_s, p2_o)
    scatter.result()
    gn = scatter.total(0, rows)
    unit, factor = normed(resid_s[...])
    gain_s[...] = jnp.sum(gn * unit, axis=0, keepdims=True)
    g = gn * g2[...]
    gr = gm_s[me.y, pl.ds(c * rows, rows)].astype(F32) + factor * (g - unit * jnp.mean(g * unit, axis=-1, keepdims=True))
    gr_s[...] = gr
    ga_s[...] = gr.astype(BF16)
    out(gr_s, gr_o)
    out(ga_s, ga_o)
    out(gain_s, gain_o)
    gather.finish()
    scatter.finish()
    for cp in outs:
        cp.wait()

    @pl.when(stays)
    def _():
        wd_b.wait_send()

    @pl.when(jnp.logical_not(stays))
    def _():
        wd_a.wait_send()


def feed_forward(args):
    n2, resid, gm, wg, wg_r, wu, wu_r, wd, g2 = args
    rows, width = n2.shape
    ff = wd.shape[0]
    length = 8 * rows
    sds = jax.ShapeDtypeStruct
    outs = [
        sds((rows, width), F32), sds((rows, width), BF16), sds((1, width), F32),
        sds((4, 2 * rows, width), BF16), sds((3, ff, width), BF16),
    ]
    by_chip = (4, 2 * rows, width)
    hidden = (4, 2 * rows, ff)
    scratch = [
        pltpu.VMEM(by_chip, BF16), pltpu.VMEM(by_chip, BF16),
        *[pltpu.VMEM((ff, width), BF16)] * 3,
        pltpu.VMEM(hidden, F32), pltpu.VMEM(hidden, F32),
        *[pltpu.VMEM(hidden, BF16)] * 3, *[pltpu.VMEM((ff, length), BF16)] * 3,
        pltpu.VMEM((3, ff, width), BF16), pltpu.VMEM(by_chip, BF16),
        pltpu.VMEM((rows, width), F32),
        pltpu.VMEM((rows, width), F32), pltpu.VMEM((rows, width), BF16), pltpu.VMEM((1, width), F32),
        *scatter_scratch(rows, width),
        dma(10), dma(10), dma(10), dma(10), dma(1), dma(2), dma(7), dma(8),
    ]
    return pl.pallas_call(
        feed_forward_kernel,
        name="feed_forward",
        out_shape=outs,
        in_specs=[ANY] * 8 + [VM],
        out_specs=[ANY] * len(outs),
        scratch_shapes=scratch,
        compiler_params=pltpu.CompilerParams(collective_id=1, has_side_effects=True, vmem_limit_bytes=62 * MIB),
    )(*args)


def attention_back_kernel(
    ga, p2, resid, tok, gr, g_one, q, k, v, ho, w3, wo, g1, cosine, sine,
    act_o, grad_o, gain_o, dwo_o, dw3_o,
    ga_s, one_s, q_s, k_s, v_s, ho_s, w3_s, wo_s, gh_s, dk_s, dv_s, g3_s, ho_t, g3_t, dwo_s, dw3_s,
    resid_s, tok_s, gr_s, act_s, gain_s,
    part2, own2, ra2, rb2, f12, f22,
    part, own, ra, rb, f1, f2,
    ag_ss, ag_rs, r2_ss, r2_rs, rs_ss, rs_rs, loc, out_sem,
):
    me = Place()
    c = me.c
    rows = ga.shape[0]
    step = 2 * rows
    meet([me.at(dy=1), me.at(dy=-1), me.sibling()])
    first = pltpu.make_async_copy(ga, ga_s.at[me.y, pl.ds(c * rows, rows)], loc.at[0])
    first.start()
    loads = [
        pltpu.make_async_copy(a, b, loc.at[1 + i])
        for i, (a, b) in enumerate(
            ((p2, part2), (wo, wo_s), (q, q_s), (k, k_s), (v, v_s), (ho, ho_s), (w3, w3_s), (g_one, one_s),
             (resid, resid_s), (tok, tok_s), (gr, gr_s))
        )
    ]
    for cp in loads:
        cp.start()
    first.wait()
    gather = Gather(me, ga_s, ag_ss, ag_rs, rows)
    gather.start()
    for cp in loads:
        cp.wait()

    def heads(d):
        at = me.yy(d)
        out = dot_nt(ga_s[at], wo_s[...]).astype(BF16)
        for half in (0, 1):
            place = pl.ds(pl.multiple_of((at + 4 * half) * rows, rows), rows)
            for head in (0, 1):
                gh_s[head, place] = out[half * rows:(half + 1) * rows, head * 128:head * 128 + 128]

    def turn(src, dst):
        for i in range(4):
            dst[:, i * step:(i + 1) * step] = src[pl.ds(i * step, step)].T

    turn(ho_s, ho_t)
    second = Scatter(me, part2, own2, ra2, rb2, f12, f22, r2_ss, r2_rs, rows)
    for d in second.order:
        second.ready(d)
    gather.got(4)
    heads(0)
    gather.forward_one()
    gather.near()
    second.stage_two()
    second.stage_one()
    gather.got(7)
    heads(-1)
    gather.got(8)
    heads(1)
    gather.far()
    gather.got(9)
    heads(2)

    outs = []

    def out(src, dst):
        cp = pltpu.make_async_copy(src, dst, out_sem.at[len(outs)])
        cp.start()
        outs.append(cp)

    scale = HEAD_DIM ** (-0.5)
    for block in range(4):
        stop = (block + 1) * step
        mine = pl.ds(block * step, step)
        seen = pl.ds(0, stop)
        for head in (0, 1):
            qb = q_s[head, mine]
            gb = gh_s[head, mine]
            s = dot_nt(qb, k_s[head, seen]) * scale
            places = block * step + lax.broadcasted_iota(jnp.int32, (step, stop), 0)
            s = jnp.where(lax.broadcasted_iota(jnp.int32, (step, stop), 1) <= places, s, -1e30)
            e = jnp.exp(s - jnp.max(s, -1, keepdims=True))
            p = e / jnp.sum(e, -1, keepdims=True)
            gp = dot_nt(gb, v_s[head, seen])
            ds = (p * (gp - jnp.sum(p * gp, -1, keepdims=True)) * scale).astype(BF16)
            gv = dot_tn(p.astype(BF16), gb)
            gk = dot_tn(ds, qb)
            gq = dot(ds, k_s[head, seen])
            cs, sn = cosine[mine], sine[mine]
            gq = (gq * cs - pltpu.roll(gq, 64, axis=1) * sn).astype(BF16)
            for half in (0, 1):
                g3_s[pl.ds(perm(2 * block + half) * rows, rows), pl.ds(head * 128, 128)] = gq[half * rows:(half + 1) * rows]
            if block:
                before = pl.ds(0, stop - step)
                dk_s[head, before] += gk[:stop - step]
                dv_s[head, before] += gv[:stop - step]
            dk_s[head, mine] = gk[stop - step:]
            dv_s[head, mine] = gv[stop - step:]
        if block == 1:
            second.stage_last()
    for head in (0, 1):
        for t in range(8):
            place = pl.ds(t * rows, rows)
            to = pl.ds(perm(t) * rows, rows)
            gk = dk_s[head, place]
            gk = gk * cosine[place] - pltpu.roll(gk, 64, axis=1) * sine[place]
            g3_s[to, pl.ds(256 + head * 128, 128)] = gk.astype(BF16)
            g3_s[to, pl.ds(512 + head * 128, 128)] = dv_s[head, place].astype(BF16)

    scatter = Scatter(me, part, own, ra, rb, f1, f2, rs_ss, rs_rs, rows)

    def back(d):
        at = me.yy(d)
        part[at] = dot_nt(g3_s[pl.ds(pl.multiple_of(at * step, step), step)], w3_s[...]).astype(BF16)
        scatter.ready(d)

    back(2)
    back(1)
    back(-1)
    scatter.stage_two()
    back(0)
    scatter.stage_one()

    def weight(dst, turned, y):
        wide = 512
        for j in range(y.shape[2] // wide):
            cols = slice(j * wide, (j + 1) * wide)
            acc = dot(turned[:, 0:step], y[0, :, cols])
            for i in range(1, 4):
                acc += dot(turned[:, i * step:(i + 1) * step], y[i, :, cols])
            dst[:, cols] = acc.astype(BF16)

    turn(g3_s, g3_t)
    weight(dw3_s, g3_t, one_s)
    out(dw3_s, dw3_o)
    scatter.stage_last()
    weight(dwo_s, ho_t, ga_s)
    out(dwo_s, dwo_o)
    second.result()
    act_s[...] = (resid_s[...] + second.total(0, rows)).astype(BF16)
    out(act_s, act_o)
    scatter.result()
    gn = scatter.total(0, rows)
    unit, factor = normed(tok_s[...].astype(F32))
    gain_s[...] = jnp.sum(gn * unit, axis=0, keepdims=True)
    g = gn * g1[...]
    gr_s[...] = gr_s[...] + factor * (g - unit * jnp.mean(g * unit, axis=-1, keepdims=True))
    out(gr_s, grad_o)
    out(gain_s, gain_o)
    gather.finish()
    second.finish()
    scatter.finish()
    for cp in outs:
        cp.wait()


def attention_back(args):
    ga = args[0]
    rows, width = ga.shape
    length = 8 * rows
    sds = jax.ShapeDtypeStruct
    outs = [
        sds((rows, width), BF16), sds((rows, width), F32), sds((1, width), F32),
        sds((256, width), BF16), sds((768, width), BF16),
    ]
    by_chip = (4, 2 * rows, width)
    head = (2, length, 128)
    scratch = [
        pltpu.VMEM(by_chip, BF16), pltpu.VMEM(by_chip, BF16),
        *[pltpu.VMEM(head, BF16)] * 3, pltpu.VMEM((length, 256), BF16),
        pltpu.VMEM((width, 768), BF16), pltpu.VMEM((256, width), BF16),
        pltpu.VMEM(head, BF16), pltpu.VMEM(head, F32), pltpu.VMEM(head, F32),
        pltpu.VMEM((length, 768), BF16), pltpu.VMEM((256, length), BF16), pltpu.VMEM((768, length), BF16),
        pltpu.VMEM((256, width), BF16), pltpu.VMEM((768, width), BF16),
        pltpu.VMEM((rows, width), F32), pltpu.VMEM((rows, width), BF16), pltpu.VMEM((rows, width), F32),
        pltpu.VMEM((rows, width), BF16), pltpu.VMEM((1, width), F32),
        *scatter_scratch(rows, width), *scatter_scratch(rows, width),
        dma(10), dma(10), dma(10), dma(10), dma(10), dma(10), dma(12), dma(5),
    ]
    return pl.pallas_call(
        attention_back_kernel,
        name="attention_back",
        out_shape=outs,
        in_specs=[ANY] * 12 + [VM] * 3,
        out_specs=[ANY] * len(outs),
        scratch_shapes=scratch,
        compiler_params=pltpu.CompilerParams(collective_id=2, has_side_effects=True, vmem_limit_bytes=62 * MIB),
    )(*args)


class Reduce:
    SEMS = 20
    STAGES = 8

    def __init__(self, me, src, dst, bufs, row, n, ss, rs, loc, done):
        self.me, self.src, self.dst, self.n = me, src, dst, n
        b, fold, xa, xb, f1, f2, zs, zr, ag = bufs
        at = pl.ds(row, n)
        ha = n // 32 * 16
        hb = n - ha
        c, zl = me.c, me.zl
        self.keep = c == zl
        wide = src.shape[1] // 2
        q = wide // 4
        self.q = q
        self.b, self.at = b, at
        z_other = lax.rem(me.z + jnp.where(zl == 0, 3, 1), 4)
        near_z = {"zl": 1 - zl, "core": 0 * c}
        far_z = {"zh": z_other // 2, "zl": lax.rem(z_other, 2), "core": 0 * c + 1}
        sib, up, down, z2 = me.sibling(), me.at(dx=1), me.at(dx=-1), {"zh": 1 - me.zh}

        def col(k):
            return pl.ds(pl.multiple_of(k * wide, wide), wide)

        def blk(d):
            return pl.ds(pl.multiple_of(lax.rem(me.x + d + 4, 4) * q, q), q)

        self.blk = blk
        self.rows_a, self.rows_b = pl.ds(row, ha), pl.ds(row + ha, hb)
        ra, rb = self.rows_a, self.rows_b
        self.local = pltpu.make_async_copy(src.at[:, col(c)], b.at[at], loc.at[0])
        self.to_sib = remote(src.at[:, col(1 - c)], b.at[at], ss.at[0], rs.at[0], sib)
        self.give0 = remote(src.at[:, pl.ds(0, wide)], fold.at[at], ss.at[1], rs.at[1], near_z)
        self.give1 = remote(src.at[:, pl.ds(wide, wide)], fold.at[at], ss.at[2], rs.at[1], far_z)
        self.a2 = remote(b.at[ra, blk(2)], xa.at[ra], ss.at[3], rs.at[3], up)
        self.b2 = remote(b.at[rb, blk(2)], xb.at[rb], ss.at[4], rs.at[4], down)
        self.b1 = remote(b.at[rb, blk(1)], f1.at[rb], ss.at[5], rs.at[5], up)
        self.am = remote(b.at[ra, blk(-1)], f2.at[ra], ss.at[6], rs.at[6], down)
        self.a1 = remote(b.at[ra, blk(1)], f1.at[ra], ss.at[7], rs.at[7], up)
        self.bm = remote(b.at[rb, blk(-1)], f2.at[rb], ss.at[8], rs.at[8], down)
        self.zx = remote(zs.at[at], zr.at[at], ss.at[9], rs.at[9], z2)
        self.g = [
            remote(ag.at[r, blk(d)], ag.at[r, blk(d)], ss.at[10 + i], rs.at[10 + i], to)
            for i, (r, d, to) in enumerate(
                ((ra, 0, up), (rb, 0, down), (rb, 0, up), (ra, 0, down), (ra, -1, up), (rb, 1, down))
            )
        ]

        def out(d):
            return pl.ds(pl.multiple_of(c * wide + lax.rem(me.x + d + 4, 4) * q, q), q)

        self.share = [
            remote(ag.at[at, blk(d)], dst.at[:, out(d)], ss.at[16 + i], rs.at[16 + i], sib)
            for i, d in enumerate((0, -1, 1, 2))
        ]
        self.save = pltpu.make_async_copy(ag.at[at], dst.at[:, col(c)], done.at[0])
        self.bufs = bufs

    def stage(self, s):
        getattr(self, f"s{s}")()

    def s0(self):
        @pl.when(self.keep)
        def _():
            self.local.start()
            self.to_sib.start()

        @pl.when(jnp.logical_not(self.keep))
        def _():
            self.give0.start()
            self.give1.start()

    def s1(self):
        @pl.when(self.keep)
        def _():
            self.local.wait()
            self.to_sib.wait_send()

        @pl.when(jnp.logical_not(self.keep))
        def _():
            self.to_sib.wait_recv()
            self.give0.wait_send()
            self.give1.wait_send()

        self.give0.wait_recv()
        b, fold, at = self.b, self.bufs[1], self.at
        b[at] = (b[at].astype(F32) + fold[at].astype(F32)).astype(BF16)
        for cp in (self.a2, self.b2, self.b1, self.am):
            cp.start()

    def plus(self, rows, d, other):
        cols = self.blk(d)
        self.b[rows, cols] = (self.b[rows, cols].astype(F32) + other[rows].astype(F32)).astype(BF16)

    def s2(self):
        self.a2.wait_recv()
        self.plus(self.rows_a, 1, self.bufs[2])
        self.a1.start()
        self.b2.wait_recv()
        self.plus(self.rows_b, -1, self.bufs[3])
        self.bm.start()

    def s3(self):
        for cp in (self.b1, self.am, self.a1, self.bm):
            cp.wait_recv()
        _, _, _, _, f1, f2, zs, _, _ = self.bufs
        at = self.at
        zs[at] = (self.b[at, self.blk(0)].astype(F32) + f1[at].astype(F32) + f2[at].astype(F32)).astype(BF16)
        self.zx.start()

    def s4(self):
        self.zx.wait_recv()
        zs, zr, ag = self.bufs[6:]
        at = self.at
        ag[at, self.blk(0)] = (zs[at].astype(F32) + zr[at].astype(F32)).astype(BF16)
        for i in range(4):
            self.g[i].start()
        self.share[0].start()

    def s5(self):
        self.g[0].wait_recv()
        self.g[4].start()
        self.g[1].wait_recv()
        self.g[5].start()
        self.g[2].wait_recv()
        self.share[1].start()
        self.g[3].wait_recv()
        self.share[2].start()

    def s6(self):
        self.g[4].wait_recv()
        self.g[5].wait_recv()
        self.share[3].start()
        self.save.start()

    def s7(self):
        for cp in self.share:
            cp.wait()
        self.save.wait()
        for cp in (self.a2, self.b2, self.b1, self.am, self.a1, self.bm, self.zx, *self.g):
            cp.wait_send()


def reduce_scratch(total):
    wide = 1024
    return [
        pltpu.VMEM((total, wide), BF16), pltpu.VMEM((total, wide), BF16),
        *[pltpu.VMEM((total, wide // 4), BF16)] * 6, pltpu.VMEM((total, wide), BF16),
    ]


def chunks_of(rows, size):
    count = max(1, round(rows / size))
    ends = [rows * i // count // 16 * 16 for i in range(count)] + [rows]
    return [(a, b - a) for a, b in zip(ends, ends[1:])]


PIECE = 256


def gradient_sums_kernel(
    dw_ff, dw3, dwo, gains, act, grad,
    ff_o, d3_o, do_o, gains_o, act_o, grad_o,
    b, fold, xa, xb, f1, f2, zs, zr, ag, gy, gx, gz, gc, act_s, grad_s,
    ss, rs, loc, done, g_ss, g_rs, t_ss, t_rs, t_loc,
):
    me = Place()
    c, zl = me.c, me.zl
    near = [me.at(dy=1), me.at(dy=-1), me.at(dy=2), me.at(dx=1), me.at(dx=-1), me.at(dx=2), me.at(dz=2), me.sibling()]
    near += [me.at(dz=s, core=k) for s in (1, -1) for k in (0, 1)]
    meet(near)
    stays = c == zl
    swap = {"zl": 1 - zl, "core": 1 - c}
    moves = [remote(a, o, t_ss.at[i], t_rs.at[i], swap) for i, (a, o) in enumerate(((act, act_o), (grad, grad_o)))]
    fetch = [pltpu.make_async_copy(a, v, t_loc.at[i]) for i, (a, v) in enumerate(((act, act_s), (grad, grad_s)))]
    store = [pltpu.make_async_copy(v, o, t_loc.at[i]) for i, (o, v) in enumerate(((act_o, act_s), (grad_o, grad_s)))]

    pieces = []
    row = 0
    for src, dst in ((dw_ff.at[0], ff_o.at[0]), (dw_ff.at[1], ff_o.at[1]), (dw_ff.at[2], ff_o.at[2]), (dw3, d3_o), (dwo, do_o)):
        for start, n in chunks_of(src.shape[0], PIECE):
            k = len(pieces)
            view = pl.ds(start, n)
            pieces.append(Reduce(
                me, src.at[view], dst.at[view], (b, fold, xa, xb, f1, f2, zs, zr, ag), row, n,
                ss.at[k], rs.at[k], loc.at[k], done.at[k],
            ))
            row += n

    places = {"y": me.y, "x": me.x, "z": me.z, "core": c}
    slots = {"y": gy, "x": gx, "z": gz, "core": gc}
    count = 0
    sends = {}
    for axis, steps in (("y", (1, 2, 3)), ("x", (1, 2, 3)), ("z", (1, 2, 3)), ("core", (1,))):
        sends[axis] = []
        for d in steps:
            if axis == "core":
                to = me.sibling()
            elif axis == "z":
                to = me.at(dz=d)
            else:
                to = me.at(**{"d" + axis: d})
            src = gains.at[me.yy(d)] if axis == "y" else slots[axis].at[places[axis]]
            sends[axis].append(remote(src, slots[axis].at[places[axis]], g_ss.at[count], g_rs.at[count], to))
            count += 1

    def gain_begin(axis, value):
        slots[axis][places[axis]] = value
        for cp in sends[axis]:
            cp.start()

    def gain_end(axis):
        for cp in sends[axis]:
            cp.wait()
        ref = slots[axis]
        total = ref[0]
        for i in range(1, ref.shape[0]):
            total = total + ref[i]
        return total

    steps = len(pieces) + Reduce.STAGES - 1
    for t in range(steps):
        for s in reversed(range(Reduce.STAGES)):
            if 0 <= t - s < len(pieces):
                pieces[t - s].stage(s)
        if t == 0:
            @pl.when(stays)
            def _():
                for cp in fetch:
                    cp.start()

            @pl.when(jnp.logical_not(stays))
            def _():
                for cp in moves:
                    cp.start()

            gain_begin("y", gains[me.y])
        if t == 1:
            gain_begin("x", gain_end("y"))

            @pl.when(stays)
            def _():
                for cp in fetch:
                    cp.wait()
                for cp in store:
                    cp.start()
        if t == 2:
            gain_begin("z", gain_end("x"))
        if t == 3:
            gain_begin("core", gain_end("z"))
        if t == 4:
            total = gain_end("core")
            gains_o[...] = total

    @pl.when(stays)
    def _():
        for cp in store:
            cp.wait()

    @pl.when(jnp.logical_not(stays))
    def _():
        for cp in moves:
            cp.wait()


def gradient_sums(args):
    dw_ff, dw3, dwo, gains, act, grad = args
    sds = jax.ShapeDtypeStruct
    outs = [sds(dw_ff.shape, BF16), sds(dw3.shape, BF16), sds(dwo.shape, BF16), sds((8, 256), F32), sds(act.shape, BF16), sds(grad.shape, F32)]
    total = 3 * dw_ff.shape[1] + dw3.shape[0] + dwo.shape[0]
    n = 3 * len(chunks_of(dw_ff.shape[1], PIECE)) + len(chunks_of(dw3.shape[0], PIECE)) + len(chunks_of(dwo.shape[0], PIECE))
    sems = pltpu.SemaphoreType.DMA((n, Reduce.SEMS))
    small = pltpu.SemaphoreType.DMA((n, 1))
    scratch = [
        *reduce_scratch(total),
        pltpu.VMEM((4, 8, 256), F32), pltpu.VMEM((4, 8, 256), F32), pltpu.VMEM((4, 8, 256), F32), pltpu.VMEM((2, 8, 256), F32),
        pltpu.VMEM(act.shape, BF16), pltpu.VMEM(grad.shape, F32),
        sems, sems, small, small, dma(10), dma(10), dma(2), dma(2), dma(2),
    ]
    return pl.pallas_call(
        gradient_sums_kernel,
        name="gradient_sums",
        out_shape=outs,
        in_specs=[ANY] * 3 + [VM] + [ANY] * 2,
        out_specs=[ANY] * 3 + [VM] + [ANY] * 2,
        scratch_shapes=scratch,
        compiler_params=pltpu.CompilerParams(collective_id=3, has_side_effects=True, vmem_limit_bytes=62 * MIB),
    )(*args)


def per_device(tokens, wq, wk, wv, wo, wg, wu, wd, attn_gain, mlp_gain, cotangent):
    tokens, cotangent = tokens[0], cotangent[0]
    length = 8 * tokens.shape[0]
    ff = wd.shape[0]
    cosine, sine = (jnp.asarray(t) for t in tables(length, HEAD_DIM))
    wg, wu = wg.T, wu.T
    g1, g2 = attn_gain[None], mlp_gain[None]
    (resid, n2, tok, gm, one, q, k, v, ho, w3, wo, wg_r, wu_r) = forward_attention(
        (tokens, cotangent, wq, wk, wv, wo, wg, wu, g1, g2, cosine, sine)
    )
    gr, ga, gain_two, p2, dw_ff = feed_forward((n2, resid, gm, wg, wg_r, wu, wu_r, wd, g2))
    act, grad, gain_one, dwo, dw3 = attention_back((ga, p2, resid, tok, gr, one, q, k, v, ho, w3, wo, g1, cosine, sine))
    gains = jnp.concatenate([gain_one, gain_two]).reshape(2, 2, 4, 256).transpose(2, 0, 1, 3).reshape(4, 4, 256)
    gains = jnp.pad(gains, ((0, 0), (0, 4), (0, 0)))
    dw_ff, dw3, dwo, gains, act, grad = gradient_sums((dw_ff, dw3, dwo, gains, act, grad))
    zl = lax.axis_index("zl")
    gains = lax.dynamic_index_in_dim(gains[:4].reshape(2, 2, 256), zl, 1, keepdims=False)
    d3 = dw3.astype(F32).T
    return (
        act[None], grad[None], d3[:, :256], d3[:, 256:512], d3[:, 512:], dwo.astype(F32),
        dw_ff[1].astype(F32).T, dw_ff[2].astype(F32).T, dw_ff[0].astype(F32), gains[0], gains[1],
    )


def solution(mesh):
    split = Mesh(mesh.devices.reshape(4, 2, 2, 2, 4), ("x", "zh", "core", "zl", "y"))
    dp, tensor = ("x", "zh", "core"), ("zl", "y")
    cols, rows, seqs = P(None, tensor), P(tensor, None), P(dp, tensor, None)
    return jax.shard_map(
        per_device,
        mesh=split,
        in_specs=(seqs, cols, cols, cols, rows, cols, cols, rows, P(), P(), seqs),
        out_specs=(seqs, seqs, cols, cols, cols, rows, cols, cols, rows, P(tensor), P(tensor)),
        check_vma=False,
    )
```

```python
import functools

import jax
import jax.numpy as jnp
import numpy as np
from jax import lax
from jax.experimental import pallas as pl
from jax.experimental.pallas import tpu as pltpu
from jax.sharding import Mesh, PartitionSpec as P

HEAD_DIM = 128
NORM_EPS = 1e-05
ROPE_BASE = 10000.0
F32, BF16 = jnp.float32, jnp.bfloat16
MESH = pl.DeviceIdType.MESH
ANY = pl.BlockSpec(memory_space=pl.ANY)
VM = pl.BlockSpec(memory_space=pltpu.VMEM)
MIB = 2**20


def tables(length, head_dim):
    half = head_dim // 2
    freqs = np.float32(ROPE_BASE) ** (-(np.float32(2.0) * np.arange(half, dtype=np.float32)) / np.float32(head_dim))
    angles = np.arange(length, dtype=np.float32)[:, None] * freqs[None, :]
    cosine, sine = np.cos(angles), np.sin(angles)
    return np.concatenate([cosine, cosine], 1), np.concatenate([-sine, sine], 1)


class Place:
    def __init__(self):
        self.x = lax.axis_index("x")
        self.zh = lax.axis_index("zh")
        self.zl = lax.axis_index("zl")
        self.c = lax.axis_index("core")
        self.y = lax.axis_index("y")
        self.z = self.zh * 2 + self.zl

    def at(self, dx=0, dy=0, dz=0, core=None):
        out = {}
        if dx:
            out["x"] = lax.rem(self.x + dx + 4, 4)
        if dy:
            out["y"] = lax.rem(self.y + dy + 4, 4)
        if dz:
            z = lax.rem(self.z + dz + 4, 4)
            out["zh"], out["zl"] = z // 2, lax.rem(z, 2)
        if core is not None:
            out["core"] = core
        return out

    def sibling(self):
        return {"core": 1 - self.c}

    def yy(self, d):
        return lax.rem(self.y + d + 4, 4)


def meet(devices):
    barrier = pltpu.get_barrier_semaphore()
    for d in devices:
        pl.semaphore_signal(barrier, inc=1, device_id=d, device_id_type=MESH)
    pl.semaphore_wait(barrier, len(devices))


def remote(src, dst, ss, rs, device):
    return pltpu.make_async_remote_copy(
        src_ref=src, dst_ref=dst, send_sem=ss, recv_sem=rs, device_id=device, device_id_type=MESH
    )


def dot(a, b):
    return jnp.dot(a, b, preferred_element_type=F32)


def dot_nt(a, b):
    return lax.dot_general(a, b, (((1,), (1,)), ((), ())), preferred_element_type=F32)


def dot_tn(a, b):
    return lax.dot_general(a, b, (((0,), (0,)), ((), ())), preferred_element_type=F32)


def normed(values):
    factor = lax.rsqrt(jnp.mean(values * values, axis=-1, keepdims=True) + NORM_EPS)
    return values * factor, factor


class Gather:
    N = 10

    def __init__(self, me, buf, ss, rs, rows):
        h = rows // 2
        c, y = me.c, me.y

        def part(d, lo, n):
            return buf.at[me.yy(d), pl.ds(c * rows + lo, n)]

        up, down, sib = me.at(dy=1), me.at(dy=-1), me.sibling()
        spec = [
            (0, 0, h, up), (0, h, h, up), (0, h, h, down), (0, 0, h, down), (0, 0, rows, sib),
            (-1, 0, h, up), (1, h, h, down), (-1, 0, rows, sib), (1, 0, rows, sib), (2, 0, rows, sib),
        ]
        self.copies = [remote(part(d, lo, n), part(d, lo, n), ss.at[i], rs.at[i], to) for i, (d, lo, n, to) in enumerate(spec)]

    def start(self):
        for i in (0, 2, 1, 3, 4):
            self.copies[i].start()

    def got(self, i):
        self.copies[i].wait_recv()

    def forward_one(self):
        self.got(0)
        self.copies[5].start()
        self.got(2)
        self.copies[6].start()

    def near(self):
        self.got(1)
        self.copies[7].start()
        self.got(3)
        self.copies[8].start()

    def far(self):
        self.got(5)
        self.got(6)
        self.copies[9].start()

    def finish(self):
        for cp in self.copies:
            cp.wait_send()


class Scatter:
    N = 10

    def __init__(self, me, part, own, ra, rb, f1, f2, ss, rs, rows):
        self.me, self.part, self.own, self.rows = me, part, own, rows
        self.ra, self.rb, self.f1, self.f2 = ra, rb, f1, f2
        self.h = rows // 2
        c = me.c
        up, down, sib = me.at(dy=1), me.at(dy=-1), me.sibling()
        h = self.h
        self.order = (2, 1, -1, 0)
        self.sib = {}
        for i, d in enumerate(self.order):
            self.sib[d] = remote(
                part.at[me.yy(d), pl.ds((1 - c) * rows, rows)], own.at[me.yy(d)], ss.at[i], rs.at[i], sib
            )

        def mine(d, lo):
            return part.at[me.yy(d), pl.ds(c * rows + lo, h)]

        self.a2 = remote(mine(2, 0), ra, ss.at[4], rs.at[4], up)
        self.b2 = remote(mine(2, h), rb, ss.at[5], rs.at[5], down)
        self.b1 = remote(mine(1, h), f1.at[pl.ds(h, h)], ss.at[6], rs.at[6], up)
        self.a1 = remote(mine(1, 0), f1.at[pl.ds(0, h)], ss.at[7], rs.at[7], up)
        self.am = remote(mine(-1, 0), f2.at[pl.ds(0, h)], ss.at[8], rs.at[8], down)
        self.bm = remote(mine(-1, h), f2.at[pl.ds(h, h)], ss.at[9], rs.at[9], down)

    def add(self, d, lo, n, other):
        rows = pl.ds(self.me.c * self.rows + lo, n)
        at = self.me.yy(d)
        self.part[at, rows] = (self.part[at, rows].astype(F32) + other.astype(F32)).astype(BF16)

    def ready(self, d):
        self.sib[d].start()

    def stage_two(self):
        self.sib[2].wait_recv()
        self.add(2, 0, self.rows, self.own[self.me.yy(2)])
        self.a2.start()
        self.b2.start()

    def stage_one(self):
        self.sib[1].wait_recv()
        self.add(1, 0, self.rows, self.own[self.me.yy(1)])
        self.b1.start()
        self.sib[-1].wait_recv()
        self.add(-1, 0, self.rows, self.own[self.me.yy(-1)])
        self.am.start()

    def stage_last(self):
        self.a2.wait_recv()
        self.add(1, 0, self.h, self.ra[...])
        self.a1.start()
        self.b2.wait_recv()
        self.add(-1, self.h, self.h, self.rb[...])
        self.bm.start()

    def result(self):
        self.sib[0].wait_recv()
        for cp in (self.b1, self.am, self.a1, self.bm):
            cp.wait_recv()

    def total(self, lo, n):
        me = self.me
        mine = self.part[me.y, pl.ds(me.c * self.rows + lo, n)].astype(F32)
        near = self.f1[pl.ds(lo, n)].astype(F32) + self.f2[pl.ds(lo, n)].astype(F32)
        return mine + self.own[me.y, pl.ds(lo, n)].astype(F32) + near

    def finish(self):
        for cp in (*self.sib.values(), self.a2, self.b2, self.b1, self.a1, self.am, self.bm):
            cp.wait_send()


def scatter_scratch(rows, width):
    return [
        pltpu.VMEM((4, 2 * rows, width), BF16),
        pltpu.VMEM((4, rows, width), BF16),
        pltpu.VMEM((rows // 2, width), BF16),
        pltpu.VMEM((rows // 2, width), BF16),
        pltpu.VMEM((rows, width), BF16),
        pltpu.VMEM((rows, width), BF16),
    ]


def dma(n):
    return pltpu.SemaphoreType.DMA((n,))


def perm(block):
    return (block % 4) * 2 + block // 4


def forward_attention_kernel(
    tok, cot, wq, wk, wv, wo, wg, wu, g1, g2, cosine, sine,
    resid_o, n2_o, tok_o, gm_o, g_o, q_o, k_o, v_o, ho_o, w3_o, wo_o, wg_o, wu_o,
    tok_s, g_s, gm_s, w3_s, wo_s, q_s, k_s, v_s, ho_s, resid_s, n2_s,
    part, own, ra, rb, f1, f2,
    ag_ss, ag_rs, ag3_ss, ag3_rs, rs_ss, rs_rs, w_ss, w_rs, loc, out_sem,
):
    me = Place()
    c, zl = me.c, me.zl
    rows = tok.shape[0]
    stays = c == zl
    swap = {"zl": 1 - zl, "core": 1 - c}
    others = [me.at(dy=1), me.at(dy=-1), me.sibling()]
    others += [me.at(dz=s, core=k) for s in (1, -1) for k in (0, 1)]
    meet(others)

    z_other = lax.rem(me.z + jnp.where(zl == 0, 3, 1), 4)
    far_z = {"zh": z_other // 2, "zl": lax.rem(z_other, 2), "core": c}

    heads = (wq, wk, wv)

    def halves(i, src, dst_all, axis_rows, near=0.5):
        h = int(axis_rows * near) // 16 * 16
        r = axis_rows - h
        a = remote(src.at[pl.ds(0, h)], dst_all.at[pl.ds(0, h)], w_ss.at[i], w_rs.at[2 * i], swap)
        b = remote(src.at[pl.ds(h, r)], dst_all.at[pl.ds(h, r)], w_ss.at[i], w_rs.at[2 * i + 1], far_z)
        return a, b

    def w3_part(i):
        return w3_s.at[:, pl.ds(256 * i, 256)]

    moved = [halves(i, w, w3_part(i), w.shape[0], 0.42) for i, w in enumerate(heads)]
    later = [halves(3, wo, wo_s, wo.shape[0]), halves(4, wg, wg_o, wg.shape[0]), halves(5, wu, wu_o, wu.shape[0])]
    tok_move = remote(tok, tok_s, w_ss.at[7], w_rs.at[14], swap)
    mine = gm_s.at[me.y, pl.ds(c * rows, rows)]
    cot_move = remote(cot, gm_s.at[me.y, pl.ds((1 - c) * rows, rows)], w_ss.at[8], w_rs.at[15], swap)
    local = [pltpu.make_async_copy(w, w3_part(i), loc.at[i]) for i, w in enumerate(heads)]
    local.append(pltpu.make_async_copy(wo, wo_s, loc.at[3]))
    cot_local = pltpu.make_async_copy(cot, mine, loc.at[4])
    tok_local = pltpu.make_async_copy(tok, tok_s, loc.at[8])

    @pl.when(stays)
    def _():
        tok_local.start()
        for cp in local:
            cp.start()
        cot_local.start()
        for _, b in moved[:2]:
            b.start()
        tok_local.wait()

    @pl.when(jnp.logical_not(stays))
    def _():
        tok_move.start()
        tok_move.wait_send()
        for a, _ in moved[:2]:
            a.start()
        tok_move.wait_recv()

    out_tok = pltpu.make_async_copy(tok_s, tok_o, out_sem.at[0])
    out_tok.start()
    unit, _ = normed(tok_s[...].astype(F32))
    g_s[me.y, pl.ds(c * rows, rows)] = (unit * g1[...]).astype(BF16)

    gather = Gather(me, g_s, ag_ss, ag_rs, rows)
    gather.start()

    @pl.when(stays)
    def _():
        moved[2][1].start()

    @pl.when(jnp.logical_not(stays))
    def _():
        moved[2][0].start()

    def have(i):
        @pl.when(stays)
        def _():
            local[i].wait()

        @pl.when(jnp.logical_not(stays))
        def _():
            for cp in (moved[:3] + later)[i]:
                cp.wait_recv()

    def project(d, lo, hi):
        at = me.yy(d)
        out = dot(g_s[at], w3_s[:, lo * 256:hi * 256])
        for half in (0, 1):
            place = pl.ds(pl.multiple_of((at + 4 * half) * rows, rows), rows)
            for i in range(lo, hi):
                ref = (q_s, k_s, v_s)[i]
                for head in (0, 1):
                    col = (i - lo) * 256 + head * 128
                    v = out[half * rows:(half + 1) * rows, col:col + 128]
                    if i < 2:
                        v = v * cosine[place] + pltpu.roll(v, 64, axis=1) * sine[place]
                    ref[head, place] = v.astype(BF16)

    gather.got(4)
    gather.forward_one()
    have(0)
    have(1)
    project(0, 0, 2)
    gather.near()

    @pl.when(stays)
    def _():
        later[0][1].start()
        cot_local.wait()

    @pl.when(jnp.logical_not(stays))
    def _():
        cot_move.start()
        later[0][0].start()

    gather.got(7)
    project(-1, 0, 2)
    gather.got(8)
    project(1, 0, 2)
    have(2)
    for d in (0, -1, 1):
        project(d, 2, 3)
    gather.far()
    gather.got(9)
    project(2, 0, 3)

    @pl.when(jnp.logical_not(stays))
    def _():
        cot_move.wait_recv()

    third = Gather(me, gm_s, ag3_ss, ag3_rs, rows)
    third.start()

    out_g = pltpu.make_async_copy(g_s, g_o, out_sem.at[1])
    out_g.start()
    outs = [out_tok, out_g]
    for i, (a, b) in enumerate(((q_s, q_o), (k_s, k_o), (v_s, v_o), (w3_s, w3_o))):
        cp = pltpu.make_async_copy(a, b, out_sem.at[2 + i])
        cp.start()
        outs.append(cp)

    scale = HEAD_DIM ** (-0.5)
    step = 2 * rows
    for block in range(4):
        stop = (block + 1) * step
        for head in (0, 1):
            s = dot_nt(q_s[head, pl.ds(block * step, step)], k_s[head, pl.ds(0, stop)]) * scale
            places = block * step + lax.broadcasted_iota(jnp.int32, (step, stop), 0)
            s = jnp.where(lax.broadcasted_iota(jnp.int32, (step, stop), 1) <= places, s, -1e30)
            e = jnp.exp(s - jnp.max(s, -1, keepdims=True))
            p = (e / jnp.sum(e, -1, keepdims=True)).astype(BF16)
            o = dot(p, v_s[head, pl.ds(0, stop)]).astype(BF16)
            for half in (0, 1):
                ho_s[pl.ds(perm(2 * block + half) * rows, rows), pl.ds(head * 128, 128)] = o[half * rows:(half + 1) * rows]
        if block == 0:
            @pl.when(stays)
            def _():
                for _, b in later[1:]:
                    b.start()

            @pl.when(jnp.logical_not(stays))
            def _():
                for a, _ in later[1:]:
                    a.start()

        if block == 1:
            third.got(4)
            third.forward_one()
    have(3)
    for i, (a, b) in enumerate(((ho_s, ho_o), (wo_s, wo_o))):
        cp = pltpu.make_async_copy(a, b, out_sem.at[6 + i])
        cp.start()
        outs.append(cp)

    scatter = Scatter(me, part, own, ra, rb, f1, f2, rs_ss, rs_rs, rows)

    def out_project(d):
        at = me.yy(d)
        part[at] = dot(ho_s[pl.ds(pl.multiple_of(at * 2 * rows, 2 * rows), 2 * rows)], wo_s[...]).astype(BF16)
        scatter.ready(d)

    out_project(2)
    out_project(1)
    out_project(-1)
    scatter.stage_two()
    out_project(0)
    scatter.stage_one()
    third.near()
    scatter.stage_last()
    third.got(7)
    third.got(8)
    third.far()
    third.got(9)
    cp = pltpu.make_async_copy(gm_s, gm_o, out_sem.at[10])
    cp.start()
    outs.append(cp)
    scatter.result()
    resid = tok_s[...].astype(F32) + scatter.total(0, rows)
    resid_s[...] = resid
    unit, _ = normed(resid)
    n2_s[...] = (unit * g2[...]).astype(BF16)
    for i, (a, b) in enumerate(((resid_s, resid_o), (n2_s, n2_o))):
        cp = pltpu.make_async_copy(a, b, out_sem.at[8 + i])
        cp.start()
        outs.append(cp)

    gather.finish()
    third.finish()
    scatter.finish()
    for cp in outs:
        cp.wait()

    @pl.when(stays)
    def _():
        for _, b in moved + later:
            b.wait_send()

    @pl.when(jnp.logical_not(stays))
    def _():
        cot_move.wait_send()
        for a, b in later[1:]:
            a.wait_recv()
            b.wait_recv()
        for a, _ in moved + later:
            a.wait_send()


def forward_attention(args):
    tok, cot, wq, wk, wv, wo, wg, wu, g1, g2, cosine, sine = args
    rows, width = tok.shape
    ff = wg.shape[0]
    length = 8 * rows
    sds = jax.ShapeDtypeStruct
    outs = [
        sds((rows, width), F32), sds((rows, width), BF16), sds((rows, width), BF16), sds((4, 2 * rows, width), BF16),
        sds((4, 2 * rows, width), BF16),
        sds((2, length, 128), BF16), sds((2, length, 128), BF16), sds((2, length, 128), BF16),
        sds((length, 256), BF16), sds((width, 768), BF16), sds((256, width), BF16),
        sds((ff, width), BF16), sds((ff, width), BF16),
    ]
    scratch = [
        pltpu.VMEM((rows, width), BF16), pltpu.VMEM((4, 2 * rows, width), BF16), pltpu.VMEM((4, 2 * rows, width), BF16),
        pltpu.VMEM((width, 768), BF16), pltpu.VMEM((256, width), BF16),
        *[pltpu.VMEM((2, length, 128), BF16)] * 3, pltpu.VMEM((length, 256), BF16),
        pltpu.VMEM((rows, width), F32), pltpu.VMEM((rows, width), BF16),
        *scatter_scratch(rows, width),
        dma(10), dma(10), dma(10), dma(10), dma(10), dma(10), dma(9), dma(16), dma(9), dma(11),
    ]
    return pl.pallas_call(
        forward_attention_kernel,
        name="forward_attention",
        out_shape=outs,
        in_specs=[ANY] * 8 + [VM] * 4,
        out_specs=[ANY] * len(outs),
        scratch_shapes=scratch,
        compiler_params=pltpu.CompilerParams(collective_id=0, has_side_effects=True, vmem_limit_bytes=60 * MIB),
    )(*args)


class Head:
    SEMS = 9

    def __init__(self, me, src, bufs, row, n, ss, rs, loc):
        b, fold, xab, f1, f2 = bufs
        self.b, self.fold, self.xab, self.f1, self.f2 = bufs
        self.at = at = pl.ds(row, n)
        ha = n // 32 * 16
        c, zl = me.c, me.zl
        self.keep = c == zl
        wide = src.shape[1] // 2
        q = wide // 4
        z_other = lax.rem(me.z + jnp.where(zl == 0, 3, 1), 4)
        near_z = {"zl": 1 - zl, "core": 0 * c}
        far_z = {"zh": z_other // 2, "zl": lax.rem(z_other, 2), "core": 0 * c + 1}
        sib, up, down = me.sibling(), me.at(dx=1), me.at(dx=-1)

        def col(k):
            return pl.ds(pl.multiple_of(k * wide, wide), wide)

        def blk(d):
            return pl.ds(pl.multiple_of(lax.rem(me.x + d + 4, 4) * q, q), q)

        self.blk = blk
        self.rows_a, self.rows_b = ra, rb = pl.ds(row, ha), pl.ds(row + ha, n - ha)
        self.local = pltpu.make_async_copy(src.at[:, col(c)], b.at[at], loc)
        self.to_sib = remote(src.at[:, col(1 - c)], b.at[at], ss.at[0], rs.at[0], sib)
        self.give0 = remote(src.at[:, pl.ds(0, wide)], fold.at[at], ss.at[1], rs.at[1], near_z)
        self.give1 = remote(src.at[:, pl.ds(wide, wide)], fold.at[at], ss.at[2], rs.at[1], far_z)
        self.a2 = remote(b.at[ra, blk(2)], xab.at[ra], ss.at[3], rs.at[3], up)
        self.b2 = remote(b.at[rb, blk(2)], xab.at[rb], ss.at[4], rs.at[4], down)
        self.b1 = remote(b.at[rb, blk(1)], f1.at[rb], ss.at[5], rs.at[5], up)
        self.am = remote(b.at[ra, blk(-1)], f2.at[ra], ss.at[6], rs.at[6], down)
        self.a1 = remote(b.at[ra, blk(1)], f1.at[ra], ss.at[7], rs.at[7], up)
        self.bm = remote(b.at[rb, blk(-1)], f2.at[rb], ss.at[8], rs.at[8], down)

    def s0(self):
        @pl.when(self.keep)
        def _():
            self.local.start()
            self.to_sib.start()

        @pl.when(jnp.logical_not(self.keep))
        def _():
            self.give0.start()
            self.give1.start()

    def folded(self):
        @pl.when(self.keep)
        def _():
            self.local.wait()
            self.to_sib.wait_send()

        @pl.when(jnp.logical_not(self.keep))
        def _():
            self.to_sib.wait_recv()
            self.give0.wait_send()
            self.give1.wait_send()

        self.give0.wait_recv()
        at = self.at
        self.b[at] = (self.b[at].astype(F32) + self.fold[at].astype(F32)).astype(BF16)

    def s1(self):
        self.folded()
        self.send()

    def send(self):
        for cp in (self.a2, self.b2, self.b1, self.am):
            cp.start()

    def plus(self, rows, d):
        cols = self.blk(d)
        self.b[rows, cols] = (self.b[rows, cols].astype(F32) + self.xab[rows].astype(F32)).astype(BF16)

    def s2(self):
        self.a2.wait_recv()
        self.plus(self.rows_a, 1)
        self.a1.start()
        self.b2.wait_recv()
        self.plus(self.rows_b, -1)
        self.bm.start()

    def s3(self):
        for cp in (self.b1, self.am, self.a1, self.bm):
            cp.wait_recv()
        at, own = self.at, self.blk(0)
        self.b[at, own] = (self.b[at, own].astype(F32) + self.f1[at].astype(F32) + self.f2[at].astype(F32)).astype(BF16)

    def done(self):
        for cp in (self.a2, self.b2, self.b1, self.am, self.a1, self.bm):
            cp.wait_send()


class Tail:
    SEMS = 11

    def __init__(self, me, own, dst, ag, zr, row, n, ss, rs, done):
        self.own, self.ag, self.zr = own, ag, zr
        self.at = at = pl.ds(row, n)
        ha = n // 32 * 16
        c = me.c
        wide = dst.shape[1] // 2
        q = wide // 4
        sib, up, down = me.sibling(), me.at(dx=1), me.at(dx=-1)

        def place(d):
            return lax.rem(me.x + d + 4, 4) * q

        def blk(d):
            return pl.ds(pl.multiple_of(place(d), q), q)

        def out(d):
            return pl.ds(pl.multiple_of(c * wide + place(d), q), q)

        self.blk = blk
        ra, rb = pl.ds(row, ha), pl.ds(row + ha, n - ha)
        self.zx = remote(own, zr.at[at], ss.at[0], rs.at[0], {"zh": 1 - me.zh})
        self.g = [
            remote(ag.at[r, blk(d)], ag.at[r, blk(d)], ss.at[1 + i], rs.at[1 + i], to)
            for i, (r, d, to) in enumerate(
                ((ra, 0, up), (rb, 0, down), (rb, 0, up), (ra, 0, down), (ra, -1, up), (rb, 1, down))
            )
        ]
        self.share = [
            remote(ag.at[at, blk(d)], dst.at[:, out(d)], ss.at[7 + i], rs.at[7 + i], sib) for i, d in enumerate((0, -1, 1, 2))
        ]
        self.save = pltpu.make_async_copy(ag.at[at], dst.at[:, pl.ds(pl.multiple_of(c * wide, wide), wide)], done)

    def t0(self):
        self.zx.start()

    def t1(self):
        self.zx.wait_recv()
        at = self.at
        self.ag[at, self.blk(0)] = (self.own[...].astype(F32) + self.zr[at].astype(F32)).astype(BF16)
        for cp in self.g[:4]:
            cp.start()
        self.share[0].start()

    def t2(self):
        self.g[0].wait_recv()
        self.g[4].start()
        self.g[1].wait_recv()
        self.g[5].start()
        self.g[2].wait_recv()
        self.share[1].start()
        self.g[3].wait_recv()
        self.share[2].start()

    def t3(self):
        self.g[4].wait_recv()
        self.g[5].wait_recv()
        self.share[3].start()
        self.save.start()

    def t4(self):
        for cp in self.share:
            cp.wait()
        self.save.wait()
        self.zx.wait_send()
        for cp in self.g:
            cp.wait_send()


def chunks_of(rows, size):
    count = max(1, round(rows / size))
    ends = [rows * i // count // 16 * 16 for i in range(count)] + [rows]
    return [(a, b - a) for a, b in zip(ends, ends[1:])]


class Sum:
    def __init__(self, head, tail):
        self.head, self.tail = head, tail
        self.s0, self.s1, self.s2 = head.s0, head.s1, head.s2
        self.t1, self.t2, self.t3 = tail.t1, tail.t2, tail.t3

    def s3(self):
        self.head.s3()
        self.tail.t0()

    def t4(self):
        self.head.done()
        self.tail.t4()


def each(pieces, *stages):
    for stage in stages:
        for piece in pieces:
            getattr(piece, stage)()


def feed_forward_kernel(
    n2, resid, gm, wg, wg_r, wu, wu_r, wd, g2,
    gr_o, ga_o, gain_o, p2_o, z_o, t_o, dw_o,
    g_s, gm_s, wg_s, wu_s, wd_s, a_s, b_s, hid_s, dg_s, du_s, turned, dw_s, cot_s, resid_s, gr_s, ga_s, gain_s,
    red_b, red_f, red_x, red_f1, red_f2,
    part, own, ra, rb, f1, f2,
    ag_ss, ag_rs, rs_ss, rs_rs, w_ss, w_rs, loc, out_sem, red_ss, red_rs, red_loc,
):
    me = Place()
    c, zl = me.c, me.zl
    rows = n2.shape[0]
    step = 2 * rows
    ff = wd.shape[0]
    stays = c == zl
    swap = {"zl": 1 - zl, "core": 1 - c}
    others = [me.at(dy=1), me.at(dy=-1), me.at(dx=1), me.at(dx=-1), me.sibling()]
    others += [me.at(dz=s, core=k) for s in (1, -1) for k in (0, 1)]
    loads = [
        pltpu.make_async_copy(n2, g_s.at[me.y, pl.ds(c * rows, rows)], loc.at[0]),
        pltpu.make_async_copy(gm, gm_s, loc.at[1]),
        pltpu.make_async_copy(resid, resid_s, loc.at[2]),
    ]
    for cp in loads:
        cp.start()
    kept = [pltpu.make_async_copy(a, b, loc.at[4 + i]) for i, (a, b) in enumerate(((wg, wg_s), (wu, wu_s), (wd, wd_s)))]
    fetched = [pltpu.make_async_copy(a, b, loc.at[4 + i]) for i, (a, b) in enumerate(((wg_r, wg_s), (wu_r, wu_s)))]
    meet(others)
    z_other = lax.rem(me.z + jnp.where(zl == 0, 3, 1), 4)
    far_z = {"zh": z_other // 2, "zl": lax.rem(z_other, 2), "core": c}
    hd = ff // 32 * 16
    wd_a = remote(wd.at[pl.ds(0, hd)], wd_s.at[pl.ds(0, hd)], w_ss.at[0], w_rs.at[0], swap)
    wd_b = remote(wd.at[pl.ds(hd, ff - hd)], wd_s.at[pl.ds(hd, ff - hd)], w_ss.at[0], w_rs.at[1], far_z)
    loads[0].wait()
    gather = Gather(me, g_s, ag_ss, ag_rs, rows)
    gather.start()

    @pl.when(stays)
    def _():
        for cp in kept:
            cp.start()
        wd_b.start()
        kept[0].wait()
        kept[1].wait()

    @pl.when(jnp.logical_not(stays))
    def _():
        for cp in fetched:
            cp.start()
        wd_a.start()
        for cp in fetched:
            cp.wait()

    def block(d):
        return me.yy(d)

    def forward(d):
        at = block(d)
        x = g_s[at]
        gate = dot_nt(x, wg_s[...])
        up = dot_nt(x, wu_s[...])
        sigma = jax.nn.sigmoid(gate)
        swish = gate * sigma
        b_s[at] = swish
        a_s[at] = up * sigma * (1.0 + gate * (1.0 - sigma))
        hid_s[at] = (swish * up).astype(BF16)

    gather.got(4)
    forward(0)
    gather.forward_one()
    gather.near()
    gather.got(7)
    forward(-1)
    gather.got(8)
    forward(1)
    gather.far()

    @pl.when(stays)
    def _():
        kept[2].wait()

    @pl.when(jnp.logical_not(stays))
    def _():
        wd_a.wait_recv()
        wd_b.wait_recv()

    for cp in loads[1:]:
        cp.wait()
    gather.got(9)
    forward(2)
    cot_s[...] = gm_s[me.y, pl.ds(c * rows, rows)]
    outs = []

    def out(src, dst):
        cp = pltpu.make_async_copy(src, dst, out_sem.at[len(outs)])
        cp.start()
        outs.append(cp)

    def turn(src):
        for i in range(4):
            turned[:, i * step:(i + 1) * step] = src[i].T

    def weight(k, src, y):
        turn(src)
        wide = 512
        for j in range(y.shape[2] // wide):
            cols = slice(j * wide, (j + 1) * wide)
            acc = dot(turned[:, 0:step], y[0, :, cols])
            for i in range(1, 4):
                acc += dot(turned[:, i * step:(i + 1) * step], y[i, :, cols])
            dw_s[k, :, cols] = acc.astype(BF16)

    def begin(k):
        heads = []
        for start, n in chunks_of(ff, 344):
            s = 2 * k + len(heads)
            heads.append(Head(
                me, dw_s.at[k].at[pl.ds(start, n)], (red_b, red_f, red_x, red_f1, red_f2), k * ff + start, n,
                red_ss.at[s], red_rs.at[s], red_loc.at[s],
            ))
        each(heads, "s0")
        return heads

    weight(0, hid_s, gm_s)
    down = begin(0)
    scatter = Scatter(me, part, own, ra, rb, f1, f2, rs_ss, rs_rs, rows)

    def backward(d):
        at = block(d)
        gh = dot_nt(gm_s[at], wd_s[...])
        dg = (gh * a_s[at]).astype(BF16)
        du = (gh * b_s[at]).astype(BF16)
        dg_s[at] = dg
        du_s[at] = du
        part[at] = (dot(dg, wg_s[...]) + dot(du, wu_s[...])).astype(BF16)
        scatter.ready(d)

    backward(2)
    backward(1)
    backward(-1)
    scatter.stage_two()
    backward(0)
    scatter.stage_one()
    weight(1, dg_s, g_s)
    gate = begin(1)
    scatter.stage_last()
    each(down, "s1")
    weight(2, du_s, g_s)
    out(dw_s.at[2], dw_o)
    for i in range(4):
        gm_s[i] = dot(hid_s[i], wd_s[...]).astype(BF16)
    out(gm_s, p2_o)
    each(down, "s2")
    scatter.result()
    gn = scatter.total(0, rows)
    unit, factor = normed(resid_s[...])
    gain_s[...] = jnp.sum(gn * unit, axis=0, keepdims=True)
    g = gn * g2[...]
    gr = cot_s[...].astype(F32) + factor * (g - unit * jnp.mean(g * unit, axis=-1, keepdims=True))
    gr_s[...] = gr
    ga_s[...] = gr.astype(BF16)
    out(gr_s, gr_o)
    out(ga_s, ga_o)
    out(gain_s, gain_o)
    each(down, "s3")
    out(red_b.at[pl.ds(0, ff), down[0].blk(0)], z_o)
    each(gate, "folded")
    out(red_b.at[pl.ds(ff, ff)], t_o)
    each(down, "done")
    gather.finish()
    scatter.finish()
    for cp in outs:
        cp.wait()

    @pl.when(stays)
    def _():
        wd_b.wait_send()

    @pl.when(jnp.logical_not(stays))
    def _():
        wd_a.wait_send()


def feed_forward(args):
    n2, resid, gm, wg, wg_r, wu, wu_r, wd, g2 = args
    rows, width = n2.shape
    ff = wd.shape[0]
    length = 8 * rows
    sds = jax.ShapeDtypeStruct
    outs = [
        sds((rows, width), F32), sds((rows, width), BF16), sds((1, width), F32),
        sds((4, 2 * rows, width), BF16), sds((ff, width // 8), BF16), sds((ff, width // 2), BF16), sds((ff, width), BF16),
    ]
    by_chip = (4, 2 * rows, width)
    hidden = (4, 2 * rows, ff)
    scratch = [
        pltpu.VMEM(by_chip, BF16), pltpu.VMEM(by_chip, BF16),
        *[pltpu.VMEM((ff, width), BF16)] * 3,
        pltpu.VMEM(hidden, F32), pltpu.VMEM(hidden, F32),
        *[pltpu.VMEM(hidden, BF16)] * 3, pltpu.VMEM((ff, length), BF16),
        pltpu.VMEM((3, ff, width), BF16), pltpu.VMEM((rows, width), BF16),
        pltpu.VMEM((rows, width), F32),
        pltpu.VMEM((rows, width), F32), pltpu.VMEM((rows, width), BF16), pltpu.VMEM((1, width), F32),
        *[pltpu.VMEM((2 * ff, width // 2), BF16)] * 2, *[pltpu.VMEM((2 * ff, width // 8), BF16)] * 3,
        *scatter_scratch(rows, width),
        dma(10), dma(10), dma(10), dma(10), dma(1), dma(2), dma(7), dma(8),
        pltpu.SemaphoreType.DMA((4, Head.SEMS)), pltpu.SemaphoreType.DMA((4, Head.SEMS)), dma(4),
    ]
    return pl.pallas_call(
        feed_forward_kernel,
        name="feed_forward",
        out_shape=outs,
        in_specs=[ANY] * 8 + [VM],
        out_specs=[ANY] * len(outs),
        scratch_shapes=scratch,
        compiler_params=pltpu.CompilerParams(collective_id=1, has_side_effects=True, vmem_limit_bytes=62 * MIB),
    )(*args)


def attention_back_kernel(
    z_part, t_part, dw_u, ga, p2, resid, tok, gr, g_one, q, k, v, ho, w3, wo, g1, cosine, sine, gain_two,
    ff_o, d3_o, do_o, gains_o, act_o, grad_o,
    ga_s, q_s, k_s, v_s, ho_s, w3_s, wo_s, gh_s, dk_s, dv_s, g3_s, ho_t, g3_t, dwo_s, dw3_s,
    resid_s, tok_s, gr_s, act_s,
    zs, tail_ag, tail_z, red_b, red_ag, red_x, red_f1, red_f2, red_z, gpart, gy, gx,
    part2, own2, ra2, rb2, f12, f22,
    part, own, ra, rb, f1, f2,
    ag_ss, ag_rs, r2_ss, r2_rs, rs_ss, rs_rs, loc, tail_ss, tail_rs, tail_done, red_ss, red_rs, red_loc, red_done, g_ss, g_rs, t_ss, t_rs, t_loc,
):
    me = Place()
    c = me.c
    rows = ga.shape[0]
    step = 2 * rows
    zl = me.zl
    near = [{**me.at(dy=d), "core": lax.rem(c + s, 2)} for d in range(4) for s in (0, 1) if d or s]
    near += [me.at(dx=d, dz=s) for d in range(4) for s in range(4) if d or s]
    near += [me.at(dz=s, core=1 - c) for s in (1, -1)]
    meet(near)
    stays = c == zl
    swap = {"zl": 1 - zl, "core": 1 - c}
    first = pltpu.make_async_copy(ga, ga_s.at[me.y, pl.ds(c * rows, rows)], loc.at[0])
    first.start()
    z_load = pltpu.make_async_copy(z_part, zs, loc.at[12])
    z_load.start()
    ff = dw_u.shape[0]
    t_load = pltpu.make_async_copy(t_part, red_b.at[pl.ds(0, ff)], loc.at[13])
    t_load.start()
    loads = [
        pltpu.make_async_copy(a, b, loc.at[1 + i])
        for i, (a, b) in enumerate(
            ((p2, part2), (wo, wo_s), (q, q_s), (k, k_s), (v, v_s), (ho, ho_s), (w3, w3_s),
             (resid, resid_s), (tok, tok_s), (gr, gr_s))
        )
    ]
    for cp in loads:
        cp.start()
    first.wait()
    gather = Gather(me, ga_s, ag_ss, ag_rs, rows)
    gather.start()
    count = [0]

    def sums(src, dst, row, size):
        out = []
        for start, n in chunks_of(src.shape[0], size):
            i = count[0]
            count[0] += 1
            view = pl.ds(start, n)
            head = Head(
                me, src.at[view], (red_b, red_ag, red_x, red_f1, red_f2), row + start, n,
                red_ss.at[i, pl.ds(0, Head.SEMS)], red_rs.at[i, pl.ds(0, Head.SEMS)], red_loc.at[i],
            )
            own = red_b.at[pl.ds(row + start, n), head.blk(0)]
            sems = pl.ds(Head.SEMS, Tail.SEMS)
            tail = Tail(me, own, dst.at[view], red_ag, red_z, row + start, n, red_ss.at[i, sems], red_rs.at[i, sems], red_done.at[i])
            out.append(Sum(head, tail))
        return out

    down = [
        Tail(me, zs.at[pl.ds(start, n)], ff_o.at[0].at[pl.ds(start, n)], tail_ag, tail_z, start, n, tail_ss.at[i], tail_rs.at[i], tail_done.at[i])
        for i, (start, n) in enumerate(chunks_of(ff, 344))
    ]
    gate = sums(dw_u, ff_o.at[1], 0, 344)
    up = sums(dw_u, ff_o.at[2], ff, 344)
    heads_sum = sums(dwo_s, do_o, 2 * ff, 256)
    three = sums(dw3_s, d3_o, 2 * ff + 256, 384)
    z_load.wait()
    each(down, "t0")
    t_load.wait()
    for p in gate:
        p.head.send()
    for cp in loads:
        cp.wait()

    def heads(d):
        at = me.yy(d)
        out = dot_nt(ga_s[at], wo_s[...]).astype(BF16)
        for half in (0, 1):
            place = pl.ds(pl.multiple_of((at + 4 * half) * rows, rows), rows)
            for head in (0, 1):
                gh_s[head, place] = out[half * rows:(half + 1) * rows, head * 128:head * 128 + 128]

    def turn(src, dst):
        for i in range(4):
            dst[:, i * step:(i + 1) * step] = src[pl.ds(i * step, step)].T

    turn(ho_s, ho_t)
    second = Scatter(me, part2, own2, ra2, rb2, f12, f22, r2_ss, r2_rs, rows)
    for d in second.order:
        second.ready(d)
    gather.got(4)
    heads(0)
    gather.forward_one()
    each(up, "s0")
    gather.near()
    second.stage_two()
    second.stage_one()
    each(gate, "s2")
    each(down, "t1")
    gather.got(7)
    heads(-1)
    gather.got(8)
    heads(1)
    gather.far()
    gather.got(9)
    heads(2)

    def weight(dst, turned, y):
        wide = 512
        for j in range(y.shape[2] // wide):
            cols = slice(j * wide, (j + 1) * wide)
            acc = dot(turned[:, 0:step], y[0, :, cols])
            for i in range(1, 4):
                acc += dot(turned[:, i * step:(i + 1) * step], y[i, :, cols])
            dst[:, cols] = acc.astype(BF16)

    weight(dwo_s, ho_t, ga_s)
    each(gate, "s3")
    each(heads_sum, "s0")
    gather.finish()
    load_one = pltpu.make_async_copy(g_one, ga_s, loc.at[11])
    load_one.start()
    scale = HEAD_DIM ** (-0.5)
    for block in range(4):
        stop = (block + 1) * step
        mine = pl.ds(block * step, step)
        seen = pl.ds(0, stop)
        for head in (0, 1):
            qb = q_s[head, mine]
            gb = gh_s[head, mine]
            s = dot_nt(qb, k_s[head, seen]) * scale
            places = block * step + lax.broadcasted_iota(jnp.int32, (step, stop), 0)
            s = jnp.where(lax.broadcasted_iota(jnp.int32, (step, stop), 1) <= places, s, -1e30)
            e = jnp.exp(s - jnp.max(s, -1, keepdims=True))
            p = e / jnp.sum(e, -1, keepdims=True)
            gp = dot_nt(gb, v_s[head, seen])
            ds = (p * (gp - jnp.sum(p * gp, -1, keepdims=True)) * scale).astype(BF16)
            gv = dot_tn(p.astype(BF16), gb)
            gk = dot_tn(ds, qb)
            gq = dot(ds, k_s[head, seen])
            cs, sn = cosine[mine], sine[mine]
            gq = (gq * cs - pltpu.roll(gq, 64, axis=1) * sn).astype(BF16)
            for half in (0, 1):
                g3_s[pl.ds(perm(2 * block + half) * rows, rows), pl.ds(head * 128, 128)] = gq[half * rows:(half + 1) * rows]
            if block:
                before = pl.ds(0, stop - step)
                dk_s[head, before] += gk[:stop - step]
                dv_s[head, before] += gv[:stop - step]
            dk_s[head, mine] = gk[stop - step:]
            dv_s[head, mine] = gv[stop - step:]
        if block == 2:
            second.stage_last()
            each(up, "s1")
    each(down, "t2")
    for head in (0, 1):
        for t in range(8):
            place = pl.ds(t * rows, rows)
            to = pl.ds(perm(t) * rows, rows)
            gk = dk_s[head, place]
            gk = gk * cosine[place] - pltpu.roll(gk, 64, axis=1) * sine[place]
            g3_s[to, pl.ds(256 + head * 128, 128)] = gk.astype(BF16)
            g3_s[to, pl.ds(512 + head * 128, 128)] = dv_s[head, place].astype(BF16)

    turn(g3_s, g3_t)
    load_one.wait()
    weight(dw3_s, g3_t, ga_s)
    each(three, "s0")
    each(up, "s2")
    each(gate, "t1")
    each(heads_sum, "s1")
    scatter = Scatter(me, part, own, ra, rb, f1, f2, rs_ss, rs_rs, rows)

    def back(d):
        at = me.yy(d)
        part[at] = dot_nt(g3_s[pl.ds(pl.multiple_of(at * step, step), step)], w3_s[...]).astype(BF16)
        scatter.ready(d)

    back(2)
    back(1)
    back(-1)
    scatter.stage_two()
    back(0)
    scatter.stage_one()

    each(up, "s3")
    each(down, "t3")
    each(gate, "t2")
    scatter.stage_last()
    each(heads_sum, "s2")
    three[0].s1()
    each(up, "t1")
    three[1].s1()
    each(heads_sum, "s3")
    each(gate, "t3")
    three[0].s2()
    three[1].s2()
    three[0].s3()
    each(heads_sum, "t1")
    each(up, "t2")
    second.result()
    act_s[...] = (resid_s[...] + second.total(0, rows)).astype(BF16)
    three[1].s3()
    scatter.result()
    gn = scatter.total(0, rows)
    unit, factor = normed(tok_s[...].astype(F32))
    gains = (jnp.sum(gn * unit, axis=0, keepdims=True), gain_two[...])
    for i in range(4):
        for j in range(2):
            for zi in range(2):
                lo = (zi * 4 + i) * 256
                gpart[i, 2 * j + zi:2 * j + zi + 1] = gains[j][:, lo:lo + 256]
    g = gn * g1[...]
    gr_s[...] = gr_s[...] + factor * (g - unit * jnp.mean(g * unit, axis=-1, keepdims=True))
    moves = [remote(a, o, t_ss.at[i], t_rs.at[i], swap) for i, (a, o) in enumerate(((act_s, act_o), (gr_s, grad_o)))]
    store = [pltpu.make_async_copy(a, o, t_loc.at[i]) for i, (a, o) in enumerate(((act_s, act_o), (gr_s, grad_o)))]

    @pl.when(stays)
    def _():
        for cp in store:
            cp.start()

    @pl.when(jnp.logical_not(stays))
    def _():
        for cp in moves:
            cp.start()

    here = me.x * 4 + me.z
    gains_a, gains_b = [], []
    for d in range(4):
        for s in (0, 1):
            if d or s:
                to = {**me.at(dy=d), "core": lax.rem(c + s, 2)}
                i = len(gains_a)
                gains_a.append(remote(gpart.at[me.yy(d)], gy.at[me.y * 2 + c], g_ss.at[i], g_rs.at[i], to))
    for d in range(4):
        for s in range(4):
            if d or s:
                i = 7 + len(gains_b)
                gains_b.append(remote(gx.at[here], gx.at[here], g_ss.at[i], g_rs.at[i], me.at(dx=d, dz=s)))

    def gain_total(sends, ref):
        for cp in sends:
            cp.wait()
        total = ref[0]
        for i in range(1, ref.shape[0]):
            total = total + ref[i]
        return total

    gy[me.y * 2 + c] = gpart[me.y]
    for cp in gains_a:
        cp.start()
    three[0].t1()
    gx[here] = gain_total(gains_a, gy)
    for cp in gains_b:
        cp.start()
    each(heads_sum, "t2")
    each(up, "t3")
    three[1].t1()
    three[0].t2()
    each(heads_sum, "t3")
    three[1].t2()
    three[0].t3()
    gains_o[...] = gain_total(gains_b, gx)
    three[1].t3()
    each(down, "t4")
    each(up, "t4")
    each(heads_sum, "t4")
    each(three, "t4")
    for p in gate:
        p.t4()
    second.finish()
    scatter.finish()

    @pl.when(stays)
    def _():
        for cp in store:
            cp.wait()

    @pl.when(jnp.logical_not(stays))
    def _():
        for cp in moves:
            cp.wait()


def attention_back(args):
    dw_u, ga = args[2:4]
    ff = dw_u.shape[0]
    rows, width = ga.shape
    length = 8 * rows
    sds = jax.ShapeDtypeStruct
    outs = [
        sds((3, ff, width), BF16), sds((768, width), BF16), sds((256, width), BF16), sds((8, 256), F32),
        sds((rows, width), BF16), sds((rows, width), F32),
    ]
    total = 2 * ff + 1024
    sem = pltpu.SemaphoreType.DMA
    many = sem((9, Head.SEMS + Tail.SEMS))
    half, eighth = width // 2, width // 8
    sums = [
        pltpu.VMEM((ff, eighth), BF16), pltpu.VMEM((ff, half), BF16), pltpu.VMEM((ff, eighth), BF16),
        *[pltpu.VMEM((total, half), BF16)] * 2, *[pltpu.VMEM((total, eighth), BF16)] * 4,
    ]
    part = pltpu.VMEM((4, 8, 256), F32)
    by_chip = (4, 2 * rows, width)
    head = (2, length, 128)
    scratch = [
        pltpu.VMEM(by_chip, BF16),
        *[pltpu.VMEM(head, BF16)] * 3, pltpu.VMEM((length, 256), BF16),
        pltpu.VMEM((width, 768), BF16), pltpu.VMEM((256, width), BF16),
        pltpu.VMEM(head, BF16), pltpu.VMEM(head, F32), pltpu.VMEM(head, F32),
        pltpu.VMEM((length, 768), BF16), pltpu.VMEM((256, length), BF16), pltpu.VMEM((768, length), BF16),
        pltpu.VMEM((256, width), BF16), pltpu.VMEM((768, width), BF16),
        pltpu.VMEM((rows, width), F32), pltpu.VMEM((rows, width), BF16), pltpu.VMEM((rows, width), F32),
        pltpu.VMEM((rows, width), BF16),
        *sums, part, pltpu.VMEM((8, 8, 256), F32), pltpu.VMEM((16, 8, 256), F32),
        *scatter_scratch(rows, width), *scatter_scratch(rows, width),
        dma(10), dma(10), dma(10), dma(10), dma(10), dma(10), dma(14), sem((2, Tail.SEMS)), sem((2, Tail.SEMS)), dma(2), many, many, dma(9), dma(9), dma(22), dma(22), dma(2), dma(2), dma(2),
    ]
    return pl.pallas_call(
        attention_back_kernel,
        name="attention_back",
        out_shape=outs,
        in_specs=[ANY] * 15 + [VM] * 4,
        out_specs=[ANY] * 3 + [VM] + [ANY] * 2,
        scratch_shapes=scratch,
        compiler_params=pltpu.CompilerParams(collective_id=2, has_side_effects=True, vmem_limit_bytes=62 * MIB),
    )(*args)


def widen_kernel(ff, three, out, d_o, g_o, u_o, q_o, k_o, v_o, o_o):
    for i, ref in enumerate((d_o, g_o, u_o)):
        ref[...] = ff[i].astype(F32)
    for i, ref in enumerate((q_o, k_o, v_o)):
        ref[...] = three[256 * i:256 * i + 256].astype(F32).T
    o_o[...] = out[...].astype(F32)


def widen(ff, three, out):
    _, n, width = ff.shape
    step = 256
    cols = lambda r: pl.BlockSpec((r, step), lambda j: (0, j))
    turned = pl.BlockSpec((step, 256), lambda j: (j, 0))
    sds = jax.ShapeDtypeStruct
    return pl.pallas_call(
        widen_kernel,
        name="widen",
        grid=(width // step,),
        out_shape=[sds((n, width), F32)] * 3 + [sds((width, 256), F32)] * 3 + [sds((256, width), F32)],
        in_specs=[pl.BlockSpec((3, n, step), lambda j: (0, 0, j)), cols(768), cols(256)],
        out_specs=[cols(n)] * 3 + [turned] * 3 + [cols(256)],
        compiler_params=pltpu.CompilerParams(vmem_limit_bytes=62 * MIB),
    )(ff, three, out)


def per_device(tokens, wq, wk, wv, wo, wg, wu, wd, attn_gain, mlp_gain, cotangent):
    tokens, cotangent = tokens[0], cotangent[0]
    length = 8 * tokens.shape[0]
    ff = wd.shape[0]
    cosine, sine = (jnp.asarray(t) for t in tables(length, HEAD_DIM))
    wg, wu = wg.T, wu.T
    g1, g2 = attn_gain[None], mlp_gain[None]
    (resid, n2, tok, gm, one, q, k, v, ho, w3, wo, wg_r, wu_r) = forward_attention(
        (tokens, cotangent, wq, wk, wv, wo, wg, wu, g1, g2, cosine, sine)
    )
    gr, ga, gain_two, p2, z_part, t_part, dw_u = feed_forward((n2, resid, gm, wg, wg_r, wu, wu_r, wd, g2))
    dw_ff, dw3, dwo, gains, act, grad = attention_back(
        (z_part, t_part, dw_u, ga, p2, resid, tok, gr, one, q, k, v, ho, w3, wo, g1, cosine, sine, gain_two)
    )
    zl = lax.axis_index("zl")
    gains = lax.dynamic_index_in_dim(gains[:4].reshape(2, 2, 256), zl, 1, keepdims=False)
    d_down, d_gate, d_up, d_query, d_key, d_value, d_out = widen(dw_ff, dw3, dwo)
    return act[None], grad[None], d_query, d_key, d_value, d_out, d_gate.T, d_up.T, d_down, gains[0], gains[1]


def solution(mesh):
    split = Mesh(mesh.devices.reshape(4, 2, 2, 2, 4), ("x", "zh", "core", "zl", "y"))
    dp, tensor = ("x", "zh", "core"), ("zl", "y")
    cols, rows, seqs = P(None, tensor), P(tensor, None), P(dp, tensor, None)
    return jax.shard_map(
        per_device,
        mesh=split,
        in_specs=(seqs, cols, cols, cols, rows, cols, cols, rows, P(), P(), seqs),
        out_specs=(seqs, seqs, cols, cols, cols, rows, cols, cols, rows, P(tensor), P(tensor)),
        check_vma=False,
    )
```

```python
import functools

import jax
import jax.numpy as jnp
import numpy as np
from jax import lax
from jax.experimental import pallas as pl
from jax.experimental.pallas import tpu as pltpu
from jax.sharding import Mesh, PartitionSpec as P

HEAD_DIM = 128
NORM_EPS = 1e-05
ROPE_BASE = 10000.0
F32, BF16 = jnp.float32, jnp.bfloat16
MESH = pl.DeviceIdType.MESH
ANY = pl.BlockSpec(memory_space=pl.ANY)
VM = pl.BlockSpec(memory_space=pltpu.VMEM)
MIB = 2**20


def tables(length, head_dim):
    half = head_dim // 2
    freqs = np.float32(ROPE_BASE) ** (-(np.float32(2.0) * np.arange(half, dtype=np.float32)) / np.float32(head_dim))
    angles = np.arange(length, dtype=np.float32)[:, None] * freqs[None, :]
    cosine, sine = np.cos(angles), np.sin(angles)
    return np.concatenate([cosine, cosine], 1), np.concatenate([-sine, sine], 1)


class Place:
    def __init__(self):
        self.x = lax.axis_index("x")
        self.zh = lax.axis_index("zh")
        self.zl = lax.axis_index("zl")
        self.c = lax.axis_index("core")
        self.y = lax.axis_index("y")
        self.z = self.zh * 2 + self.zl

    def at(self, dx=0, dy=0, dz=0, core=None):
        out = {}
        if dx:
            out["x"] = lax.rem(self.x + dx + 4, 4)
        if dy:
            out["y"] = lax.rem(self.y + dy + 4, 4)
        if dz:
            z = lax.rem(self.z + dz + 4, 4)
            out["zh"], out["zl"] = z // 2, lax.rem(z, 2)
        if core is not None:
            out["core"] = core
        return out

    def sibling(self):
        return {"core": 1 - self.c}

    def yy(self, d):
        return lax.rem(self.y + d + 4, 4)


def meet(devices):
    barrier = pltpu.get_barrier_semaphore()
    for d in devices:
        pl.semaphore_signal(barrier, inc=1, device_id=d, device_id_type=MESH)
    pl.semaphore_wait(barrier, len(devices))


def remote(src, dst, ss, rs, device):
    return pltpu.make_async_remote_copy(
        src_ref=src, dst_ref=dst, send_sem=ss, recv_sem=rs, device_id=device, device_id_type=MESH
    )


def dot(a, b):
    return jnp.dot(a, b, preferred_element_type=F32)


def dot_nt(a, b):
    return lax.dot_general(a, b, (((1,), (1,)), ((), ())), preferred_element_type=F32)


def dot_tn(a, b):
    return lax.dot_general(a, b, (((0,), (0,)), ((), ())), preferred_element_type=F32)


def normed(values):
    factor = lax.rsqrt(jnp.mean(values * values, axis=-1, keepdims=True) + NORM_EPS)
    return values * factor, factor


class Gather:
    N = 10

    def __init__(self, me, buf, ss, rs, rows):
        h = rows // 2
        c, y = me.c, me.y

        def part(d, lo, n):
            return buf.at[me.yy(d), pl.ds(c * rows + lo, n)]

        up, down, sib = me.at(dy=1), me.at(dy=-1), me.sibling()
        spec = [
            (0, 0, h, up), (0, h, h, up), (0, h, h, down), (0, 0, h, down), (0, 0, rows, sib),
            (-1, 0, h, up), (1, h, h, down), (-1, 0, rows, sib), (1, 0, rows, sib), (2, 0, rows, sib),
        ]
        self.copies = [remote(part(d, lo, n), part(d, lo, n), ss.at[i], rs.at[i], to) for i, (d, lo, n, to) in enumerate(spec)]

    def start(self):
        for i in (0, 2, 1, 3, 4):
            self.copies[i].start()

    def got(self, i):
        self.copies[i].wait_recv()

    def forward_one(self):
        self.got(0)
        self.copies[5].start()
        self.got(2)
        self.copies[6].start()

    def near(self):
        self.got(1)
        self.copies[7].start()
        self.got(3)
        self.copies[8].start()

    def far(self):
        self.got(5)
        self.got(6)
        self.copies[9].start()

    def finish(self):
        for cp in self.copies:
            cp.wait_send()


class Scatter:
    N = 10

    def __init__(self, me, part, own, ra, rb, f1, f2, ss, rs, rows):
        self.me, self.part, self.own, self.rows = me, part, own, rows
        self.ra, self.rb, self.f1, self.f2 = ra, rb, f1, f2
        self.h = rows // 2
        c = me.c
        up, down, sib = me.at(dy=1), me.at(dy=-1), me.sibling()
        h = self.h
        self.order = (2, 1, -1, 0)
        self.sib = {}
        for i, d in enumerate(self.order):
            self.sib[d] = remote(
                part.at[me.yy(d), pl.ds((1 - c) * rows, rows)], own.at[me.yy(d)], ss.at[i], rs.at[i], sib
            )

        def mine(d, lo):
            return part.at[me.yy(d), pl.ds(c * rows + lo, h)]

        self.a2 = remote(mine(2, 0), ra, ss.at[4], rs.at[4], up)
        self.b2 = remote(mine(2, h), rb, ss.at[5], rs.at[5], down)
        self.b1 = remote(mine(1, h), f1.at[pl.ds(h, h)], ss.at[6], rs.at[6], up)
        self.a1 = remote(mine(1, 0), f1.at[pl.ds(0, h)], ss.at[7], rs.at[7], up)
        self.am = remote(mine(-1, 0), f2.at[pl.ds(0, h)], ss.at[8], rs.at[8], down)
        self.bm = remote(mine(-1, h), f2.at[pl.ds(h, h)], ss.at[9], rs.at[9], down)

    def add(self, d, lo, n, other):
        rows = pl.ds(self.me.c * self.rows + lo, n)
        at = self.me.yy(d)
        self.part[at, rows] = (self.part[at, rows].astype(F32) + other.astype(F32)).astype(BF16)

    def ready(self, d):
        self.sib[d].start()

    def stage_two(self):
        self.sib[2].wait_recv()
        self.add(2, 0, self.rows, self.own[self.me.yy(2)])
        self.a2.start()
        self.b2.start()

    def stage_one(self):
        self.sib[1].wait_recv()
        self.add(1, 0, self.rows, self.own[self.me.yy(1)])
        self.b1.start()
        self.sib[-1].wait_recv()
        self.add(-1, 0, self.rows, self.own[self.me.yy(-1)])
        self.am.start()

    def stage_last(self):
        self.a2.wait_recv()
        self.add(1, 0, self.h, self.ra[...])
        self.a1.start()
        self.b2.wait_recv()
        self.add(-1, self.h, self.h, self.rb[...])
        self.bm.start()

    def result(self):
        self.sib[0].wait_recv()
        for cp in (self.b1, self.am, self.a1, self.bm):
            cp.wait_recv()

    def total(self, lo, n):
        me = self.me
        mine = self.part[me.y, pl.ds(me.c * self.rows + lo, n)].astype(F32)
        near = self.f1[pl.ds(lo, n)].astype(F32) + self.f2[pl.ds(lo, n)].astype(F32)
        return mine + self.own[me.y, pl.ds(lo, n)].astype(F32) + near

    def finish(self):
        for cp in (*self.sib.values(), self.a2, self.b2, self.b1, self.a1, self.am, self.bm):
            cp.wait_send()


def scatter_scratch(rows, width):
    return [
        pltpu.VMEM((4, 2 * rows, width), BF16),
        pltpu.VMEM((4, rows, width), BF16),
        pltpu.VMEM((rows // 2, width), BF16),
        pltpu.VMEM((rows // 2, width), BF16),
        pltpu.VMEM((rows, width), BF16),
        pltpu.VMEM((rows, width), BF16),
    ]


def dma(n):
    return pltpu.SemaphoreType.DMA((n,))


class Head:
    SEMS = 9

    def __init__(self, me, src, bufs, row, n, ss, rs, loc):
        b, fold, xab, f1, f2 = bufs
        self.b, self.fold, self.xab, self.f1, self.f2 = bufs
        self.at = at = pl.ds(row, n)
        ha = n // 32 * 16
        c, zl = me.c, me.zl
        self.keep = c == zl
        wide = src.shape[1] // 2
        q = wide // 4
        z_other = lax.rem(me.z + jnp.where(zl == 0, 3, 1), 4)
        near_z = {"zl": 1 - zl, "core": 0 * c}
        far_z = {"zh": z_other // 2, "zl": lax.rem(z_other, 2), "core": 0 * c + 1}
        sib, up, down = me.sibling(), me.at(dx=1), me.at(dx=-1)

        def col(k):
            return pl.ds(pl.multiple_of(k * wide, wide), wide)

        def blk(d):
            return pl.ds(pl.multiple_of(lax.rem(me.x + d + 4, 4) * q, q), q)

        self.blk = blk
        self.rows_a, self.rows_b = ra, rb = pl.ds(row, ha), pl.ds(row + ha, n - ha)
        self.local = pltpu.make_async_copy(src.at[:, col(c)], b.at[at], loc)
        self.to_sib = remote(src.at[:, col(1 - c)], b.at[at], ss.at[0], rs.at[0], sib)
        self.give0 = remote(src.at[:, pl.ds(0, wide)], fold.at[at], ss.at[1], rs.at[1], near_z)
        self.give1 = remote(src.at[:, pl.ds(wide, wide)], fold.at[at], ss.at[2], rs.at[1], far_z)
        self.a2 = remote(b.at[ra, blk(2)], xab.at[ra], ss.at[3], rs.at[3], up)
        self.b2 = remote(b.at[rb, blk(2)], xab.at[rb], ss.at[4], rs.at[4], down)
        self.b1 = remote(b.at[rb, blk(1)], f1.at[rb], ss.at[5], rs.at[5], up)
        self.am = remote(b.at[ra, blk(-1)], f2.at[ra], ss.at[6], rs.at[6], down)
        self.a1 = remote(b.at[ra, blk(1)], f1.at[ra], ss.at[7], rs.at[7], up)
        self.bm = remote(b.at[rb, blk(-1)], f2.at[rb], ss.at[8], rs.at[8], down)

    def s0(self):
        @pl.when(self.keep)
        def _():
            self.local.start()
            self.to_sib.start()

        @pl.when(jnp.logical_not(self.keep))
        def _():
            self.give0.start()
            self.give1.start()

    def folded(self):
        @pl.when(self.keep)
        def _():
            self.local.wait()
            self.to_sib.wait_send()

        @pl.when(jnp.logical_not(self.keep))
        def _():
            self.to_sib.wait_recv()
            self.give0.wait_send()
            self.give1.wait_send()

        self.give0.wait_recv()
        at = self.at
        self.b[at] = (self.b[at].astype(F32) + self.fold[at].astype(F32)).astype(BF16)

    def s1(self):
        self.folded()
        self.send()

    def send(self):
        for cp in (self.a2, self.b2, self.b1, self.am):
            cp.start()

    def plus(self, rows, d):
        cols = self.blk(d)
        self.b[rows, cols] = (self.b[rows, cols].astype(F32) + self.xab[rows].astype(F32)).astype(BF16)

    def s2(self):
        self.a2.wait_recv()
        self.plus(self.rows_a, 1)
        self.a1.start()
        self.b2.wait_recv()
        self.plus(self.rows_b, -1)
        self.bm.start()

    def s3(self):
        for cp in (self.b1, self.am, self.a1, self.bm):
            cp.wait_recv()
        at, own = self.at, self.blk(0)
        self.b[at, own] = (self.b[at, own].astype(F32) + self.f1[at].astype(F32) + self.f2[at].astype(F32)).astype(BF16)

    def done(self):
        for cp in (self.a2, self.b2, self.b1, self.am, self.a1, self.bm):
            cp.wait_send()


class Tail:
    SEMS = 11

    def __init__(self, me, own, dst, ag, zr, row, n, ss, rs, done):
        self.own, self.ag, self.zr = own, ag, zr
        self.at = at = pl.ds(row, n)
        ha = n // 32 * 16
        c = me.c
        wide = dst.shape[1] // 2
        q = wide // 4
        sib, up, down = me.sibling(), me.at(dx=1), me.at(dx=-1)

        def place(d):
            return lax.rem(me.x + d + 4, 4) * q

        def blk(d):
            return pl.ds(pl.multiple_of(place(d), q), q)

        def out(d):
            return pl.ds(pl.multiple_of(c * wide + place(d), q), q)

        self.blk = blk
        ra, rb = pl.ds(row, ha), pl.ds(row + ha, n - ha)
        self.zx = remote(own, zr.at[at], ss.at[0], rs.at[0], {"zh": 1 - me.zh})
        self.g = [
            remote(ag.at[r, blk(d)], ag.at[r, blk(d)], ss.at[1 + i], rs.at[1 + i], to)
            for i, (r, d, to) in enumerate(
                ((ra, 0, up), (rb, 0, down), (rb, 0, up), (ra, 0, down), (ra, -1, up), (rb, 1, down))
            )
        ]
        self.share = [
            remote(ag.at[at, blk(d)], dst.at[:, out(d)], ss.at[7 + i], rs.at[7 + i], sib) for i, d in enumerate((0, -1, 1, 2))
        ]
        self.save = pltpu.make_async_copy(ag.at[at], dst.at[:, pl.ds(pl.multiple_of(c * wide, wide), wide)], done)

    def t0(self):
        self.zx.start()

    def t1(self):
        self.zx.wait_recv()
        at = self.at
        self.ag[at, self.blk(0)] = (self.own[...].astype(F32) + self.zr[at].astype(F32)).astype(BF16)
        for cp in self.g[:4]:
            cp.start()
        self.share[0].start()

    def t2(self):
        self.g[0].wait_recv()
        self.g[4].start()
        self.g[1].wait_recv()
        self.g[5].start()
        self.g[2].wait_recv()
        self.share[1].start()
        self.g[3].wait_recv()
        self.share[2].start()

    def t3(self):
        self.g[4].wait_recv()
        self.g[5].wait_recv()
        self.share[3].start()
        self.save.start()

    def t4(self):
        for cp in self.share:
            cp.wait()
        self.save.wait()
        self.zx.wait_send()
        for cp in self.g:
            cp.wait_send()


def chunks_of(rows, size):
    count = max(1, round(rows / size))
    ends = [rows * i // count // 16 * 16 for i in range(count)] + [rows]
    return [(a, b - a) for a, b in zip(ends, ends[1:])]


class Sum:
    def __init__(self, head, tail):
        self.head, self.tail = head, tail
        self.s0, self.s1, self.s2 = head.s0, head.s1, head.s2
        self.send = head.send
        self.t1, self.t2, self.t3 = tail.t1, tail.t2, tail.t3

    def s3(self):
        self.head.s3()
        self.tail.t0()

    def t4(self):
        self.head.done()
        self.tail.t4()


def each(pieces, *stages):
    for stage in stages:
        for piece in pieces:
            getattr(piece, stage)()


def perm(block):
    return (block % 4) * 2 + block // 4


def layer_kernel(
    tok, cot, wq, wk, wv, wo, wg, wu, wd, g1, g2, cosine, sine,
    resid_o, tok_o, g_o, q_o, k_o, v_o, ho_o, w3_o, wo_o, gr_o, ga_o, gain_o, p2_o, z_o, t_o, dw_o,
    tok_s, g_s, gm_s, pool, q_s, k_s, v_s, ho_s, resid_s, wg_s, wu_s, wd_s,
    a_s, b_s, hid_s, dg_s, du_s, turned, dw_s, cot_s, gr_s, ga_s, gain_s,
    red_f, red_x, red_f1, red_f2, part, own, ra, rb, f1, f2,
    ag_ss, ag_rs, ag3_ss, ag3_rs, rs_ss, rs_rs, ag2_ss, ag2_rs, rs3_ss, rs3_rs,
    w_ss, w_rs, loc, out_sem, red_ss, red_rs, red_loc,
):
    me = Place()
    c, zl = me.c, me.zl
    rows = tok.shape[0]
    stays = c == zl
    swap = {"zl": 1 - zl, "core": 1 - c}
    others = [me.at(dy=1), me.at(dy=-1), me.at(dx=1), me.at(dx=-1), me.at(dx=2), me.sibling()]
    others += [me.at(dz=s, core=k) for s in (1, -1) for k in (0, 1)]
    width = tok.shape[1]
    ff = wd.shape[0]
    step = 2 * rows
    w3_s = pool.at[:, pl.ds(0, 768)]
    wo_s = dw_s.at[2, pl.ds(0, 256)]
    red_b = pool.at[pl.ds(0, 2 * ff)]
    meet(others)

    z_other = lax.rem(me.z + jnp.where(zl == 0, 3, 1), 4)
    far_z = {"zh": z_other // 2, "zl": lax.rem(z_other, 2), "core": c}

    heads = (wq, wk, wv)

    def halves(i, src, dst_all, axis_rows, near=0.5):
        h = int(axis_rows * near) // 16 * 16
        r = axis_rows - h
        a = remote(src.at[pl.ds(0, h)], dst_all.at[pl.ds(0, h)], w_ss.at[i], w_rs.at[2 * i], swap)
        b = remote(src.at[pl.ds(h, r)], dst_all.at[pl.ds(h, r)], w_ss.at[i], w_rs.at[2 * i + 1], far_z)
        return a, b

    def w3_part(i):
        return pool.at[:, pl.ds(256 * i, 256)]

    moved = [halves(i, w, w3_part(i), w.shape[0], 0.42) for i, w in enumerate(heads)]
    later = [halves(3, wo, wo_s, wo.shape[0]), halves(4, wg, wg_s, ff), halves(5, wu, wu_s, ff)]
    quarter = pl.ds(pl.multiple_of(me.x * (width // 4), width // 4), width // 4)
    later.append(halves(6, wd.at[:, quarter], wd_s.at[:, quarter], ff))
    spread = [
        remote(wd_s.at[:, quarter], wd_s.at[:, quarter], w_ss.at[8 + d], w_rs.at[15 + d], me.at(dx=d)) for d in (1, 2, 3)
    ]
    tok_move = remote(tok, tok_s, w_ss.at[7], w_rs.at[14], swap)
    mine = gm_s.at[me.y, pl.ds(c * rows, rows)]
    cot_move = remote(cot, gm_s.at[me.y, pl.ds((1 - c) * rows, rows)], w_ss.at[8], w_rs.at[15], swap)
    local = [pltpu.make_async_copy(w, w3_part(i), loc.at[i]) for i, w in enumerate(heads)]
    local.append(pltpu.make_async_copy(wo, wo_s, loc.at[3]))
    cot_local = pltpu.make_async_copy(cot, mine, loc.at[4])
    kept = [pltpu.make_async_copy(a, b, loc.at[5 + i]) for i, (a, b) in enumerate(((wg, wg_s), (wu, wu_s), (wd, wd_s)))]
    tok_local = pltpu.make_async_copy(tok, tok_s, loc.at[8])

    @pl.when(stays)
    def _():
        tok_local.start()
        for cp in local:
            cp.start()
        cot_local.start()
        for cp in kept:
            cp.start()
        for _, b in moved[:2]:
            b.start()
        tok_local.wait()

    @pl.when(jnp.logical_not(stays))
    def _():
        tok_move.start()
        tok_move.wait_send()
        for a, _ in moved[:2]:
            a.start()
        tok_move.wait_recv()

    out_tok = pltpu.make_async_copy(tok_s, tok_o, out_sem.at[0])
    out_tok.start()
    unit, _ = normed(tok_s[...].astype(F32))
    g_s[me.y, pl.ds(c * rows, rows)] = (unit * g1[...]).astype(BF16)

    gather = Gather(me, g_s, ag_ss, ag_rs, rows)
    gather.start()

    @pl.when(stays)
    def _():
        moved[2][1].start()

    @pl.when(jnp.logical_not(stays))
    def _():
        moved[2][0].start()

    def have(i):
        @pl.when(stays)
        def _():
            local[i].wait()

        @pl.when(jnp.logical_not(stays))
        def _():
            for cp in (moved[:3] + later)[i]:
                cp.wait_recv()

    def project(d, lo, hi):
        at = me.yy(d)
        out = dot(g_s[at], pool[:, lo * 256:hi * 256])
        for half in (0, 1):
            place = pl.ds(pl.multiple_of((at + 4 * half) * rows, rows), rows)
            for i in range(lo, hi):
                ref = (q_s, k_s, v_s)[i]
                for head in (0, 1):
                    col = (i - lo) * 256 + head * 128
                    v = out[half * rows:(half + 1) * rows, col:col + 128]
                    if i < 2:
                        v = v * cosine[place] + pltpu.roll(v, 64, axis=1) * sine[place]
                    ref[head, place] = v.astype(BF16)

    gather.got(4)
    gather.forward_one()
    have(0)
    have(1)
    project(0, 0, 2)
    gather.near()

    @pl.when(stays)
    def _():
        later[0][1].start()
        later[3][1].start()
        cot_local.wait()

    @pl.when(jnp.logical_not(stays))
    def _():
        later[0][0].start()
        later[3][0].start()

    gather.got(7)
    project(-1, 0, 2)
    gather.got(8)
    project(1, 0, 2)
    have(2)
    for d in (0, -1, 1):
        project(d, 2, 3)
    gather.far()
    gather.got(9)
    project(2, 0, 3)

    third = Gather(me, gm_s, ag3_ss, ag3_rs, rows)

    @pl.when(stays)
    def _():
        third.start()

    @pl.when(jnp.logical_not(stays))
    def _():
        cot_move.start()


    def out(src, dst):
        cp = pltpu.make_async_copy(src, dst, out_sem.at[len(outs) + 1])
        cp.start()
        outs.append(cp)

    out_g = pltpu.make_async_copy(g_s, g_o, out_sem.at[17])
    out_g.start()
    outs = [out_tok]
    for a, b in ((q_s, q_o), (k_s, k_o), (v_s, v_o), (w3_s, w3_o)):
        out(a, b)

    scale = HEAD_DIM ** (-0.5)
    for block in range(4):
        stop = (block + 1) * step
        for head in (0, 1):
            s = dot_nt(q_s[head, pl.ds(block * step, step)], k_s[head, pl.ds(0, stop)]) * scale
            places = block * step + lax.broadcasted_iota(jnp.int32, (step, stop), 0)
            s = jnp.where(lax.broadcasted_iota(jnp.int32, (step, stop), 1) <= places, s, -1e30)
            e = jnp.exp(s - jnp.max(s, -1, keepdims=True))
            p = (e / jnp.sum(e, -1, keepdims=True)).astype(BF16)
            o = dot(p, v_s[head, pl.ds(0, stop)]).astype(BF16)
            for half in (0, 1):
                ho_s[pl.ds(perm(2 * block + half) * rows, rows), pl.ds(head * 128, 128)] = o[half * rows:(half + 1) * rows]
        if block == 0:
            @pl.when(stays)
            def _():
                for _, b in later[1:3]:
                    b.start()

            @pl.when(jnp.logical_not(stays))
            def _():
                for a, _ in later[1:3]:
                    a.start()

        if block == 2:
            pl.when(stays)(third.forward_one)
    have(3)

    @pl.when(jnp.logical_not(stays))
    def _():
        for cp in later[3]:
            cp.wait_recv()
        for cp in spread:
            cp.start()

    out(ho_s, ho_o)
    out(wo_s, wo_o)
    keep_w3, keep_wo = outs[4], outs[6]

    scatter = Scatter(me, part, own, ra, rb, f1, f2, rs_ss, rs_rs, rows)
    gather.finish()
    out_g.wait()

    def out_project(d):
        at = me.yy(d)
        part[at] = dot(ho_s[pl.ds(pl.multiple_of(at * 2 * rows, 2 * rows), 2 * rows)], dw_s[2, 0:256]).astype(BF16)
        scatter.ready(d)

    out_project(2)
    out_project(1)
    out_project(-1)
    scatter.stage_two()
    out_project(0)
    scatter.stage_one()
    pl.when(stays)(third.near)

    scatter.stage_last()

    @pl.when(jnp.logical_not(stays))
    def _():
        cot_move.wait_recv()
        third.start()

    scatter.result()
    resid = tok_s[...].astype(F32) + scatter.total(0, rows)
    resid_s[...] = resid
    unit, _ = normed(resid)
    g_s[me.y, pl.ds(c * rows, rows)] = (unit * g2[...]).astype(BF16)
    keep_w3.wait()
    keep_wo.wait()
    gather = Gather(me, g_s, ag2_ss, ag2_rs, rows)
    gather.start()
    out(resid_s, resid_o)
    scatter.finish()

    def block(d):
        return me.yy(d)

    def forward(d):
        at = block(d)
        x = g_s[at]
        gate = dot_nt(x, wg_s[...])
        up = dot_nt(x, wu_s[...])
        sigma = jax.nn.sigmoid(gate)
        swish = gate * sigma
        b_s[at] = swish.astype(BF16)
        a_s[at] = (up * sigma * (1.0 + gate * (1.0 - sigma))).astype(BF16)
        hid_s[at] = (swish * up).astype(BF16)

    def weight_here(i):
        @pl.when(stays)
        def _():
            kept[i].wait()

        @pl.when(jnp.logical_not(stays))
        def _():
            for cp in (later[1], later[2], spread)[i]:
                cp.wait_recv()

    def slot(j, d):
        turned[:, j * step:(j + 1) * step] = hid_s[block(d)].T

    def hidden_back(d):
        at = block(d)
        gh = dot_nt(gm_s[at], wd_s[...])
        dg_s[at] = (gh * a_s[at].astype(F32)).astype(BF16)
        du_s[at] = (gh * b_s[at].astype(F32)).astype(BF16)

    wide = 512
    near = (0, -1, 1)
    gather.got(4)
    weight_here(0)
    weight_here(1)
    forward(0)
    gather.forward_one()
    weight_here(2)
    slot(0, 0)
    third.got(4)
    hidden_back(0)
    @pl.when(jnp.logical_not(stays))
    def _():
        third.forward_one()
        third.near()

    gather.near()
    gather.got(7)
    forward(-1)
    slot(1, -1)
    gather.got(8)
    forward(1)
    slot(2, 1)
    gather.far()
    third.got(7)
    third.got(8)
    third.far()
    hidden_back(-1)
    hidden_back(1)
    for j in range(gm_s.shape[2] // wide):
        cols = slice(j * wide, (j + 1) * wide)
        acc = dot(turned[:, 0:step], gm_s[block(0), :, cols])
        for i in (1, 2):
            acc += dot(turned[:, i * step:(i + 1) * step], gm_s[block(near[i]), :, cols])
        dw_s[0, :, cols] = acc.astype(BF16)
    cot_s[...] = gm_s[me.y, pl.ds(c * rows, rows)]

    def turn(src):
        for i in range(4):
            turned[:, i * step:(i + 1) * step] = src[i].T

    def weight(k, src, y):
        turn(src)
        for j in range(y.shape[2] // wide):
            cols = slice(j * wide, (j + 1) * wide)
            acc = dot(turned[:, 0:step], y[0, :, cols])
            for i in range(1, 4):
                acc += dot(turned[:, i * step:(i + 1) * step], y[i, :, cols])
            dw_s[k, :, cols] = acc.astype(BF16)

    def pieces(k, parts):
        heads = []
        for start, n in parts:
            s = 2 * k + len(heads)
            heads.append(Head(
                me, dw_s.at[k].at[pl.ds(start, n)], (pool, red_f, red_x, red_f1, red_f2), k * ff + start, n,
                red_ss.at[s], red_rs.at[s], red_loc.at[s],
            ))
        return heads

    cuts = chunks_of(ff, ff / 2)
    (down0, down1), gate = pieces(0, cuts), pieces(1, cuts)
    scatter = Scatter(me, part, own, ra, rb, f1, f2, rs3_ss, rs3_rs, rows)

    def back(d):
        at = block(d)
        part[at] = (dot(dg_s[at], wg_s[...]) + dot(du_s[at], wu_s[...])).astype(BF16)
        scatter.ready(d)

    gather.got(9)
    forward(2)
    slot(3, 2)
    third.got(9)
    for j in range(gm_s.shape[2] // wide):
        cols = slice(j * wide, (j + 1) * wide)
        last = dot(turned[:, 3 * step:4 * step], gm_s[block(2), :, cols])
        dw_s[0, :, cols] = (dw_s[0, :, cols].astype(F32) + last).astype(BF16)
    down0.s0()
    hidden_back(2)
    back(2)
    back(1)
    down1.s0()
    scatter.stage_two()
    back(-1)
    back(0)
    scatter.stage_one()
    down0.s1()
    weight(1, dg_s, g_s)
    each(gate, "s0")
    scatter.stage_last()
    down1.s1()
    weight(2, du_s, g_s)
    down0.s2()
    out(dw_s.at[2], dw_o)
    third.finish()
    for i in range(4):
        gm_s[i] = dot(hid_s[i], wd_s[...]).astype(BF16)
    out(gm_s, p2_o)
    down1.s2()
    down0.s3()
    scatter.result()
    gn = scatter.total(0, rows)
    unit, factor = normed(resid_s[...])
    gain_s[...] = jnp.sum(gn * unit, axis=0, keepdims=True)
    g = gn * g2[...]
    gr = cot_s[...].astype(F32) + factor * (g - unit * jnp.mean(g * unit, axis=-1, keepdims=True))
    gr_s[...] = gr
    ga_s[...] = gr.astype(BF16)
    out(gr_s, gr_o)
    out(ga_s, ga_o)
    out(gain_s, gain_o)
    down1.s3()
    out(pool.at[pl.ds(0, ff), down0.blk(0)], z_o)
    each(gate, "folded")
    out(pool.at[pl.ds(ff, ff)], t_o)
    down0.done()
    down1.done()
    gather.finish()
    scatter.finish()
    for cp in outs:
        if cp is not keep_w3 and cp is not keep_wo:
            cp.wait()

    @pl.when(stays)
    def _():
        for _, b in moved + later:
            b.wait_send()

    @pl.when(jnp.logical_not(stays))
    def _():
        cot_move.wait_send()
        for a, _ in moved + later:
            a.wait_send()
        for cp in spread:
            cp.wait_send()


def layer(args):
    tok, cot, wq, wk, wv, wo, wg, wu, wd, g1, g2, cosine, sine = args
    rows, width = tok.shape
    ff = wd.shape[0]
    length = 8 * rows
    by_chip, hidden, head = (4, 2 * rows, width), (4, 2 * rows, ff), (2, length, 128)
    sds = jax.ShapeDtypeStruct
    outs = [
        sds((rows, width), F32), sds((rows, width), BF16), sds(by_chip, BF16),
        *[sds(head, BF16)] * 3, sds((length, 256), BF16), sds((width, 768), BF16), sds((256, width), BF16),
        sds((rows, width), F32), sds((rows, width), BF16), sds((1, width), F32),
        sds(by_chip, BF16), sds((ff, width // 8), BF16), sds((ff, width // 2), BF16), sds((ff, width), BF16),
    ]
    sem = pltpu.SemaphoreType.DMA
    scratch = [
        pltpu.VMEM((rows, width), BF16), pltpu.VMEM(by_chip, BF16), pltpu.VMEM(by_chip, BF16),
        pltpu.VMEM((width, width // 2), BF16), *[pltpu.VMEM(head, BF16)] * 3, pltpu.VMEM((length, 256), BF16),
        pltpu.VMEM((rows, width), F32), *[pltpu.VMEM((ff, width), BF16)] * 3,
        pltpu.VMEM(hidden, BF16), pltpu.VMEM(hidden, BF16),
        *[pltpu.VMEM(hidden, BF16)] * 3, pltpu.VMEM((ff, length), BF16),
        pltpu.VMEM((3, ff, width), BF16), pltpu.VMEM((rows, width), BF16),
        pltpu.VMEM((rows, width), F32), pltpu.VMEM((rows, width), BF16), pltpu.VMEM((1, width), F32),
        pltpu.VMEM((2 * ff, width // 2), BF16), *[pltpu.VMEM((2 * ff, width // 8), BF16)] * 3,
        *scatter_scratch(rows, width),
        *[dma(10)] * 10, dma(12), dma(19), dma(9), dma(18), sem((4, Head.SEMS)), sem((4, Head.SEMS)), dma(4),
    ]
    return pl.pallas_call(
        layer_kernel,
        name="layer",
        out_shape=outs,
        in_specs=[ANY] * 9 + [VM] * 4,
        out_specs=[ANY] * len(outs),
        scratch_shapes=scratch,
        compiler_params=pltpu.CompilerParams(collective_id=0, has_side_effects=True, vmem_limit_bytes=63 * MIB),
    )(*args)


DOWN_PARTS, GATE_PARTS, UP_PARTS, THREE_PARTS = 2, 2, 2, 2
ORDER = {
    "start": (
        ("up0", "s0"), ("up1", "s0"), ("gate0", "send"), ("gate1", "send"), ("down0", "t0"), ("down1", "t0"),
    ),
    "fwd1": (
        ("up0", "s1"),
    ),
    "2two": (
        ("gate0", "s2"),
    ),
    "2one": (
        ("gate1", "s2"),
    ),
    "far": (
        ("up0", "s2"), ("down0", "t1"), ("up1", "s1"), ("gate0", "s3"),
    ),
    "heads2": (
        ("down1", "t1"), ("gate1", "s3"), ("up0", "s3"),
    ),
    "dwo": (
        ("dwo0", "s0"),
    ),
    "att0": (
        ("gate0", "t1"),
    ),
    "att1": (
        ("gate1", "t1"), ("up1", "s2"),
    ),
    "dw3a": (
        ("up0", "t1"), ("threea0", "s0"), ("threea1", "s0"),
    ),
    "att3": (
        ("dwo0", "s1"),
    ),
    "dw3b": (
        ("up1", "s3"), ("threea0", "s1"), ("threeb0", "s0"), ("threeb1", "s0"),
    ),
    "back3": (
        ("dwo0", "s2"), ("threea1", "s1"), ("up1", "t1"),
    ),
    "back0": (
        ("dwo0", "s3"), ("threea0", "s2"), ("threeb0", "s1"), ("threea1", "s2"),
    ),
    "one": (
        ("threeb1", "s1"), ("threea0", "s3"),
    ),
    "last": (
        ("threeb0", "s2"), ("dwo0", "t1"),
    ),
    "act": (
        ("threea1", "s3"), ("threeb1", "s2"), ("threea0", "t1"), ("threeb0", "s3"), ("up0", "t2"), ("up1", "t2"),
        ("down0", "t2"), ("threeb1", "s3"), ("dwo0", "t2"),
    ),
    "res": (
        ("threea1", "t1"), ("threeb0", "t1"), ("threeb1", "t1"),
    ),
    "gtot": (
        ("threea0", "t2"), ("down1", "t2"), ("threea1", "t2"), ("gate0", "t2"), ("gate1", "t2"),
    ),
    "gend": (
        ("threeb0", "t2"), ("threeb1", "t2"), ("down0", "t3"), ("down1", "t3"), ("up0", "t3"), ("up1", "t3"),
        ("dwo0", "t3"), ("gate0", "t3"), ("gate1", "t3"), ("threea0", "t3"), ("threea1", "t3"), ("threeb0", "t3"),
        ("threeb1", "t3"), ("down0", "t4"), ("down1", "t4"), ("up0", "t4"), ("up1", "t4"), ("dwo0", "t4"),
        ("gate0", "t4"), ("gate1", "t4"), ("threea0", "t4"), ("threea1", "t4"), ("threeb0", "t4"), ("threeb1", "t4"),
    ),
}


def attention_back_kernel(
    z_part, t_part, dw_u, ga, p2, resid, tok, gr, g_one, q, k, v, ho, w3, wo, g1, cosine, sine, gain_two,
    ff_o, d3_o, do_o, gains_o, act_o, grad_o,
    ga_s, q_s, k_s, v_s, ho_s, w3_s, wo_s, gh_s, dk_s, dv_s, g3_s, ho_t, g3_t, dwo_s, dw3_s,
    resid_s, tok_s, gr_s, act_s,
    zs, tail_ag, tail_z, red_b, red_ag, red_x, red_f1, red_f2, red_z, gpart, gy, gx,
    part2, own2, ra2, rb2, f12, f22,
    part, own, ra, rb, f1, f2,
    ag_ss, ag_rs, r2_ss, r2_rs, rs_ss, rs_rs, loc, tail_ss, tail_rs, tail_done, red_ss, red_rs, red_loc, red_done, g_ss, g_rs, t_ss, t_rs, t_loc,
):
    me = Place()
    c = me.c
    rows = ga.shape[0]
    step = 2 * rows
    zl = me.zl
    near = [{**me.at(dy=d), "core": lax.rem(c + s, 2)} for d in range(4) for s in (0, 1) if d or s]
    near += [me.at(dx=d, dz=s) for d in range(4) for s in range(4) if d or s]
    near += [me.at(dz=s, core=1 - c) for s in (1, -1)]
    meet(near)
    stays = c == zl
    swap = {"zl": 1 - zl, "core": 1 - c}
    first = pltpu.make_async_copy(ga, ga_s.at[me.y, pl.ds(c * rows, rows)], loc.at[0])
    first.start()
    z_load = pltpu.make_async_copy(z_part, zs, loc.at[12])
    z_load.start()
    ff = dw_u.shape[0]
    t_load = pltpu.make_async_copy(t_part, red_b.at[pl.ds(0, ff)], loc.at[13])
    t_load.start()
    loads = [
        pltpu.make_async_copy(a, b, loc.at[1 + i])
        for i, (a, b) in enumerate(
            ((p2, part2), (wo, wo_s), (q, q_s), (k, k_s), (v, v_s), (ho, ho_s),
             (resid, resid_s), (tok, tok_s), (gr, gr_s))
        )
    ]
    for i in range(6):
        head, kind = divmod(i, 3)
        at = pl.ds(head * 384 + kind * 128, 128)
        loads.append(pltpu.make_async_copy(w3.at[:, pl.ds(kind * 256 + head * 128, 128)], w3_s.at[:, at], loc.at[14 + i]))
    for cp in loads:
        cp.start()
    first.wait()
    gather = Gather(me, ga_s, ag_ss, ag_rs, rows)
    gather.start()
    count = [0]
    pieces = {}

    def whole(name, src, dst, row):
        n = dst.shape[0]
        i = count[0]
        count[0] += 1
        head = Head(
            me, src, (red_b, red_ag, red_x, red_f1, red_f2), row, n,
            red_ss.at[i, pl.ds(0, Head.SEMS)], red_rs.at[i, pl.ds(0, Head.SEMS)], red_loc.at[i],
        )
        own = red_b.at[pl.ds(row, n), head.blk(0)]
        sems = pl.ds(Head.SEMS, Tail.SEMS)
        tail = Tail(me, own, dst, red_ag, red_z, row, n, red_ss.at[i, sems], red_rs.at[i, sems], red_done.at[i])
        pieces[name] = Sum(head, tail)

    def parts(name, src, dst, row, pieces_of):
        for j, (start, n) in enumerate(chunks_of(dst.shape[0], dst.shape[0] / pieces_of)):
            whole(f"{name}{j}", src.at[pl.ds(start, n)], dst.at[pl.ds(start, n)], row + start)

    for i, (start, n) in enumerate(chunks_of(ff, ff / DOWN_PARTS)):
        pieces[f"down{i}"] = Tail(
            me, zs.at[pl.ds(start, n)], ff_o.at[0].at[pl.ds(start, n)], tail_ag, tail_z, start, n,
            tail_ss.at[i], tail_rs.at[i], tail_done.at[i],
        )
    parts("gate", dw_u, ff_o.at[1], 0, GATE_PARTS)
    parts("up", dw_u, ff_o.at[2], ff, UP_PARTS)
    parts("dwo", dwo_s, do_o, 2 * ff, 1)
    for j in (0, 1):
        parts("three" + "ab"[j], dw3_s.at[pl.ds(384 * j, 384)], d3_o.at[pl.ds(384 * j, 384)], 2 * ff + 256 + 384 * j, THREE_PARTS)

    def after(step):
        for name, stage in ORDER.get(step, ()):
            getattr(pieces[name], stage)()

    z_load.wait()
    t_load.wait()
    after("start")
    for cp in loads:
        cp.wait()

    def heads(d):
        at = me.yy(d)
        out = dot_nt(ga_s[at], wo_s[...]).astype(BF16)
        for half in (0, 1):
            place = pl.ds(pl.multiple_of((at + 4 * half) * rows, rows), rows)
            for head in (0, 1):
                gh_s[head, place] = out[half * rows:(half + 1) * rows, head * 128:head * 128 + 128]

    def turn(src, dst):
        for i in range(4):
            dst[:, i * step:(i + 1) * step] = src[pl.ds(i * step, step)].T

    turn(ho_s, ho_t)
    second = Scatter(me, part2, own2, ra2, rb2, f12, f22, r2_ss, r2_rs, rows)
    for d in second.order:
        second.ready(d)
    after("loads")
    gather.got(4)
    heads(0)
    after("heads0")
    gather.forward_one()
    after("fwd1")
    gather.near()
    after("near")
    second.stage_two()
    after("2two")
    second.stage_one()
    after("2one")
    gather.got(7)
    heads(-1)
    gather.got(8)
    heads(1)
    after("headsn")
    gather.far()
    after("far")
    gather.got(9)
    heads(2)
    after("heads2")

    def weight(dst, turned, y):
        wide = 512
        for j in range(y.shape[2] // wide):
            cols = slice(j * wide, (j + 1) * wide)
            acc = dot(turned[:, 0:step], y[0, :, cols])
            for i in range(1, 4):
                acc += dot(turned[:, i * step:(i + 1) * step], y[i, :, cols])
            dst[:, cols] = acc.astype(BF16)

    weight(dwo_s, ho_t, ga_s)
    after("dwo")
    gather.finish()
    load_one = pltpu.make_async_copy(g_one, ga_s, loc.at[11])
    load_one.start()
    scale = HEAD_DIM ** (-0.5)

    def attend(head, block):
        stop = (block + 1) * step
        mine = pl.ds(block * step, step)
        seen = pl.ds(0, stop)
        qb = q_s[head, mine]
        gb = gh_s[head, mine]
        s = dot_nt(qb, k_s[head, seen]) * scale
        places = block * step + lax.broadcasted_iota(jnp.int32, (step, stop), 0)
        s = jnp.where(lax.broadcasted_iota(jnp.int32, (step, stop), 1) <= places, s, -1e30)
        e = jnp.exp(s - jnp.max(s, -1, keepdims=True))
        p = e / jnp.sum(e, -1, keepdims=True)
        gp = dot_nt(gb, v_s[head, seen])
        ds = (p * (gp - jnp.sum(p * gp, -1, keepdims=True)) * scale).astype(BF16)
        gv = dot_tn(p.astype(BF16), gb)
        gk = dot_tn(ds, qb)
        gq = dot(ds, k_s[head, seen])
        gq = (gq * cosine[mine] - pltpu.roll(gq, 64, axis=1) * sine[mine]).astype(BF16)
        for half in (0, 1):
            g3_s[pl.ds(perm(2 * block + half) * rows, rows), pl.ds(head * 384, 128)] = gq[half * rows:(half + 1) * rows]
        if block:
            before = pl.ds(0, stop - step)
            dk_s[head, before] += gk[:stop - step]
            dv_s[head, before] += gv[:stop - step]
        dk_s[head, mine] = gk[stop - step:]
        dv_s[head, mine] = gv[stop - step:]

    def finish_head(head):
        for t in range(8):
            place = pl.ds(t * rows, rows)
            to = pl.ds(perm(t) * rows, rows)
            gk = dk_s[head, place]
            gk = gk * cosine[place] - pltpu.roll(gk, 64, axis=1) * sine[place]
            g3_s[to, pl.ds(head * 384 + 128, 128)] = gk.astype(BF16)
            g3_s[to, pl.ds(head * 384 + 256, 128)] = dv_s[head, place].astype(BF16)
        mine = pl.ds(head * 384, 384)
        for i in range(4):
            g3_t[mine, i * step:(i + 1) * step] = g3_s[pl.ds(i * step, step), mine].T
        weight(dw3_s.at[mine], g3_t.at[mine], ga_s)

    attend(0, 0)
    attend(0, 1)
    after("att0")
    attend(0, 2)
    second.stage_last()
    attend(0, 3)
    after("att1")
    load_one.wait()
    finish_head(0)
    after("dw3a")
    attend(1, 0)
    attend(1, 1)
    after("att2")
    attend(1, 2)
    attend(1, 3)
    after("att3")
    finish_head(1)
    after("dw3b")
    scatter = Scatter(me, part, own, ra, rb, f1, f2, rs_ss, rs_rs, rows)

    def back(d):
        at = me.yy(d)
        part[at] = dot_nt(g3_s[pl.ds(pl.multiple_of(at * step, step), step)], w3_s[...]).astype(BF16)
        scatter.ready(d)

    back(2)
    back(1)
    after("back3")
    scatter.stage_two()
    after("two")
    back(-1)
    back(0)
    after("back0")
    scatter.stage_one()
    after("one")
    scatter.stage_last()
    after("last")
    second.result()
    act_s[...] = (resid_s[...] + second.total(0, rows)).astype(BF16)
    moves = [remote(a, o, t_ss.at[i], t_rs.at[i], swap) for i, (a, o) in enumerate(((act_s, act_o), (gr_s, grad_o)))]
    store = [pltpu.make_async_copy(a, o, t_loc.at[i]) for i, (a, o) in enumerate(((act_s, act_o), (gr_s, grad_o)))]

    def home(i):
        @pl.when(stays)
        def _():
            store[i].start()

        @pl.when(jnp.logical_not(stays))
        def _():
            moves[i].start()

    home(0)
    after("act")
    scatter.result()
    gn = scatter.total(0, rows)
    unit, factor = normed(tok_s[...].astype(F32))
    gains = (jnp.sum(gn * unit, axis=0, keepdims=True), gain_two[...])
    for i in range(4):
        for j in range(2):
            for zi in range(2):
                lo = (zi * 4 + i) * 256
                gpart[i, 2 * j + zi:2 * j + zi + 1] = gains[j][:, lo:lo + 256]
    g = gn * g1[...]
    gr_s[...] = gr_s[...] + factor * (g - unit * jnp.mean(g * unit, axis=-1, keepdims=True))
    home(1)
    here = me.x * 4 + me.z
    gains_a, gains_b = [], []
    for d in range(4):
        for s in (0, 1):
            if d or s:
                to = {**me.at(dy=d), "core": lax.rem(c + s, 2)}
                i = len(gains_a)
                gains_a.append(remote(gpart.at[me.yy(d)], gy.at[me.y * 2 + c], g_ss.at[i], g_rs.at[i], to))
    for d in range(4):
        for s in range(4):
            if d or s:
                i = 7 + len(gains_b)
                gains_b.append(remote(gx.at[here], gx.at[here], g_ss.at[i], g_rs.at[i], me.at(dx=d, dz=s)))

    def gain_total(sends, ref):
        for cp in sends:
            cp.wait()
        total = ref[0]
        for i in range(1, ref.shape[0]):
            total = total + ref[i]
        return total

    gy[me.y * 2 + c] = gpart[me.y]
    for cp in gains_a:
        cp.start()
    after("res")
    gx[here] = gain_total(gains_a, gy)
    for cp in gains_b:
        cp.start()
    after("gtot")
    gains_o[...] = gain_total(gains_b, gx)
    after("gend")
    second.finish()
    scatter.finish()

    @pl.when(stays)
    def _():
        for cp in store:
            cp.wait()

    @pl.when(jnp.logical_not(stays))
    def _():
        for cp in moves:
            cp.wait()


def attention_back(args):
    dw_u, ga = args[2:4]
    ff = dw_u.shape[0]
    rows, width = ga.shape
    length = 8 * rows
    sds = jax.ShapeDtypeStruct
    outs = [
        sds((3, ff, width), BF16), sds((768, width), BF16), sds((256, width), BF16), sds((8, 256), F32),
        sds((rows, width), BF16), sds((rows, width), F32),
    ]
    total = 2 * ff + 1024
    sem = pltpu.SemaphoreType.DMA
    n = 1 + GATE_PARTS + UP_PARTS + 2 * THREE_PARTS
    many = sem((n, Head.SEMS + Tail.SEMS))
    half, eighth = width // 2, width // 8
    sums = [
        pltpu.VMEM((ff, eighth), BF16), pltpu.VMEM((ff, half), BF16), pltpu.VMEM((ff, eighth), BF16),
        *[pltpu.VMEM((total, half), BF16)] * 2, *[pltpu.VMEM((total, eighth), BF16)] * 4,
    ]
    part = pltpu.VMEM((4, 8, 256), F32)
    by_chip = (4, 2 * rows, width)
    head = (2, length, 128)
    scratch = [
        pltpu.VMEM(by_chip, BF16),
        *[pltpu.VMEM(head, BF16)] * 3, pltpu.VMEM((length, 256), BF16),
        pltpu.VMEM((width, 768), BF16), pltpu.VMEM((256, width), BF16),
        pltpu.VMEM(head, BF16), pltpu.VMEM(head, F32), pltpu.VMEM(head, F32),
        pltpu.VMEM((length, 768), BF16), pltpu.VMEM((256, length), BF16), pltpu.VMEM((768, length), BF16),
        pltpu.VMEM((256, width), BF16), pltpu.VMEM((768, width), BF16),
        pltpu.VMEM((rows, width), F32), pltpu.VMEM((rows, width), BF16), pltpu.VMEM((rows, width), F32),
        pltpu.VMEM((rows, width), BF16),
        *sums, part, pltpu.VMEM((8, 8, 256), F32), pltpu.VMEM((16, 8, 256), F32),
        *scatter_scratch(rows, width), *scatter_scratch(rows, width),
        dma(10), dma(10), dma(10), dma(10), dma(10), dma(10), dma(20), sem((DOWN_PARTS, Tail.SEMS)), sem((DOWN_PARTS, Tail.SEMS)), dma(DOWN_PARTS), many, many, dma(n), dma(n), dma(22), dma(22), dma(2), dma(2), dma(2),
    ]
    return pl.pallas_call(
        attention_back_kernel,
        name="attention_back",
        out_shape=outs,
        in_specs=[ANY] * 15 + [VM] * 4,
        out_specs=[ANY] * 3 + [VM] + [ANY] * 2,
        scratch_shapes=scratch,
        compiler_params=pltpu.CompilerParams(collective_id=2, has_side_effects=True, vmem_limit_bytes=62 * MIB),
    )(*args)


def widen_kernel(
    ff, three, out, act, grad, gains, d_o, g_o, u_o, q_o, k_o, v_o, o_o, act_o, grad_o, one_o, two_o,
    ff_s, three_s, out_s, wide_s, turned_s, last_s, act_s, grad_s, sem, done,
):
    rows = chunks_of(ff.shape[1], ff.shape[1] / 4)
    work = [(i, pl.ds(lo, n)) for i in range(3) for lo, n in rows]
    loads = [pltpu.make_async_copy(three, three_s, sem.at[0]), pltpu.make_async_copy(out, out_s, sem.at[1])]
    loads += [pltpu.make_async_copy(ff.at[i, at], ff_s.at[i, at], sem.at[2 + j]) for j, (i, at) in enumerate(work)]
    loads += [pltpu.make_async_copy(act, act_s, sem.at[14]), pltpu.make_async_copy(grad, grad_s, sem.at[15])]
    for cp in loads:
        cp.start()
    zl = lax.axis_index("zl")
    one_o[...] = jnp.where(zl == 0, gains[0:1], gains[1:2])
    two_o[...] = jnp.where(zl == 0, gains[2:3], gains[3:4])
    saves = []

    def save(src, dst):
        cp = pltpu.make_async_copy(src, dst, done.at[len(saves)])
        cp.start()
        saves.append(cp)

    loads[0].wait()
    for i, ref in enumerate((q_o, k_o, v_o)):
        for head in (0, 1):
            row = head * 384 + i * 128
            turned_s[i, :, head * 128:head * 128 + 128] = three_s[row:row + 128].astype(F32).T
        save(turned_s.at[i], ref)
    loads[1].wait()
    last_s[...] = out_s[...].astype(F32)
    save(last_s, o_o)
    for j, (i, at) in enumerate(work):
        loads[2 + j].wait()
        wide_s[i, at] = ff_s[i, at].astype(F32)
        save(wide_s.at[i, at], (d_o, g_o, u_o)[i].at[at])
    loads[-2].wait()
    save(act_s, act_o)
    loads[-1].wait()
    save(grad_s, grad_o)
    for cp in saves:
        cp.wait()


def widen(ff, three, out, act, grad, gains):
    _, n, width = ff.shape
    sds = jax.ShapeDtypeStruct
    return pl.pallas_call(
        widen_kernel,
        name="widen",
        out_shape=[sds((n, width), F32)] * 3 + [sds((width, 256), F32)] * 3 + [
            sds((256, width), F32), sds(act.shape, BF16), sds(grad.shape, F32), sds((1, 256), F32), sds((1, 256), F32)
        ],
        in_specs=[ANY] * 5 + [VM],
        out_specs=[ANY] * 9 + [VM] * 2,
        scratch_shapes=[
            pltpu.VMEM((3, n, width), BF16), pltpu.VMEM((768, width), BF16), pltpu.VMEM((256, width), BF16),
            pltpu.VMEM((3, n, width), F32), pltpu.VMEM((3, width, 256), F32), pltpu.VMEM((256, width), F32),
            pltpu.VMEM(act.shape, BF16), pltpu.VMEM(grad.shape, F32), dma(16), dma(18),
        ],
        compiler_params=pltpu.CompilerParams(vmem_limit_bytes=62 * MIB),
    )(ff, three, out, act, grad, gains)


def per_device(tokens, wq, wk, wv, wo, wg, wu, wd, attn_gain, mlp_gain, cotangent):
    tokens, cotangent = tokens[0], cotangent[0]
    length = 8 * tokens.shape[0]
    ff = wd.shape[0]
    cosine, sine = (jnp.asarray(t) for t in tables(length, HEAD_DIM))
    wg, wu = wg.T, wu.T
    g1, g2 = attn_gain[None], mlp_gain[None]
    (resid, tok, one, q, k, v, ho, w3, wo, gr, ga, gain_two, p2, z_part, t_part, dw_u) = layer(
        (tokens, cotangent, wq, wk, wv, wo, wg, wu, wd, g1, g2, cosine, sine)
    )
    dw_ff, dw3, dwo, gains, act, grad = attention_back(
        (z_part, t_part, dw_u, ga, p2, resid, tok, gr, one, q, k, v, ho, w3, wo, g1, cosine, sine, gain_two)
    )
    d_down, d_gate, d_up, d_query, d_key, d_value, d_out, act, grad, one, two = widen(dw_ff, dw3, dwo, act, grad, gains)
    return act[None], grad[None], d_query, d_key, d_value, d_out, d_gate.T, d_up.T, d_down, one[0], two[0]


def solution(mesh):
    split = Mesh(mesh.devices.reshape(4, 2, 2, 2, 4), ("x", "zh", "core", "zl", "y"))
    dp, tensor = ("x", "zh", "core"), ("zl", "y")
    cols, rows, seqs = P(None, tensor), P(tensor, None), P(dp, tensor, None)
    return jax.shard_map(
        per_device,
        mesh=split,
        in_specs=(seqs, cols, cols, cols, rows, cols, cols, rows, P(), P(), seqs),
        out_specs=(seqs, seqs, cols, cols, cols, rows, cols, cols, rows, P(tensor), P(tensor)),
        check_vma=False,
    )
```

```python
import functools

import jax
import jax.numpy as jnp
import numpy as np
from jax import lax
from jax.experimental import pallas as pl
from jax.experimental.pallas import tpu as pltpu
from jax.sharding import Mesh, PartitionSpec as P

HEAD_DIM = 128
NORM_EPS = 1e-05
ROPE_BASE = 10000.0
F32, BF16 = jnp.float32, jnp.bfloat16
MESH = pl.DeviceIdType.MESH
ANY = pl.BlockSpec(memory_space=pl.ANY)
VM = pl.BlockSpec(memory_space=pltpu.VMEM)
MIB = 2**20


def tables(length, head_dim):
    half = head_dim // 2
    freqs = np.float32(ROPE_BASE) ** (-(np.float32(2.0) * np.arange(half, dtype=np.float32)) / np.float32(head_dim))
    angles = np.arange(length, dtype=np.float32)[:, None] * freqs[None, :]
    cosine, sine = np.cos(angles), np.sin(angles)
    return np.concatenate([cosine, cosine], 1), np.concatenate([-sine, sine], 1)


class Place:
    def __init__(self):
        self.x = lax.axis_index("x")
        self.zh = lax.axis_index("zh")
        self.zl = lax.axis_index("zl")
        self.c = lax.axis_index("core")
        self.y = lax.axis_index("y")
        self.z = self.zh * 2 + self.zl

    def at(self, dx=0, dy=0, dz=0, core=None):
        out = {}
        if dx:
            out["x"] = lax.rem(self.x + dx + 4, 4)
        if dy:
            out["y"] = lax.rem(self.y + dy + 4, 4)
        if dz:
            z = lax.rem(self.z + dz + 4, 4)
            out["zh"], out["zl"] = z // 2, lax.rem(z, 2)
        if core is not None:
            out["core"] = core
        return out

    def sibling(self):
        return {"core": 1 - self.c}

    def yy(self, d):
        return lax.rem(self.y + d + 4, 4)


def meet(devices):
    barrier = pltpu.get_barrier_semaphore()
    for d in devices:
        pl.semaphore_signal(barrier, inc=1, device_id=d, device_id_type=MESH)
    pl.semaphore_wait(barrier, len(devices))


def remote(src, dst, ss, rs, device):
    return pltpu.make_async_remote_copy(
        src_ref=src, dst_ref=dst, send_sem=ss, recv_sem=rs, device_id=device, device_id_type=MESH
    )


def dot(a, b):
    return jnp.dot(a, b, preferred_element_type=F32)


def dot_nt(a, b):
    return lax.dot_general(a, b, (((1,), (1,)), ((), ())), preferred_element_type=F32)


def dot_tn(a, b):
    return lax.dot_general(a, b, (((0,), (0,)), ((), ())), preferred_element_type=F32)


def normed(values):
    factor = lax.rsqrt(jnp.mean(values * values, axis=-1, keepdims=True) + NORM_EPS)
    return values * factor, factor


class Gather:
    N = 10

    def __init__(self, me, buf, ss, rs, rows):
        h = rows // 2
        c, y = me.c, me.y

        def part(d, lo, n):
            return buf.at[me.yy(d), pl.ds(c * rows + lo, n)]

        up, down, sib = me.at(dy=1), me.at(dy=-1), me.sibling()
        spec = [
            (0, 0, h, up), (0, h, h, up), (0, h, h, down), (0, 0, h, down), (0, 0, rows, sib),
            (-1, 0, h, up), (1, h, h, down), (-1, 0, rows, sib), (1, 0, rows, sib), (2, 0, rows, sib),
        ]
        self.copies = [remote(part(d, lo, n), part(d, lo, n), ss.at[i], rs.at[i], to) for i, (d, lo, n, to) in enumerate(spec)]

    def start(self):
        for i in (0, 2, 1, 3, 4):
            self.copies[i].start()

    def start_first(self):
        self.copies[0].start()
        self.copies[3].start()

    def start_second(self):
        for i in (2, 1, 4):
            self.copies[i].start()

    def got(self, i):
        self.copies[i].wait_recv()

    def forward_one(self):
        self.got(0)
        self.copies[5].start()
        self.got(2)
        self.copies[6].start()

    def near(self):
        self.got(1)
        self.copies[7].start()
        self.got(3)
        self.copies[8].start()

    def far(self):
        self.got(5)
        self.got(6)
        self.copies[9].start()

    def finish(self):
        for cp in self.copies:
            cp.wait_send()


class Scatter:
    N = 10

    def __init__(self, me, part, own, ra, rb, f1, f2, ss, rs, rows):
        self.me, self.part, self.own, self.rows = me, part, own, rows
        self.ra, self.rb, self.f1, self.f2 = ra, rb, f1, f2
        self.h = rows // 2
        c = me.c
        up, down, sib = me.at(dy=1), me.at(dy=-1), me.sibling()
        h = self.h
        self.order = (2, 1, -1, 0)
        self.sib = {}
        for i, d in enumerate(self.order):
            self.sib[d] = remote(
                part.at[me.yy(d), pl.ds((1 - c) * rows, rows)], own.at[me.yy(d)], ss.at[i], rs.at[i], sib
            )

        def mine(d, lo):
            return part.at[me.yy(d), pl.ds(c * rows + lo, h)]

        self.a2 = remote(mine(2, 0), ra, ss.at[4], rs.at[4], up)
        self.b2 = remote(mine(2, h), rb, ss.at[5], rs.at[5], down)
        self.b1 = remote(mine(1, h), f1.at[pl.ds(h, h)], ss.at[6], rs.at[6], up)
        self.a1 = remote(mine(1, 0), f1.at[pl.ds(0, h)], ss.at[7], rs.at[7], up)
        self.am = remote(mine(-1, 0), f2.at[pl.ds(0, h)], ss.at[8], rs.at[8], down)
        self.bm = remote(mine(-1, h), f2.at[pl.ds(h, h)], ss.at[9], rs.at[9], down)

    def add(self, d, lo, n, other):
        rows = pl.ds(self.me.c * self.rows + lo, n)
        at = self.me.yy(d)
        self.part[at, rows] = (self.part[at, rows].astype(F32) + other.astype(F32)).astype(BF16)

    def ready(self, d):
        self.sib[d].start()

    def stage_two(self):
        h, at = self.h, self.me.yy(2)
        self.sib[2].wait_recv()
        self.add(2, 0, h, self.own[at, pl.ds(0, h)])
        self.a2.start()
        self.add(2, h, h, self.own[at, pl.ds(h, h)])
        self.b2.start()

    def stage_one(self):
        h, above, below = self.h, self.me.yy(1), self.me.yy(-1)
        self.sib[1].wait_recv()
        self.add(1, h, h, self.own[above, pl.ds(h, h)])
        self.b1.start()
        self.sib[-1].wait_recv()
        self.add(-1, 0, h, self.own[below, pl.ds(0, h)])
        self.am.start()
        self.add(1, 0, h, self.own[above, pl.ds(0, h)])
        self.add(-1, h, h, self.own[below, pl.ds(h, h)])

    def stage_last(self):
        self.a2.wait_recv()
        self.add(1, 0, self.h, self.ra[...])
        self.a1.start()
        self.b2.wait_recv()
        self.add(-1, self.h, self.h, self.rb[...])
        self.bm.start()

    def result(self):
        self.sib[0].wait_recv()
        for cp in (self.b1, self.am, self.a1, self.bm):
            cp.wait_recv()

    def total(self, lo, n):
        me = self.me
        mine = self.part[me.y, pl.ds(me.c * self.rows + lo, n)].astype(F32)
        near = self.f1[pl.ds(lo, n)].astype(F32) + self.f2[pl.ds(lo, n)].astype(F32)
        return mine + self.own[me.y, pl.ds(lo, n)].astype(F32) + near

    def finish(self):
        for cp in (*self.sib.values(), self.a2, self.b2, self.b1, self.a1, self.am, self.bm):
            cp.wait_send()


def scatter_scratch(rows, width):
    return [
        pltpu.VMEM((4, 2 * rows, width), BF16),
        pltpu.VMEM((4, rows, width), BF16),
        pltpu.VMEM((rows // 2, width), BF16),
        pltpu.VMEM((rows // 2, width), BF16),
        pltpu.VMEM((rows, width), BF16),
        pltpu.VMEM((rows, width), BF16),
    ]


def dma(n):
    return pltpu.SemaphoreType.DMA((n,))


class Head:
    SEMS = 9

    def __init__(self, me, src, bufs, row, n, ss, rs, loc):
        b, fold, xab, f1, f2 = bufs
        self.b, self.fold, self.xab, self.f1, self.f2 = bufs
        self.at = at = pl.ds(row, n)
        ha = n // 32 * 16
        c, zl = me.c, me.zl
        self.keep = c == zl
        wide = src.shape[1] // 2
        q = wide // 4
        z_other = lax.rem(me.z + jnp.where(zl == 0, 3, 1), 4)
        near_z = {"zl": 1 - zl, "core": 0 * c}
        far_z = {"zh": z_other // 2, "zl": lax.rem(z_other, 2), "core": 0 * c + 1}
        sib, up, down = me.sibling(), me.at(dx=1), me.at(dx=-1)

        def col(k):
            return pl.ds(pl.multiple_of(k * wide, wide), wide)

        def blk(d):
            return pl.ds(pl.multiple_of(lax.rem(me.x + d + 4, 4) * q, q), q)

        self.blk = blk
        self.rows_a, self.rows_b = ra, rb = pl.ds(row, ha), pl.ds(row + ha, n - ha)
        self.local = pltpu.make_async_copy(src.at[:, col(c)], b.at[at], loc)
        self.to_sib = remote(src.at[:, col(1 - c)], b.at[at], ss.at[0], rs.at[0], sib)
        self.give0 = remote(src.at[:, pl.ds(0, wide)], fold.at[at], ss.at[1], rs.at[1], near_z)
        self.give1 = remote(src.at[:, pl.ds(wide, wide)], fold.at[at], ss.at[2], rs.at[1], far_z)
        self.a2 = remote(b.at[ra, blk(2)], xab.at[ra], ss.at[3], rs.at[3], up)
        self.b2 = remote(b.at[rb, blk(2)], xab.at[rb], ss.at[4], rs.at[4], down)
        self.b1 = remote(b.at[rb, blk(1)], f1.at[rb], ss.at[5], rs.at[5], up)
        self.am = remote(b.at[ra, blk(-1)], f2.at[ra], ss.at[6], rs.at[6], down)
        self.a1 = remote(b.at[ra, blk(1)], f1.at[ra], ss.at[7], rs.at[7], up)
        self.bm = remote(b.at[rb, blk(-1)], f2.at[rb], ss.at[8], rs.at[8], down)

    def s0(self):
        @pl.when(self.keep)
        def _():
            self.local.start()
            self.to_sib.start()

        @pl.when(jnp.logical_not(self.keep))
        def _():
            self.give0.start()
            self.give1.start()

    def folded(self):
        @pl.when(self.keep)
        def _():
            self.local.wait()
            self.to_sib.wait_send()

        @pl.when(jnp.logical_not(self.keep))
        def _():
            self.to_sib.wait_recv()
            self.give0.wait_send()
            self.give1.wait_send()

        self.give0.wait_recv()
        at = self.at
        self.b[at] = (self.b[at].astype(F32) + self.fold[at].astype(F32)).astype(BF16)

    def s1(self):
        self.folded()
        self.send()

    def send(self):
        for cp in (self.a2, self.b2, self.b1, self.am):
            cp.start()

    def plus(self, rows, d):
        cols = self.blk(d)
        self.b[rows, cols] = (self.b[rows, cols].astype(F32) + self.xab[rows].astype(F32)).astype(BF16)

    def s2(self):
        self.a2.wait_recv()
        self.plus(self.rows_a, 1)
        self.a1.start()
        self.b2.wait_recv()
        self.plus(self.rows_b, -1)
        self.bm.start()

    def s3(self):
        for cp in (self.b1, self.am, self.a1, self.bm):
            cp.wait_recv()
        at, own = self.at, self.blk(0)
        self.b[at, own] = (self.b[at, own].astype(F32) + self.f1[at].astype(F32) + self.f2[at].astype(F32)).astype(BF16)

    def done(self):
        for cp in (self.a2, self.b2, self.b1, self.am, self.a1, self.bm):
            cp.wait_send()


class Tail:
    SEMS = 11

    def __init__(self, me, own, dst, ag, zr, row, n, ss, rs, done):
        self.own, self.ag, self.zr = own, ag, zr
        self.at = at = pl.ds(row, n)
        ha = n // 32 * 16
        c = me.c
        wide = dst.shape[1] // 2
        q = wide // 4
        sib, up, down = me.sibling(), me.at(dx=1), me.at(dx=-1)

        def place(d):
            return lax.rem(me.x + d + 4, 4) * q

        def blk(d):
            return pl.ds(pl.multiple_of(place(d), q), q)

        def out(d):
            return pl.ds(pl.multiple_of(c * wide + place(d), q), q)

        self.blk = blk
        ra, rb = pl.ds(row, ha), pl.ds(row + ha, n - ha)
        self.zx = remote(own, zr.at[at], ss.at[0], rs.at[0], {"zh": 1 - me.zh})
        self.g = [
            remote(ag.at[r, blk(d)], ag.at[r, blk(d)], ss.at[1 + i], rs.at[1 + i], to)
            for i, (r, d, to) in enumerate(
                ((ra, 0, up), (rb, 0, down), (rb, 0, up), (ra, 0, down), (ra, -1, up), (rb, 1, down))
            )
        ]
        self.share = [
            remote(ag.at[at, blk(d)], dst.at[:, out(d)], ss.at[7 + i], rs.at[7 + i], sib) for i, d in enumerate((0, -1, 1, 2))
        ]
        self.save = pltpu.make_async_copy(ag.at[at], dst.at[:, pl.ds(pl.multiple_of(c * wide, wide), wide)], done)

    def t0(self):
        self.zx.start()

    def t1(self):
        self.zx.wait_recv()
        at = self.at
        self.ag[at, self.blk(0)] = (self.own[...].astype(F32) + self.zr[at].astype(F32)).astype(BF16)
        for cp in self.g[:4]:
            cp.start()
        self.share[0].start()

    def t2(self):
        self.g[0].wait_recv()
        self.g[4].start()
        self.g[1].wait_recv()
        self.g[5].start()
        self.g[2].wait_recv()
        self.share[1].start()
        self.g[3].wait_recv()
        self.share[2].start()

    def t3(self):
        self.g[4].wait_recv()
        self.g[5].wait_recv()
        self.share[3].start()
        self.save.start()

    def t4(self):
        for cp in self.share:
            cp.wait()
        self.save.wait()
        self.zx.wait_send()
        for cp in self.g:
            cp.wait_send()


def chunks_of(rows, size):
    count = max(1, round(rows / size))
    ends = [rows * i // count // 16 * 16 for i in range(count)] + [rows]
    return [(a, b - a) for a, b in zip(ends, ends[1:])]


class Sum:
    def __init__(self, head, tail):
        self.head, self.tail = head, tail
        self.s0, self.s1, self.s2 = head.s0, head.s1, head.s2
        self.send = head.send
        self.t1, self.t2, self.t3 = tail.t1, tail.t2, tail.t3

    def s3(self):
        self.head.s3()
        self.tail.t0()

    def t4(self):
        self.head.done()
        self.tail.t4()


def each(pieces, *stages):
    for stage in stages:
        for piece in pieces:
            getattr(piece, stage)()


def perm(block):
    return (block % 4) * 2 + block // 4


def layer_kernel(
    tok, cot, wq, wk, wv, wo, wg, wu, wd, g1, g2, cosine, sine,
    resid_o, tok_o, g_o, q_o, k_o, v_o, ho_o, w3_o, wo_o, gr_o, ga_o, gain_o, p2_o, z_o, t_o, dw_o,
    tok_s, g_s, gm_s, pool, q_s, k_s, v_s, ho_s, resid_s, wg_s, wu_s, wd_s,
    a_s, b_s, hid_s, dg_s, du_s, turned, dw_s, cot_s, gr_s, ga_s, gain_s,
    red_f, red_x, red_f1, red_f2, part, own, ra, rb, f1, f2,
    ag_ss, ag_rs, ag3_ss, ag3_rs, rs_ss, rs_rs, ag2_ss, ag2_rs, rs3_ss, rs3_rs,
    w_ss, w_rs, loc, out_sem, red_ss, red_rs, red_loc,
):
    me = Place()
    c, zl = me.c, me.zl
    rows = tok.shape[0]
    stays = c == zl
    swap = {"zl": 1 - zl, "core": 1 - c}
    others = [me.at(dy=1), me.at(dy=-1), me.at(dx=1), me.at(dx=-1), me.at(dx=2), me.sibling()]
    others += [me.at(dz=s, core=k) for s in (1, -1) for k in (0, 1)]
    width = tok.shape[1]
    ff = wd.shape[0]
    step = 2 * rows
    w3_s = pool.at[:, pl.ds(0, 768)]
    wo_s = dw_s.at[2, pl.ds(0, 256)]
    red_b = pool.at[pl.ds(0, 2 * ff)]
    meet(others)

    z_other = lax.rem(me.z + jnp.where(zl == 0, 3, 1), 4)
    far_z = {"zh": z_other // 2, "zl": lax.rem(z_other, 2), "core": c}

    heads = (wq, wk, wv)

    def halves(i, src, dst_all, axis_rows, near=0.5):
        h = int(axis_rows * near) // 16 * 16
        r = axis_rows - h
        a = remote(src.at[pl.ds(0, h)], dst_all.at[pl.ds(0, h)], w_ss.at[i], w_rs.at[2 * i], swap)
        b = remote(src.at[pl.ds(h, r)], dst_all.at[pl.ds(h, r)], w_ss.at[i], w_rs.at[2 * i + 1], far_z)
        return a, b

    def w3_part(i):
        return pool.at[:, pl.ds(256 * i, 256)]

    band = pl.ds(pl.multiple_of(me.x * (width // 4), width // 4), width // 4)
    moved = [halves(i, w, w3_part(i), w.shape[0], 0.32) for i, w in enumerate(heads[:2])]
    moved.append(halves(2, wv.at[band], w3_part(2).at[band], width // 4))
    value_spread = [
        remote(w3_part(2).at[band], w3_part(2).at[band], w_ss.at[12 + d], w_rs.at[19 + d], me.at(dx=d)) for d in (1, 2, 3)
    ]
    later = [halves(3, wo, wo_s, wo.shape[0]), halves(4, wg, wg_s, ff), halves(5, wu, wu_s, ff)]
    later.append(halves(6, wd.at[:, band], wd_s.at[:, band], ff))
    spread = [
        remote(wd_s.at[:, band], wd_s.at[:, band], w_ss.at[8 + d], w_rs.at[15 + d], me.at(dx=d)) for d in (1, 2, 3)
    ]
    h = rows // 2
    first, second = pl.ds(0, h), pl.ds(h, h)
    tok_move = [
        remote(tok.at[first], tok_s.at[first], w_ss.at[7], w_rs.at[14], swap),
        remote(tok.at[second], tok_s.at[second], w_ss.at[12], w_rs.at[19], swap),
    ]
    mine = gm_s.at[me.y, pl.ds(c * rows, rows)]
    cot_move = remote(cot, gm_s.at[me.y, pl.ds((1 - c) * rows, rows)], w_ss.at[8], w_rs.at[15], swap)
    local = [pltpu.make_async_copy(w, w3_part(i), loc.at[i]) for i, w in enumerate(heads)]
    local.append(pltpu.make_async_copy(wo, wo_s, loc.at[3]))
    cot_local = pltpu.make_async_copy(cot, mine, loc.at[4])
    kept = [pltpu.make_async_copy(a, b, loc.at[5 + i]) for i, (a, b) in enumerate(((wg, wg_s), (wu, wu_s), (wd, wd_s)))]
    tok_local = pltpu.make_async_copy(tok, tok_s, loc.at[8])

    @pl.when(stays)
    def _():
        tok_local.start()
        for cp in local:
            cp.start()
        cot_local.start()
        for cp in kept:
            cp.start()
        for i in (2, 0, 1):
            moved[i][1].start()
        tok_local.wait()

    @pl.when(jnp.logical_not(stays))
    def _():
        tok_move[0].start()
        tok_move[0].wait_send()
        tok_move[1].start()
        tok_move[0].wait_recv()

    gather = Gather(me, g_s, ag_ss, ag_rs, rows)

    def norm_one(lo):
        unit, _ = normed(tok_s[pl.ds(lo, h)].astype(F32))
        g_s[me.y, pl.ds(c * rows + lo, h)] = (unit * g1[...]).astype(BF16)

    norm_one(0)
    gather.start_first()

    @pl.when(jnp.logical_not(stays))
    def _():
        tok_move[1].wait_send()
        for i in (2, 0, 1):
            moved[i][0].start()
        tok_move[1].wait_recv()

    norm_one(h)
    gather.start_second()
    out_tok = pltpu.make_async_copy(tok_s, tok_o, out_sem.at[0])
    out_tok.start()

    @pl.when(jnp.logical_not(stays))
    def _():
        for cp in moved[2]:
            cp.wait_recv()
        for cp in value_spread:
            cp.start()

    def have(i):
        @pl.when(stays)
        def _():
            local[i].wait()

        @pl.when(jnp.logical_not(stays))
        def _():
            for cp in (moved[0], moved[1], value_spread, later[0])[i]:
                cp.wait_recv()

    def project(d, lo, hi):
        at = me.yy(d)
        out = dot(g_s[at], pool[:, lo * 256:hi * 256])
        for half in (0, 1):
            place = pl.ds(pl.multiple_of((at + 4 * half) * rows, rows), rows)
            for i in range(lo, hi):
                ref = (q_s, k_s, v_s)[i]
                for head in (0, 1):
                    col = (i - lo) * 256 + head * 128
                    v = out[half * rows:(half + 1) * rows, col:col + 128]
                    if i < 2:
                        v = v * cosine[place] + pltpu.roll(v, 64, axis=1) * sine[place]
                    ref[head, place] = v.astype(BF16)

    gather.got(4)
    gather.forward_one()
    have(0)
    have(1)
    project(0, 0, 2)
    gather.near()

    @pl.when(stays)
    def _():
        later[0][1].start()
        later[3][1].start()
        cot_local.wait()

    @pl.when(jnp.logical_not(stays))
    def _():
        later[0][0].start()
        later[3][0].start()

    gather.got(7)
    project(-1, 0, 2)
    gather.got(8)
    project(1, 0, 2)
    have(2)
    for d in (0, -1, 1):
        project(d, 2, 3)
    gather.far()
    gather.got(9)
    project(2, 0, 3)

    third = Gather(me, gm_s, ag3_ss, ag3_rs, rows)

    @pl.when(stays)
    def _():
        third.start()

    @pl.when(jnp.logical_not(stays))
    def _():
        cot_move.start()


    def out(src, dst):
        cp = pltpu.make_async_copy(src, dst, out_sem.at[len(outs) + 1])
        cp.start()
        outs.append(cp)

    out_g = pltpu.make_async_copy(g_s, g_o, out_sem.at[17])
    out_g.start()
    outs = [out_tok]
    for a, b in ((q_s, q_o), (k_s, k_o), (v_s, v_o), (w3_s, w3_o)):
        out(a, b)

    scale = HEAD_DIM ** (-0.5)
    for block in range(4):
        stop = (block + 1) * step
        for head in (0, 1):
            s = dot_nt(q_s[head, pl.ds(block * step, step)], k_s[head, pl.ds(0, stop)]) * scale
            places = block * step + lax.broadcasted_iota(jnp.int32, (step, stop), 0)
            s = jnp.where(lax.broadcasted_iota(jnp.int32, (step, stop), 1) <= places, s, -1e30)
            e = jnp.exp(s - jnp.max(s, -1, keepdims=True))
            p = (e / jnp.sum(e, -1, keepdims=True)).astype(BF16)
            o = dot(p, v_s[head, pl.ds(0, stop)]).astype(BF16)
            for half in (0, 1):
                ho_s[pl.ds(perm(2 * block + half) * rows, rows), pl.ds(head * 128, 128)] = o[half * rows:(half + 1) * rows]
        if block == 0:
            @pl.when(stays)
            def _():
                for _, b in later[1:3]:
                    b.start()

            @pl.when(jnp.logical_not(stays))
            def _():
                for a, _ in later[1:3]:
                    a.start()

        if block == 2:
            pl.when(stays)(third.forward_one)
    have(3)

    @pl.when(jnp.logical_not(stays))
    def _():
        for cp in later[3]:
            cp.wait_recv()
        for cp in spread:
            cp.start()

    out(ho_s, ho_o)
    out(wo_s, wo_o)
    keep_w3, keep_wo = outs[4], outs[6]

    scatter = Scatter(me, part, own, ra, rb, f1, f2, rs_ss, rs_rs, rows)
    gather.finish()
    out_g.wait()

    def out_project(d):
        at = me.yy(d)
        part[at] = dot(ho_s[pl.ds(pl.multiple_of(at * 2 * rows, 2 * rows), 2 * rows)], dw_s[2, 0:256]).astype(BF16)
        scatter.ready(d)

    out_project(2)
    out_project(1)
    out_project(-1)
    scatter.stage_two()
    out_project(0)
    scatter.stage_one()
    pl.when(stays)(third.near)

    scatter.stage_last()

    @pl.when(jnp.logical_not(stays))
    def _():
        cot_move.wait_recv()
        third.start()

    scatter.result()
    resid = tok_s[...].astype(F32) + scatter.total(0, rows)
    resid_s[...] = resid
    unit, _ = normed(resid)
    g_s[me.y, pl.ds(c * rows, rows)] = (unit * g2[...]).astype(BF16)
    keep_w3.wait()
    keep_wo.wait()

    @pl.when(jnp.logical_not(stays))
    def _():
        for cp in value_spread:
            cp.wait_send()

    gather = Gather(me, g_s, ag2_ss, ag2_rs, rows)
    gather.start()
    out(resid_s, resid_o)
    scatter.finish()

    def block(d):
        return me.yy(d)

    def forward(d):
        at = block(d)
        x = g_s[at]
        gate = dot_nt(x, wg_s[...])
        up = dot_nt(x, wu_s[...])
        sigma = jax.nn.sigmoid(gate)
        swish = gate * sigma
        b_s[at] = swish.astype(BF16)
        a_s[at] = (up * sigma * (1.0 + gate * (1.0 - sigma))).astype(BF16)
        hid_s[at] = (swish * up).astype(BF16)

    def weight_here(i):
        @pl.when(stays)
        def _():
            kept[i].wait()

        @pl.when(jnp.logical_not(stays))
        def _():
            for cp in (later[1], later[2], spread)[i]:
                cp.wait_recv()

    def slot(j, d):
        turned[:, j * step:(j + 1) * step] = hid_s[block(d)].T

    def hidden_back(d):
        at = block(d)
        gh = dot_nt(gm_s[at], wd_s[...])
        dg_s[at] = (gh * a_s[at].astype(F32)).astype(BF16)
        du_s[at] = (gh * b_s[at].astype(F32)).astype(BF16)

    wide = 512
    near = (0, -1, 1)
    gather.got(4)
    weight_here(0)
    weight_here(1)
    forward(0)
    gather.forward_one()
    weight_here(2)
    slot(0, 0)
    third.got(4)
    hidden_back(0)
    @pl.when(jnp.logical_not(stays))
    def _():
        third.forward_one()
        third.near()

    gather.near()
    gather.got(7)
    forward(-1)
    slot(1, -1)
    gather.got(8)
    forward(1)
    slot(2, 1)
    gather.far()
    third.got(7)
    third.got(8)
    third.far()
    hidden_back(-1)
    hidden_back(1)
    for j in range(gm_s.shape[2] // wide):
        cols = slice(j * wide, (j + 1) * wide)
        acc = dot(turned[:, 0:step], gm_s[block(0), :, cols])
        for i in (1, 2):
            acc += dot(turned[:, i * step:(i + 1) * step], gm_s[block(near[i]), :, cols])
        dw_s[0, :, cols] = acc.astype(BF16)
    cot_s[...] = gm_s[me.y, pl.ds(c * rows, rows)]

    def turn(src):
        for i in range(4):
            turned[:, i * step:(i + 1) * step] = src[i].T

    def weight(k, src, y):
        turn(src)
        for j in range(y.shape[2] // wide):
            cols = slice(j * wide, (j + 1) * wide)
            acc = dot(turned[:, 0:step], y[0, :, cols])
            for i in range(1, 4):
                acc += dot(turned[:, i * step:(i + 1) * step], y[i, :, cols])
            dw_s[k, :, cols] = acc.astype(BF16)

    def pieces(k, parts):
        heads = []
        for start, n in parts:
            s = 2 * k + len(heads)
            heads.append(Head(
                me, dw_s.at[k].at[pl.ds(start, n)], (pool, red_f, red_x, red_f1, red_f2), k * ff + start, n,
                red_ss.at[s], red_rs.at[s], red_loc.at[s],
            ))
        return heads

    cuts = chunks_of(ff, ff / 2)
    (down0, down1), gate = pieces(0, cuts), pieces(1, cuts)
    scatter = Scatter(me, part, own, ra, rb, f1, f2, rs3_ss, rs3_rs, rows)

    def back(d):
        at = block(d)
        part[at] = (dot(dg_s[at], wg_s[...]) + dot(du_s[at], wu_s[...])).astype(BF16)
        scatter.ready(d)

    gather.got(9)
    forward(2)
    slot(3, 2)
    third.got(9)
    for j in range(gm_s.shape[2] // wide):
        cols = slice(j * wide, (j + 1) * wide)
        last = dot(turned[:, 3 * step:4 * step], gm_s[block(2), :, cols])
        dw_s[0, :, cols] = (dw_s[0, :, cols].astype(F32) + last).astype(BF16)
    down0.s0()
    hidden_back(2)
    back(2)
    back(1)
    down1.s0()
    scatter.stage_two()
    back(-1)
    back(0)
    scatter.stage_one()
    down0.s1()
    weight(1, dg_s, g_s)
    each(gate, "s0")
    scatter.stage_last()
    down1.s1()
    weight(2, du_s, g_s)
    down0.s2()
    out(dw_s.at[2], dw_o)
    third.finish()
    for i in range(4):
        gm_s[i] = dot(hid_s[i], wd_s[...]).astype(BF16)
    out(gm_s, p2_o)
    down1.s2()
    down0.s3()
    scatter.result()
    gn = scatter.total(0, rows)
    unit, factor = normed(resid_s[...])
    gain_s[...] = jnp.sum(gn * unit, axis=0, keepdims=True)
    g = gn * g2[...]
    gr = cot_s[...].astype(F32) + factor * (g - unit * jnp.mean(g * unit, axis=-1, keepdims=True))
    gr_s[...] = gr
    ga_s[...] = gr.astype(BF16)
    out(gr_s, gr_o)
    out(ga_s, ga_o)
    out(gain_s, gain_o)
    down1.s3()
    out(pool.at[pl.ds(0, ff), down0.blk(0)], z_o)
    each(gate, "folded")
    out(pool.at[pl.ds(ff, ff)], t_o)
    down0.done()
    down1.done()
    gather.finish()
    scatter.finish()
    for cp in outs:
        if cp is not keep_w3 and cp is not keep_wo:
            cp.wait()

    @pl.when(stays)
    def _():
        for _, b in moved + later:
            b.wait_send()

    @pl.when(jnp.logical_not(stays))
    def _():
        cot_move.wait_send()
        for a, _ in moved + later:
            a.wait_send()
        for cp in spread:
            cp.wait_send()


def layer(args):
    tok, cot, wq, wk, wv, wo, wg, wu, wd, g1, g2, cosine, sine = args
    rows, width = tok.shape
    ff = wd.shape[0]
    length = 8 * rows
    by_chip, hidden, head = (4, 2 * rows, width), (4, 2 * rows, ff), (2, length, 128)
    sds = jax.ShapeDtypeStruct
    outs = [
        sds((rows, width), F32), sds((rows, width), BF16), sds(by_chip, BF16),
        *[sds(head, BF16)] * 3, sds((length, 256), BF16), sds((width, 768), BF16), sds((256, width), BF16),
        sds((rows, width), F32), sds((rows, width), BF16), sds((1, width), F32),
        sds(by_chip, BF16), sds((ff, width // 8), BF16), sds((ff, width // 2), BF16), sds((ff, width), BF16),
    ]
    sem = pltpu.SemaphoreType.DMA
    scratch = [
        pltpu.VMEM((rows, width), BF16), pltpu.VMEM(by_chip, BF16), pltpu.VMEM(by_chip, BF16),
        pltpu.VMEM((width, width // 2), BF16), *[pltpu.VMEM(head, BF16)] * 3, pltpu.VMEM((length, 256), BF16),
        pltpu.VMEM((rows, width), F32), *[pltpu.VMEM((ff, width), BF16)] * 3,
        pltpu.VMEM(hidden, BF16), pltpu.VMEM(hidden, BF16),
        *[pltpu.VMEM(hidden, BF16)] * 3, pltpu.VMEM((ff, length), BF16),
        pltpu.VMEM((3, ff, width), BF16), pltpu.VMEM((rows, width), BF16),
        pltpu.VMEM((rows, width), F32), pltpu.VMEM((rows, width), BF16), pltpu.VMEM((1, width), F32),
        pltpu.VMEM((2 * ff, width // 2), BF16), *[pltpu.VMEM((2 * ff, width // 8), BF16)] * 3,
        *scatter_scratch(rows, width),
        *[dma(10)] * 10, dma(16), dma(23), dma(9), dma(18), sem((4, Head.SEMS)), sem((4, Head.SEMS)), dma(4),
    ]
    return pl.pallas_call(
        layer_kernel,
        name="layer",
        out_shape=outs,
        in_specs=[ANY] * 9 + [VM] * 4,
        out_specs=[ANY] * len(outs),
        scratch_shapes=scratch,
        compiler_params=pltpu.CompilerParams(collective_id=0, has_side_effects=True, vmem_limit_bytes=63 * MIB),
    )(*args)


DOWN_PARTS, GATE_PARTS, UP_PARTS, THREE_PARTS = 1, 2, 2, 2
ORDER = {
    "start": (
        ("up0", "s0"), ("up1", "s0"),
    ),
    "loads": (
        ("gate0", "send"), ("gate1", "send"),
    ),
    "fwd1": (
        ("down0", "t0"), ("up0", "s1"),
    ),
    "2one": (
        ("gate0", "s2"), ("gate1", "s2"),
    ),
    "far": (
        ("up0", "s2"), ("up1", "s1"),
    ),
    "heads2": (
        ("down0", "t1"), ("gate0", "s3"), ("gate1", "s3"),
    ),
    "dwo": (
        ("dwo0", "s0"),
    ),
    "att0": (
        ("up1", "s2"),
    ),
    "att1": (
        ("gate0", "t1"),
    ),
    "dw3a": (
        ("threea0", "s0"), ("threea1", "s0"), ("gate1", "t1"),
    ),
    "att3": (
        ("dwo0", "s1"),
    ),
    "dw3b": (
        ("threeb0", "s0"), ("threeb1", "s0"), ("threea0", "s1"),
    ),
    "back3": (
        ("down0", "t2"), ("threea1", "s1"), ("up0", "s3"), ("up1", "s3"), ("threea0", "s2"),
    ),
    "back0": (
        ("threeb0", "s1"), ("dwo0", "s2"), ("threeb1", "s1"), ("threea1", "s2"),
    ),
    "one": (
        ("threeb0", "s2"), ("up0", "t1"),
    ),
    "act": (
        ("threeb1", "s2"), ("threea0", "s3"), ("up1", "t1"), ("dwo0", "s3"), ("threea1", "s3"), ("threeb0", "s3"),
        ("gate0", "t2"), ("gate1", "t2"), ("up0", "t2"), ("threeb1", "s3"), ("down0", "t3"), ("up1", "t2"),
    ),
    "res": (
        ("dwo0", "t1"), ("threea0", "t1"), ("threea1", "t1"), ("threeb0", "t1"), ("up0", "t3"),
    ),
    "gtot": (
        ("threeb1", "t1"), ("up1", "t3"), ("gate0", "t3"), ("gate1", "t3"), ("dwo0", "t2"), ("threea0", "t2"),
        ("threea1", "t2"), ("threeb0", "t2"),
    ),
    "gend": (
        ("threeb1", "t2"), ("dwo0", "t3"), ("threea0", "t3"), ("threea1", "t3"), ("threeb0", "t3"), ("threeb1", "t3"),
        ("down0", "t4"), ("up0", "t4"), ("up1", "t4"), ("gate0", "t4"), ("gate1", "t4"), ("dwo0", "t4"),
        ("threea0", "t4"), ("threeb0", "t4"), ("threea1", "t4"), ("threeb1", "t4"),
    ),
}


def attention_back_kernel(
    z_part, t_part, dw_u, ga, p2, resid, tok, gr, g_one, q, k, v, ho, w3, wo, g1, cosine, sine, gain_two,
    ff_o, d3_o, do_o, gains_o, act_o, grad_o,
    ga_s, q_s, k_s, v_s, ho_s, w3_s, wo_s, gh_s, dk_s, dv_s, g3_s, ho_t, g3_t, dwo_s, dw3_s,
    resid_s, tok_s, gr_s, act_s,
    zs, tail_ag, tail_z, red_b, red_ag, red_x, red_f1, red_f2, red_z, gpart, gy, gx,
    part2, own2, ra2, rb2, f12, f22,
    part, own, ra, rb, f1, f2,
    ag_ss, ag_rs, r2_ss, r2_rs, rs_ss, rs_rs, loc, tail_ss, tail_rs, tail_done, red_ss, red_rs, red_loc, red_done, g_ss, g_rs, t_ss, t_rs, t_loc,
):
    me = Place()
    c = me.c
    rows = ga.shape[0]
    step = 2 * rows
    zl = me.zl
    near = [{**me.at(dy=d), "core": lax.rem(c + s, 2)} for d in range(4) for s in (0, 1) if d or s]
    near += [me.at(dx=d, dz=s) for d in range(4) for s in range(4) if d or s]
    near += [me.at(dz=s, core=1 - c) for s in (1, -1)]
    meet(near)
    stays = c == zl
    swap = {"zl": 1 - zl, "core": 1 - c}
    first = pltpu.make_async_copy(ga, ga_s.at[me.y, pl.ds(c * rows, rows)], loc.at[0])
    first.start()
    z_load = pltpu.make_async_copy(z_part, zs, loc.at[12])
    z_load.start()
    ff = dw_u.shape[0]
    t_load = pltpu.make_async_copy(t_part, red_b.at[pl.ds(0, ff)], loc.at[13])
    t_load.start()
    loads = [
        pltpu.make_async_copy(a, b, loc.at[1 + i])
        for i, (a, b) in enumerate(
            ((p2, part2), (wo, wo_s), (q, q_s), (k, k_s), (v, v_s), (ho, ho_s),
             (resid, resid_s), (tok, tok_s), (gr, gr_s))
        )
    ]
    for i in range(6):
        head, kind = divmod(i, 3)
        at = pl.ds(head * 384 + kind * 128, 128)
        loads.append(pltpu.make_async_copy(w3.at[:, pl.ds(kind * 256 + head * 128, 128)], w3_s.at[:, at], loc.at[14 + i]))
    for cp in loads:
        cp.start()
    first.wait()
    gather = Gather(me, ga_s, ag_ss, ag_rs, rows)
    gather.start()
    count = [0]
    pieces = {}

    def whole(name, src, dst, row):
        n = dst.shape[0]
        i = count[0]
        count[0] += 1
        head = Head(
            me, src, (red_b, red_ag, red_x, red_f1, red_f2), row, n,
            red_ss.at[i, pl.ds(0, Head.SEMS)], red_rs.at[i, pl.ds(0, Head.SEMS)], red_loc.at[i],
        )
        own = red_b.at[pl.ds(row, n), head.blk(0)]
        sems = pl.ds(Head.SEMS, Tail.SEMS)
        tail = Tail(me, own, dst, red_ag, red_z, row, n, red_ss.at[i, sems], red_rs.at[i, sems], red_done.at[i])
        pieces[name] = Sum(head, tail)

    def parts(name, src, dst, row, pieces_of):
        for j, (start, n) in enumerate(chunks_of(dst.shape[0], dst.shape[0] / pieces_of)):
            whole(f"{name}{j}", src.at[pl.ds(start, n)], dst.at[pl.ds(start, n)], row + start)

    for i, (start, n) in enumerate(chunks_of(ff, ff / DOWN_PARTS)):
        pieces[f"down{i}"] = Tail(
            me, zs.at[pl.ds(start, n)], ff_o.at[0].at[pl.ds(start, n)], tail_ag, tail_z, start, n,
            tail_ss.at[i], tail_rs.at[i], tail_done.at[i],
        )
    parts("gate", dw_u, ff_o.at[1], 0, GATE_PARTS)
    parts("up", dw_u, ff_o.at[2], ff, UP_PARTS)
    parts("dwo", dwo_s, do_o, 2 * ff, 1)
    for j in (0, 1):
        parts("three" + "ab"[j], dw3_s.at[pl.ds(384 * j, 384)], d3_o.at[pl.ds(384 * j, 384)], 2 * ff + 256 + 384 * j, THREE_PARTS)

    def after(step):
        for name, stage in ORDER.get(step, ()):
            getattr(pieces[name], stage)()

    z_load.wait()
    t_load.wait()
    after("start")
    for cp in loads:
        cp.wait()

    def heads(d):
        at = me.yy(d)
        out = dot_nt(ga_s[at], wo_s[...]).astype(BF16)
        for half in (0, 1):
            place = pl.ds(pl.multiple_of((at + 4 * half) * rows, rows), rows)
            for head in (0, 1):
                gh_s[head, place] = out[half * rows:(half + 1) * rows, head * 128:head * 128 + 128]

    def turn(src, dst):
        for i in range(4):
            dst[:, i * step:(i + 1) * step] = src[pl.ds(i * step, step)].T

    turn(ho_s, ho_t)
    second = Scatter(me, part2, own2, ra2, rb2, f12, f22, r2_ss, r2_rs, rows)
    for d in second.order:
        second.ready(d)
    after("loads")
    gather.got(4)
    heads(0)
    after("heads0")
    gather.forward_one()
    after("fwd1")
    gather.near()
    after("near")
    second.stage_two()
    after("2two")
    second.stage_one()
    after("2one")
    gather.got(7)
    heads(-1)
    gather.got(8)
    heads(1)
    after("headsn")
    gather.far()
    after("far")
    gather.got(9)
    heads(2)
    after("heads2")

    def weight(dst, turned, y):
        wide = 512
        for j in range(y.shape[2] // wide):
            cols = slice(j * wide, (j + 1) * wide)
            acc = dot(turned[:, 0:step], y[0, :, cols])
            for i in range(1, 4):
                acc += dot(turned[:, i * step:(i + 1) * step], y[i, :, cols])
            dst[:, cols] = acc.astype(BF16)

    weight(dwo_s, ho_t, ga_s)
    after("dwo")
    gather.finish()
    load_one = pltpu.make_async_copy(g_one, ga_s, loc.at[11])
    load_one.start()
    scale = HEAD_DIM ** (-0.5)

    def attend(head, block):
        stop = (block + 1) * step
        mine = pl.ds(block * step, step)
        seen = pl.ds(0, stop)
        qb = q_s[head, mine]
        gb = gh_s[head, mine]
        s = dot_nt(qb, k_s[head, seen]) * scale
        places = block * step + lax.broadcasted_iota(jnp.int32, (step, stop), 0)
        s = jnp.where(lax.broadcasted_iota(jnp.int32, (step, stop), 1) <= places, s, -1e30)
        e = jnp.exp(s - jnp.max(s, -1, keepdims=True))
        p = e / jnp.sum(e, -1, keepdims=True)
        gp = dot_nt(gb, v_s[head, seen])
        ds = (p * (gp - jnp.sum(p * gp, -1, keepdims=True)) * scale).astype(BF16)
        gv = dot_tn(p.astype(BF16), gb)
        gk = dot_tn(ds, qb)
        gq = dot(ds, k_s[head, seen])
        gq = (gq * cosine[mine] - pltpu.roll(gq, 64, axis=1) * sine[mine]).astype(BF16)
        for half in (0, 1):
            g3_s[pl.ds(perm(2 * block + half) * rows, rows), pl.ds(head * 384, 128)] = gq[half * rows:(half + 1) * rows]
        if block:
            before = pl.ds(0, stop - step)
            dk_s[head, before] += gk[:stop - step]
            dv_s[head, before] += gv[:stop - step]
        dk_s[head, mine] = gk[stop - step:]
        dv_s[head, mine] = gv[stop - step:]

    def finish_head(head):
        for t in range(8):
            place = pl.ds(t * rows, rows)
            to = pl.ds(perm(t) * rows, rows)
            gk = dk_s[head, place]
            gk = gk * cosine[place] - pltpu.roll(gk, 64, axis=1) * sine[place]
            g3_s[to, pl.ds(head * 384 + 128, 128)] = gk.astype(BF16)
            g3_s[to, pl.ds(head * 384 + 256, 128)] = dv_s[head, place].astype(BF16)
        mine = pl.ds(head * 384, 384)
        for i in range(4):
            g3_t[mine, i * step:(i + 1) * step] = g3_s[pl.ds(i * step, step), mine].T
        weight(dw3_s.at[mine], g3_t.at[mine], ga_s)

    attend(0, 0)
    attend(0, 1)
    after("att0")
    attend(0, 2)
    second.stage_last()
    attend(0, 3)
    after("att1")
    load_one.wait()
    finish_head(0)
    after("dw3a")
    attend(1, 0)
    attend(1, 1)
    after("att2")
    attend(1, 2)
    attend(1, 3)
    after("att3")
    finish_head(1)
    after("dw3b")
    scatter = Scatter(me, part, own, ra, rb, f1, f2, rs_ss, rs_rs, rows)

    def back(d):
        at = me.yy(d)
        part[at] = dot_nt(g3_s[pl.ds(pl.multiple_of(at * step, step), step)], w3_s[...]).astype(BF16)
        scatter.ready(d)

    back(2)
    back(1)
    after("back3")
    scatter.stage_two()
    after("two")
    back(-1)
    back(0)
    after("back0")
    scatter.stage_one()
    after("one")
    scatter.stage_last()
    after("last")
    second.result()
    act_s[...] = (resid_s[...] + second.total(0, rows)).astype(BF16)
    moves = [remote(a, o, t_ss.at[i], t_rs.at[i], swap) for i, (a, o) in enumerate(((act_s, act_o), (gr_s, grad_o)))]
    store = [pltpu.make_async_copy(a, o, t_loc.at[i]) for i, (a, o) in enumerate(((act_s, act_o), (gr_s, grad_o)))]

    def home(i):
        @pl.when(stays)
        def _():
            store[i].start()

        @pl.when(jnp.logical_not(stays))
        def _():
            moves[i].start()

    home(0)
    after("act")
    scatter.result()
    gn = scatter.total(0, rows)
    unit, factor = normed(tok_s[...].astype(F32))
    gains = (jnp.sum(gn * unit, axis=0, keepdims=True), gain_two[...])
    for i in range(4):
        for j in range(2):
            for zi in range(2):
                lo = (zi * 4 + i) * 256
                gpart[i, 2 * j + zi:2 * j + zi + 1] = gains[j][:, lo:lo + 256]
    g = gn * g1[...]
    gr_s[...] = gr_s[...] + factor * (g - unit * jnp.mean(g * unit, axis=-1, keepdims=True))
    home(1)
    here = me.x * 4 + me.z
    gains_a, gains_b = [], []
    for d in range(4):
        for s in (0, 1):
            if d or s:
                to = {**me.at(dy=d), "core": lax.rem(c + s, 2)}
                i = len(gains_a)
                gains_a.append(remote(gpart.at[me.yy(d)], gy.at[me.y * 2 + c], g_ss.at[i], g_rs.at[i], to))
    for d in range(4):
        for s in range(4):
            if d or s:
                i = 7 + len(gains_b)
                gains_b.append(remote(gx.at[here], gx.at[here], g_ss.at[i], g_rs.at[i], me.at(dx=d, dz=s)))

    def gain_total(sends, ref):
        for cp in sends:
            cp.wait()
        total = ref[0]
        for i in range(1, ref.shape[0]):
            total = total + ref[i]
        return total

    gy[me.y * 2 + c] = gpart[me.y]
    for cp in gains_a:
        cp.start()
    after("res")
    gx[here] = gain_total(gains_a, gy)
    for cp in gains_b:
        cp.start()
    after("gtot")
    gains_o[...] = gain_total(gains_b, gx)
    after("gend")
    second.finish()
    scatter.finish()

    @pl.when(stays)
    def _():
        for cp in store:
            cp.wait()

    @pl.when(jnp.logical_not(stays))
    def _():
        for cp in moves:
            cp.wait()


def attention_back(args):
    dw_u, ga = args[2:4]
    ff = dw_u.shape[0]
    rows, width = ga.shape
    length = 8 * rows
    sds = jax.ShapeDtypeStruct
    outs = [
        sds((3, ff, width), BF16), sds((768, width), BF16), sds((256, width), BF16), sds((8, 256), F32),
        sds((rows, width), BF16), sds((rows, width), F32),
    ]
    total = 2 * ff + 1024
    sem = pltpu.SemaphoreType.DMA
    n = 1 + GATE_PARTS + UP_PARTS + 2 * THREE_PARTS
    many = sem((n, Head.SEMS + Tail.SEMS))
    half, eighth = width // 2, width // 8
    sums = [
        pltpu.VMEM((ff, eighth), BF16), pltpu.VMEM((ff, half), BF16), pltpu.VMEM((ff, eighth), BF16),
        *[pltpu.VMEM((total, half), BF16)] * 2, *[pltpu.VMEM((total, eighth), BF16)] * 4,
    ]
    part = pltpu.VMEM((4, 8, 256), F32)
    by_chip = (4, 2 * rows, width)
    head = (2, length, 128)
    scratch = [
        pltpu.VMEM(by_chip, BF16),
        *[pltpu.VMEM(head, BF16)] * 3, pltpu.VMEM((length, 256), BF16),
        pltpu.VMEM((width, 768), BF16), pltpu.VMEM((256, width), BF16),
        pltpu.VMEM(head, BF16), pltpu.VMEM(head, F32), pltpu.VMEM(head, F32),
        pltpu.VMEM((length, 768), BF16), pltpu.VMEM((256, length), BF16), pltpu.VMEM((768, length), BF16),
        pltpu.VMEM((256, width), BF16), pltpu.VMEM((768, width), BF16),
        pltpu.VMEM((rows, width), F32), pltpu.VMEM((rows, width), BF16), pltpu.VMEM((rows, width), F32),
        pltpu.VMEM((rows, width), BF16),
        *sums, part, pltpu.VMEM((8, 8, 256), F32), pltpu.VMEM((16, 8, 256), F32),
        *scatter_scratch(rows, width), *scatter_scratch(rows, width),
        dma(10), dma(10), dma(10), dma(10), dma(10), dma(10), dma(20), sem((DOWN_PARTS, Tail.SEMS)), sem((DOWN_PARTS, Tail.SEMS)), dma(DOWN_PARTS), many, many, dma(n), dma(n), dma(22), dma(22), dma(2), dma(2), dma(2),
    ]
    return pl.pallas_call(
        attention_back_kernel,
        name="attention_back",
        out_shape=outs,
        in_specs=[ANY] * 15 + [VM] * 4,
        out_specs=[ANY] * 3 + [VM] + [ANY] * 2,
        scratch_shapes=scratch,
        compiler_params=pltpu.CompilerParams(collective_id=2, has_side_effects=True, vmem_limit_bytes=62 * MIB),
    )(*args)


def widen_kernel(
    ff, three, out, act, grad, gains, d_o, g_o, u_o, q_o, k_o, v_o, o_o, act_o, grad_o, one_o, two_o,
    ff_s, three_s, out_s, wide_s, turned_s, last_s, act_s, grad_s, sem, done,
):
    rows = chunks_of(ff.shape[1], ff.shape[1] / 4)
    work = [(i, pl.ds(lo, n)) for i in range(3) for lo, n in rows]
    loads = [pltpu.make_async_copy(three, three_s, sem.at[0]), pltpu.make_async_copy(out, out_s, sem.at[1])]
    loads += [pltpu.make_async_copy(ff.at[i, at], ff_s.at[i, at], sem.at[2 + j]) for j, (i, at) in enumerate(work)]
    loads += [pltpu.make_async_copy(act, act_s, sem.at[14]), pltpu.make_async_copy(grad, grad_s, sem.at[15])]
    for cp in loads:
        cp.start()
    zl = lax.axis_index("zl")
    one_o[...] = jnp.where(zl == 0, gains[0:1], gains[1:2])
    two_o[...] = jnp.where(zl == 0, gains[2:3], gains[3:4])
    saves = []

    def save(src, dst):
        cp = pltpu.make_async_copy(src, dst, done.at[len(saves)])
        cp.start()
        saves.append(cp)

    loads[0].wait()
    for i, ref in enumerate((q_o, k_o, v_o)):
        for head in (0, 1):
            row = head * 384 + i * 128
            turned_s[i, :, head * 128:head * 128 + 128] = three_s[row:row + 128].astype(F32).T
        save(turned_s.at[i], ref)
    loads[1].wait()
    last_s[...] = out_s[...].astype(F32)
    save(last_s, o_o)
    for j, (i, at) in enumerate(work):
        loads[2 + j].wait()
        wide_s[i, at] = ff_s[i, at].astype(F32)
        save(wide_s.at[i, at], (d_o, g_o, u_o)[i].at[at])
    loads[-2].wait()
    save(act_s, act_o)
    loads[-1].wait()
    save(grad_s, grad_o)
    for cp in saves:
        cp.wait()


def widen(ff, three, out, act, grad, gains):
    _, n, width = ff.shape
    sds = jax.ShapeDtypeStruct
    return pl.pallas_call(
        widen_kernel,
        name="widen",
        out_shape=[sds((n, width), F32)] * 3 + [sds((width, 256), F32)] * 3 + [
            sds((256, width), F32), sds(act.shape, BF16), sds(grad.shape, F32), sds((1, 256), F32), sds((1, 256), F32)
        ],
        in_specs=[ANY] * 5 + [VM],
        out_specs=[ANY] * 9 + [VM] * 2,
        scratch_shapes=[
            pltpu.VMEM((3, n, width), BF16), pltpu.VMEM((768, width), BF16), pltpu.VMEM((256, width), BF16),
            pltpu.VMEM((3, n, width), F32), pltpu.VMEM((3, width, 256), F32), pltpu.VMEM((256, width), F32),
            pltpu.VMEM(act.shape, BF16), pltpu.VMEM(grad.shape, F32), dma(16), dma(18),
        ],
        compiler_params=pltpu.CompilerParams(vmem_limit_bytes=62 * MIB),
    )(ff, three, out, act, grad, gains)


def per_device(tokens, wq, wk, wv, wo, wg, wu, wd, attn_gain, mlp_gain, cotangent):
    tokens, cotangent = tokens[0], cotangent[0]
    length = 8 * tokens.shape[0]
    ff = wd.shape[0]
    cosine, sine = (jnp.asarray(t) for t in tables(length, HEAD_DIM))
    wg, wu = wg.T, wu.T
    g1, g2 = attn_gain[None], mlp_gain[None]
    (resid, tok, one, q, k, v, ho, w3, wo, gr, ga, gain_two, p2, z_part, t_part, dw_u) = layer(
        (tokens, cotangent, wq, wk, wv, wo, wg, wu, wd, g1, g2, cosine, sine)
    )
    dw_ff, dw3, dwo, gains, act, grad = attention_back(
        (z_part, t_part, dw_u, ga, p2, resid, tok, gr, one, q, k, v, ho, w3, wo, g1, cosine, sine, gain_two)
    )
    d_down, d_gate, d_up, d_query, d_key, d_value, d_out, act, grad, one, two = widen(dw_ff, dw3, dwo, act, grad, gains)
    return act[None], grad[None], d_query, d_key, d_value, d_out, d_gate.T, d_up.T, d_down, one[0], two[0]


def solution(mesh):
    split = Mesh(mesh.devices.reshape(4, 2, 2, 2, 4), ("x", "zh", "core", "zl", "y"))
    dp, tensor = ("x", "zh", "core"), ("zl", "y")
    cols, rows, seqs = P(None, tensor), P(tensor, None), P(dp, tensor, None)
    return jax.shard_map(
        per_device,
        mesh=split,
        in_specs=(seqs, cols, cols, cols, rows, cols, cols, rows, P(), P(), seqs),
        out_specs=(seqs, seqs, cols, cols, cols, rows, cols, cols, rows, P(tensor), P(tensor)),
        check_vma=False,
    )
```
